256 devices in a mesh: gx: 8 (over y, core), gy: 32 (over z, x).
Axes of the slice: x: 4, y: 4, z: 8, core: 2. Of those that a mesh axis runs over, the one named last changes fastest.
Arguments:
- tracer_adjoint: float32 [2, 50, 1280, 1024], P(None, None, 'gy', 'gx'), may hold values from -6 to 6
- surface_adjoint: float32 [1280, 1024], P('gy', 'gx'), may hold values from -6 to 6
- flow_east: float32 [50, 1280, 1024], P(None, 'gy', 'gx'), may hold values from -0.4 to 0.4, as said below
- flow_north: float32 [50, 1280, 1024], P(None, 'gy', 'gx'), may hold values from -0.4 to 0.4, as said below
- vertical_mix: float32 [49, 1280, 1024], P(None, 'gy', 'gx'), may hold values from 0.1 to 10
- land_mask: int32 [50, 1280, 1024], P(None, 'gy', 'gx'), may hold values from 0 to 1, as said below
- conduct_east: float32 [1280, 1024], P('gy', 'gx'), may hold values from 0 to 4, as said below
- conduct_north: float32 [1280, 1024], P('gy', 'gx'), may hold values from 0 to 4, as said below
- surface_diagonal: float32 [1280, 1024], P('gy', 'gx'), may hold values from 0.02 to 0.2
- pressure_load: float32 [2, 50], replicated, may hold values from -0.5 to 0.5
- surface_forcing: float32 [2, 50], replicated, may hold values from -0.1 to 0.1
- control_map: int32 [4608], replicated, may hold values from 0 to 2559
- control_weight: float32 [4608], replicated, may hold values from 0.5 to 1.5
Outputs:
- tracer_grad: float32 [2, 50, 1280, 1024], P(None, None, 'gy', 'gx')
- surface_grad: float32 [1280, 1024], P('gy', 'gx')
- control_grad: float32 [2, 50, 2560], P(None, None, ('gx', 'gy'))
The draws below stay inside these ranges and needn't reach their ends.
Inputs may be any that keep to these rules, and one draw needn't show every extreme that they name: `land_mask`: 1 marks an ocean cell and 0 land; where a cell is ocean, the cell above it is ocean too. `flow_east`: zero on every face that touches land or lies on the grid's eastern edge. `flow_north`: zero on every face that touches land or lies on the grid's northern edge. `conduct_east`: zero on faces that touch land at the surface or lie on the eastern edge, positive elsewhere. `conduct_north`: zero on faces that touch land at the surface or lie on the northern edge, positive elsewhere.
All inputs are finite; a program needn't handle non-finite values.
Results may differ from the reference program's by a relative error of at most 0.0003.
Values sent between devices are 32-bit elements; how exact they have to be, the bound alone decides.
No kernel may reach another device: no remote copies, remote signals or barrier semaphores. Data moves between devices by JAX's collectives and lax.ppermute only.
A program may use at most 128 MiB of HBM per device.

```python
import math
import jax
import jax.numpy as jnp

K = 50
CX = 128
CY = 40
ITERS = 3
CTRL_DEV = 10
NX = 1024
NY = 1280
POINTS = 4608
CONTROLS = 2560


def ocean_bottom(key):
    coarse = jax.random.randint(jax.random.fold_in(key, 101), (NY // 8, NX // 8), -(K // 8), K + K // 4 + 1)
    blocks = jnp.repeat(jnp.repeat(coarse, 8, axis=0), 8, axis=1)
    jitter = jax.random.randint(jax.random.fold_in(key, 102), (NY, NX), -(K // 10) - 1, K // 10 + 2)
    return jnp.clip(blocks + jitter, 0, K)


def water_levels(key):
    bottom = ocean_bottom(key)
    levels = jnp.arange(K, dtype=jnp.int32)[:, None, None]
    return levels < bottom[None]


def draw_land_mask(key, part):
    wet_level = water_levels(key)
    return wet_level.astype(jnp.int32)


def draw_flow_east(key, part):
    wet_level = water_levels(key).astype(jnp.float32)
    key = jax.random.fold_in(key, 2)
    east_wet = jnp.pad(wet_level[:, :, 1:], ((0, 0), (0, 0), (0, 1)))
    velocity = jax.random.uniform(key, (K, NY, NX), jnp.float32, -0.3, 0.3)
    return velocity * wet_level * east_wet


def draw_flow_north(key, part):
    wet_level = water_levels(key).astype(jnp.float32)
    key = jax.random.fold_in(key, 3)
    north_wet = jnp.pad(wet_level[:, 1:, :], ((0, 0), (0, 1), (0, 0)))
    velocity = jax.random.uniform(key, (K, NY, NX), jnp.float32, -0.3, 0.3)
    return velocity * wet_level * north_wet


def draw_conduct_east(key, part):
    surface_wet = (ocean_bottom(key) > 0).astype(jnp.float32)
    key = jax.random.fold_in(key, 4)
    east_wet = jnp.pad(surface_wet[:, 1:], ((0, 0), (0, 1)))
    spread = jnp.log(2.0)
    value = jnp.exp(jax.random.uniform(key, (NY, NX), jnp.float32, -spread, spread))
    return value * surface_wet * east_wet


def draw_conduct_north(key, part):
    surface_wet = (ocean_bottom(key) > 0).astype(jnp.float32)
    key = jax.random.fold_in(key, 5)
    north_wet = jnp.pad(surface_wet[1:, :], ((0, 1), (0, 0)))
    spread = jnp.log(2.0)
    value = jnp.exp(jax.random.uniform(key, (NY, NX), jnp.float32, -spread, spread))
    return value * surface_wet * north_wet


def draw_control_map(key, part):
    key = jax.random.fold_in(key, 6)
    tiles_lon = NX // CX
    tiles_lat = NY // CY
    device_count = tiles_lon * tiles_lat
    points = jnp.arange(POINTS, dtype=jnp.int32)
    first_seg = points < NX
    second_seg = points < 2 * NX
    third_seg = points < 2 * NX + NY
    column_idx = jnp.where(first_seg, points // CX, jnp.where(second_seg, (points - NX) // CX, jnp.where(third_seg, 0, tiles_lon - 1)))
    row_idx = jnp.where(first_seg, 0, jnp.where(second_seg, tiles_lat - 1, jnp.where(third_seg, (points - 2 * NX) // CY, (points - 2 * NX - NY) // CY)))
    holder = column_idx * tiles_lat + row_idx
    random_owner = jax.random.randint(jax.random.fold_in(key, 1), (POINTS,), 0, device_count)
    phase = points % 4
    owner = jnp.where(phase == 0, holder + device_count // 2, jnp.where(phase == 1, holder + 1, jnp.where(phase == 2, holder + device_count - 1, random_owner)))
    owner = owner % device_count
    slot = jax.random.randint(jax.random.fold_in(key, 2), (POINTS,), 0, CTRL_DEV)
    chosen = owner * CTRL_DEV + slot
    chosen = jnp.where(points == 0, 0, chosen)
    chosen = jnp.where(points == POINTS - 1, CONTROLS - 1, chosen)
    return chosen.astype(jnp.int32)


def block_levels(stream_key, dims, cuts, smallest, largest):
    def one(dim, blocks):
        steps = jax.random.uniform(jax.random.fold_in(jax.random.fold_in(stream_key, 6), dim), (blocks,), jnp.float32, smallest / len(cuts), largest / len(cuts))
        return jnp.repeat(jnp.exp(steps), dims[dim] // blocks).reshape((-1,) + (1,) * (len(dims) - dim - 1))

    level = one(*cuts[0])
    for cut in cuts[1:]:
        level = level * one(*cut)
    return level


def gaussian(stream_key, shape, scale, limit, pieces=(), kind=jnp.bfloat16):
    gain = block_levels(stream_key, shape, pieces, -0.22, 0.18) if pieces else 1.0
    values = jax.random.normal(stream_key, shape, jnp.float32) * scale * gain
    return jnp.minimum(jnp.maximum(values, -limit), limit).astype(kind)


def setup_inputs(seed: int = 0) -> dict:
    keys = jax.random.split(jax.random.key(seed), 14)
    tracer_adjoint = gaussian(keys[0], (2, K, NY, NX), 1.0, 6.0, ((2, 32), (3, 8)), jnp.float32)
    surface_adjoint = gaussian(keys[1], (NY, NX), 1.0, 6.0, ((0, 32), (1, 8)), jnp.float32)
    flow_east = draw_flow_east(jax.random.fold_in(keys[13], 71), 0)
    flow_north = draw_flow_north(jax.random.fold_in(keys[13], 71), 0)
    vertical_mix = jnp.clip(jnp.exp(math.log(10.0) - 4.6051702 * jax.random.uniform(keys[4], (K - 1, NY, NX), jnp.float32) ** block_levels(keys[4], (K - 1, NY, NX), ((1, 32), (2, 8)), -0.2, 0.2)), 0.1, 10.0)
    land_mask = draw_land_mask(jax.random.fold_in(keys[13], 71), 0)
    conduct_east = draw_conduct_east(jax.random.fold_in(keys[13], 71), 0)
    conduct_north = draw_conduct_north(jax.random.fold_in(keys[13], 71), 0)
    surface_diagonal = jnp.clip(jnp.exp(math.log(0.2) - 2.3025851 * jax.random.uniform(keys[8], (NY, NX), jnp.float32) ** block_levels(keys[8], (NY, NX), ((0, 32), (1, 8)), -0.2, 0.2)), 0.02, 0.2)
    pressure_load = jnp.clip(jax.random.uniform(keys[9], (2, K), jnp.float32, -0.5, 0.5), -0.5, 0.5)
    surface_forcing = jnp.clip(jax.random.uniform(keys[10], (2, K), jnp.float32, -0.1, 0.1), -0.1, 0.1)
    control_map = draw_control_map(jax.random.fold_in(keys[13], 71), 0)
    control_weight = jnp.clip(jax.random.uniform(keys[12], (POINTS,), jnp.float32, 0.5, 1.5), 0.5, 1.5)
    return {"tracer_adjoint": tracer_adjoint, "surface_adjoint": surface_adjoint, "flow_east": flow_east, "flow_north": flow_north, "vertical_mix": vertical_mix, "land_mask": land_mask, "conduct_east": conduct_east, "conduct_north": conduct_north, "surface_diagonal": surface_diagonal, "pressure_load": pressure_load, "surface_forcing": surface_forcing, "control_map": control_map, "control_weight": control_weight}


def column_solve(right_side, kappa_vert):
    levels = right_side.shape[-3]
    ratios = []
    reduced = []
    for level in range(levels):
        diag_term = 1.0
        if level > 0:
            diag_term = diag_term + kappa_vert[level - 1]
        if level < levels - 1:
            diag_term = diag_term + kappa_vert[level]
        if level == 0:
            pivot_val = diag_term
            carried = right_side[..., 0, :, :]
        else:
            pivot_val = diag_term - kappa_vert[level - 1] * ratios[level - 1]
            carried = right_side[..., level, :, :] + kappa_vert[level - 1] * reduced[level - 1]
        reduced.append(carried / pivot_val)
        if level < levels - 1:
            ratios.append(kappa_vert[level] / pivot_val)
    solution = [reduced[levels - 1]]
    for level in range(levels - 2, -1, -1):
        solution.insert(0, reduced[level] + ratios[level] * solution[0])
    return jnp.stack(solution, axis=-3)


def surface_apply(surface, conduct_east, conduct_north, surface_diagonal):
    east_side = jnp.pad(surface[:, 1:], ((0, 0), (0, 1)))
    west_side = jnp.pad(surface[:, :-1], ((0, 0), (1, 0)))
    north_side = jnp.pad(surface[1:, :], ((0, 1), (0, 0)))
    south_side = jnp.pad(surface[:-1, :], ((1, 0), (0, 0)))
    conduct_west = jnp.pad(conduct_east[:, :-1], ((0, 0), (1, 0)))
    conduct_south = jnp.pad(conduct_north[:-1, :], ((1, 0), (0, 0)))
    return (surface_diagonal * surface + conduct_east * (surface - east_side)
            + conduct_west * (surface - west_side) + conduct_north * (surface - north_side)
            + conduct_south * (surface - south_side))


def reference(tracer_adjoint, surface_adjoint, flow_east, flow_north, vertical_mix, land_mask,
              conduct_east, conduct_north, surface_diagonal, pressure_load, surface_forcing,
              control_map, control_weight):
    wet_cells = land_mask.astype(jnp.float32)
    forcing_sum = surface_adjoint + jnp.sum(surface_forcing[:, :, None, None] * wet_cells[None] * tracer_adjoint, axis=(0, 1))
    iterate = jnp.zeros_like(forcing_sum)
    remain = forcing_sum
    search = remain
    norm_now = jnp.sum(remain * remain)
    for iteration in range(ITERS):
        image = surface_apply(search, conduct_east, conduct_north, surface_diagonal)
        step_len = norm_now / jnp.sum(search * image)
        iterate = iterate + step_len * search
        remain = remain - step_len * image
        if iteration + 1 < ITERS:
            norm_next = jnp.sum(remain * remain)
            search = remain + (norm_next / norm_now) * search
            norm_now = norm_next
    solved = iterate
    kappa_vert = vertical_mix * wet_cells[1:]
    lifted = tracer_adjoint + wet_cells[None] * pressure_load[:, :, None, None] * solved[None, None]
    lam_field = wet_cells[None] * column_solve(lifted, kappa_vert)
    east_side = jnp.pad(lam_field[..., 1:], ((0, 0), (0, 0), (0, 0), (0, 1)))
    west_side = jnp.pad(lam_field[..., :-1], ((0, 0), (0, 0), (0, 0), (1, 0)))
    north_side = jnp.pad(lam_field[..., 1:, :], ((0, 0), (0, 0), (0, 1), (0, 0)))
    south_side = jnp.pad(lam_field[..., :-1, :], ((0, 0), (0, 0), (1, 0), (0, 0)))
    flow_west = jnp.pad(flow_east[..., :-1], ((0, 0), (0, 0), (1, 0)))
    flow_south = jnp.pad(flow_north[:, :-1, :], ((0, 0), (1, 0), (0, 0)))
    tracer_grad = (lam_field + 0.5 * flow_east * (east_side - lam_field)
                   + 0.5 * flow_west * (lam_field - west_side)
                   + 0.5 * flow_north * (north_side - lam_field)
                   + 0.5 * flow_south * (lam_field - south_side))
    edge_vals = jnp.concatenate([tracer_grad[:, :, 0, :], tracer_grad[:, :, -1, :],
                                 tracer_grad[:, :, :, 0], tracer_grad[:, :, :, -1]], axis=2)
    weighted = (edge_vals * control_weight).reshape(2 * K, POINTS)
    totals = jax.ops.segment_sum(weighted.T, control_map, num_segments=CONTROLS)
    control_grad = totals.T.reshape(2, K, CONTROLS)
    return tracer_grad, solved, control_grad
```

```python
import functools

import jax
import jax.numpy as jnp
from jax import lax
from jax.experimental import pallas as pl
from jax.experimental.pallas import tpu as pltpu
from jax.sharding import PartitionSpec as P

SLOTS = 10
LANES = 128
BLOCK = 8
GRAM = ((0, 0), (0, 1), (0, 2), (0, 3), (1, 1), (1, 2), (1, 3), (2, 2), (2, 3))
VMEM = pl.BlockSpec(memory_space=pltpu.VMEM)
SMEM = pl.BlockSpec(memory_space=pltpu.SMEM)
HBM = pl.BlockSpec(memory_space=pltpu.HBM)
MIB = 1024 * 1024
BIG = pltpu.CompilerParams(vmem_limit_bytes=16 * MIB)
MIDDLE = pltpu.CompilerParams(vmem_limit_bytes=8 * MIB)
SMALL = pltpu.CompilerParams(vmem_limit_bytes=3 * MIB)


def lanes_of(shape):
    return lax.broadcasted_iota(jnp.int32, shape, len(shape) - 1)


def moved(value, source, target):
    shift = target - source
    shift = shift % LANES if isinstance(shift, int) else lax.rem(shift + 4 * LANES, LANES)
    return pltpu.roll(value, shift, 1)


def columns_kernel(
    forcing_in, loads_in, tracer_in, surface_in, east_flow, north_flow, mix_in, mask_in, c_east_in,
    c_north_in, diag_in,
    b_out, u_out, v_out, west_pack, east_pack, south_rows, north_rows,
    ratios, forcing, loads, tracer, surface, flow_east, flow_north, mix, mask, c_east, c_north, diag,
    sems,
):
    levels, rows, cols = mask.shape
    shape = (rows, cols)
    zero = jnp.zeros(shape, jnp.float32)
    last = levels - 1
    chunk = 7
    started = []

    def fetch(source, target):
        copy = pltpu.make_async_copy(source, target, sems.at[len(started)])
        copy.start()
        started.append(copy)
        return copy

    scalars = [fetch(forcing_in, forcing), fetch(loads_in, loads)]
    chunks = []
    for at in range(0, last, chunk):
        here = pl.ds(at, chunk if at + chunk < last else chunk + 1)
        below = pl.ds(at + 1, chunk) if at else pl.ds(0, chunk + 1)
        chunks.append([
            fetch(mask_in.at[below], mask.at[below]),
            fetch(mix_in.at[pl.ds(at, chunk)], mix.at[pl.ds(at, chunk)]),
            fetch(tracer_in.at[:, here], tracer.at[:, here]),
        ])
    flats = [
        fetch(source, target)
        for source, target in (
            (surface_in, surface), (c_east_in, c_east), (c_north_in, c_north), (diag_in, diag),
            (north_flow.at[:, pl.ds(rows - BLOCK, BLOCK)], flow_north), (east_flow, flow_east),
        )
    ]
    for copy in scalars:
        copy.wait()

    def level_step(k, carry, kappa):
        before, ratio, r0, r1, r2, r3, total = carry
        wet = mask[k].astype(jnp.float32)
        t0, t1 = tracer[0, k], tracer[1, k]
        total = total + wet * (forcing[0, k] * t0 + forcing[1, k] * t1)
        inverse = 1.0 / (1.0 + before + kappa - before * ratio)
        r0 = (t0 + before * r0) * inverse
        r1 = (t1 + before * r1) * inverse
        r2 = (wet * loads[0, k] + before * r2) * inverse
        r3 = (wet * loads[1, k] + before * r3) * inverse
        return kappa * inverse, r0, r1, r2, r3, total

    carry = (zero,) * 7
    for k in range(last):
        if k % chunk == 0:
            for copy in chunks[k // chunk]:
                copy.wait()
        kappa = mix[k] * mask[k + 1].astype(jnp.float32)
        ratio, *reds, total = level_step(k, carry, kappa)
        ratios[k] = ratio
        u_out[0, k], u_out[1, k], v_out[0, k], v_out[1, k] = reds
        carry = (kappa, ratio, *reds, total)
    _, *sols, total = level_step(last, carry, zero)
    for copy in flats:
        copy.wait()
    total = total + surface[...]
    b_out[...] = total

    for k in range(last, -1, -1):
        if k < last:
            ratio = ratios[k]
            reds = (u_out[0, k], u_out[1, k], v_out[0, k], v_out[1, k])
            sols = [red + ratio * sol for red, sol in zip(reds, sols)]
        wet = mask[k].astype(jnp.float32)
        fields = [wet * sol for sol in sols]
        u_out[0, k], u_out[1, k], v_out[0, k], v_out[1, k] = fields
        for q, field in enumerate(fields):
            south_rows[q * levels + k : q * levels + k + 1, :] = field[0:1]
            north_rows[q * levels + k : q * levels + k + 1, :] = field[rows - 1 : rows]
    lane = lanes_of(shape)
    side = slice(LANES, 2 * LANES)
    west_pack[:, side] = zero
    east_pack[:, side] = zero
    for tile in range(2):
        west, east = zero, zero
        for spot in range(4 * min(32, levels - 32 * tile)):
            k, q = 32 * tile + spot // 4, spot % 4
            field = u_out[q, k] if q < 2 else v_out[q - 2, k]
            west = jnp.where(lane == spot, moved(field, 0, spot), west)
            east = jnp.where(lane == spot, moved(field, cols - 1, spot), east)
        west_pack[:, tile * LANES : (tile + 1) * LANES] = west
        east_pack[:, tile * LANES : (tile + 1) * LANES] = east
    value = east_pack[:, side]
    for k in range(levels):
        value = jnp.where(lane == 72 + k, moved(flow_east[k], cols - 1, 72 + k), value)
        north_rows[240 + k : 241 + k, :] = flow_north[k, BLOCK - 1 : BLOCK, :]
    east_pack[:, side] = value
    west, east = zero, zero
    for a, field in enumerate((total, c_east[...], c_north[...], diag[...])):
        here = (lane >= 4 * a) & (lane < 4 * a + 3)
        west = jnp.where(here, moved(field, 0, 4 * a), west)
        east = jnp.where(here, moved(field, cols - 3, 4 * a), east)
    west_pack[:, 2 * LANES :], east_pack[:, 2 * LANES :] = west, east


def rows_kernel(b, c_east, c_north, diag, west_in, east_in, _s, _n, south_rows, north_rows, side):
    shape = b.shape
    rows = shape[0]
    lane = lanes_of(shape)
    both = jnp.where(
        lane < 64, west_in[:, 2 * LANES :], moved(east_in[:, 2 * LANES :], 0, 64)
    )
    side[...] = both
    for a, field in enumerate((b, c_east, c_north, diag, side)):
        south_rows[8 * a : 8 * a + 8, :] = field[0:BLOCK, :]
        north_rows[8 * a : 8 * a + 8, :] = field[rows - BLOCK :, :]


def krylov_kernel(b, c_east, c_north, diag, side, south_in, north_in, v0_out, v1_out, v2_out, sums):
    rows = b.shape[0]
    sides = jnp.concatenate([south_in[232:240, :], side[...], north_in[232:240, :]], axis=0)
    lane = lanes_of(sides.shape)
    full = []
    for a, field in enumerate((b, c_east, c_north, diag)):
        at = slice(200 + 8 * a, 208 + 8 * a)
        main = jnp.concatenate([south_in[at, :], field[...], north_in[at, :]], axis=0)
        beside = jnp.where(
            lane >= LANES - 3,
            moved(sides, 4 * a, LANES - 3),
            jnp.where(lane < 3, moved(sides, 64 + 4 * a, 0), 0.0),
        )
        full.append(jnp.concatenate([main, beside], axis=1))
    vec, ce, cn, dg = full
    tall, wide = vec.shape
    cw = pltpu.roll(ce, 1, 1)
    cs = pltpu.roll(cn, 1, 0)
    vecs = [vec]
    for _ in range(3):
        vec = (
            dg * vec
            + ce * (vec - pltpu.roll(vec, wide - 1, 1))
            + cw * (vec - pltpu.roll(vec, 1, 1))
            + cn * (vec - pltpu.roll(vec, tall - 1, 0))
            + cs * (vec - pltpu.roll(vec, 1, 0))
        )
        vecs.append(vec)
    v0_out[...], v1_out[...], v2_out[...] = vecs[:3]
    inner = [value[BLOCK : BLOCK + rows, :LANES] for value in vecs]
    spot = lanes_of((1, LANES))
    row = jnp.zeros((1, LANES), jnp.float32)
    for n, (i, j) in enumerate(GRAM):
        part = jnp.sum(inner[i] * inner[j], axis=0, keepdims=True)
        row = jnp.where(spot == n, jnp.sum(part, axis=1, keepdims=True), row)
    sums[...] = row


def krylov_weights(gram):
    def form(left, right):
        total = 0.0
        for i, x in left.items():
            for j, y in right.items():
                total = total + x * y * gram[min(i, j), max(i, j)]
        return total

    one = jnp.ones_like(gram[0, 0])
    remain, search = {0: one}, {0: one}
    weights = {}
    norm = gram[0, 0]
    for iteration in range(3):
        image = {i + 1: x for i, x in search.items()}
        step = norm / form(search, image)
        for i, x in search.items():
            weights[i] = weights.get(i, 0.0) + step * x
        if iteration < 2:
            remain = {
                i: remain.get(i, 0.0) - step * image.get(i, 0.0) for i in range(iteration + 2)
            }
            renewed = form(remain, remain)
            ratio = renewed / norm
            search = {i: x + ratio * search.get(i, 0.0) for i, x in remain.items()}
            norm = renewed
    return weights


def fields_kernel(
    place, sums_in, v0, v1, v2, u, v, flow_east, flow_north, west_in, east_in, south_in, north_in,
    grad_out, x_out, rim, grad, x_full, south_lam, north_lam, lam_buf, flux_buf, sems,
):
    levels, rows, cols = flow_east.shape
    shape = (rows, cols)
    lane = lanes_of(shape)
    totals = jnp.sum(sums_in[...], axis=0, keepdims=True)
    gram = {pair: totals[:, n : n + 1] for n, pair in enumerate(GRAM)}
    weights = krylov_weights(gram)
    x_full[...] = weights[0] * v0[...] + weights[1] * v1[...] + weights[2] * v2[...]
    x = x_full[BLOCK : BLOCK + rows, :cols]
    x_out[...] = x
    count = 2 * levels
    south_lam[...] = (
        south_in[0:count, :] + south_in[count : 2 * count, :] * x_full[BLOCK - 1 : BLOCK, :cols]
    )
    north_lam[...] = (
        north_in[0:count, :]
        + north_in[count : 2 * count, :] * x_full[BLOCK + rows : BLOCK + rows + 1, :cols]
    )
    x_west = x_full[BLOCK : BLOCK + rows, 2 * LANES - 1 :]
    x_east = x_full[BLOCK : BLOCK + rows, LANES : LANES + 1]
    part = lane & 3
    halos = []
    for tile in range(2):
        at = slice(tile * LANES, (tile + 1) * LANES)
        west, east = west_in[:, at], east_in[:, at]
        west = west + pltpu.roll(west, LANES - 2, 1) * x_west
        east = east + pltpu.roll(east, LANES - 2, 1) * x_east
        later = jnp.where(part == 2, pltpu.roll(west, 1, 1), pltpu.roll(east, LANES - 1, 1))
        halos.append(jnp.where(part == 0, west, jnp.where(part == 1, east, later)))
    rim_row = jnp.where(place[1] == 0, 0, rows - 1)
    rim_shift = jnp.where(place[0] == 0, 0, 1)
    rim_base = 104
    rim[2 * levels : rim_base, :] = jnp.zeros((rim_base - 2 * levels, LANES), jnp.float32)
    copies = []
    for k in range(levels):
        fe, fn = 0.5 * flow_east[k], 0.5 * flow_north[k]
        fw = jnp.where(
            lane == 0, 0.5 * moved(west_in[:, LANES : 2 * LANES], 72 + k, 0), pltpu.roll(fe, 1, 1)
        )
        fs = 0.5 * south_in[240 + k : 241 + k, :]
        for s in range(2):
            n = s * levels + k
            slot = n % 10
            lam = u[s, k] + v[s, k] * x
            lam_buf[slot, 0:rows, :] = lam
            lam_buf[slot, rows : rows + 1, :] = north_lam[n : n + 1, :]
            halo = moved(halos[k // 32], 4 * (k % 32) + 2 * s, 0)
            east = jnp.where(lane == cols - 1, halo, pltpu.roll(lam, cols - 1, 1))
            west = jnp.where(lane == 0, halo, pltpu.roll(lam, 1, 1))
            flux = fn * (lam_buf[slot, 1 : rows + 1, :] - lam)
            flux_buf[slot, BLOCK : BLOCK + rows, :] = flux
            flux_buf[slot, BLOCK - 1 : BLOCK, :] = fs * (lam[0:1] - south_lam[n : n + 1, :])
            out = (
                lam
                + fe * (east - lam)
                + fw * (lam - west)
                + flux
                + flux_buf[slot, BLOCK - 1 : BLOCK - 1 + rows, :]
            )
            grad[s, k] = out
            rim[n : n + 1, :] = grad[s, k, pl.ds(rim_row, 1), :]
        if k % 10 == 9:
            at = pl.ds(k - 9, 10)
            copies.append(
                pltpu.make_async_copy(grad.at[:, at], grad_out.at[:, at], sems.at[k // 10])
            )
            copies[-1].start()
    rim_side = jnp.zeros(shape, jnp.float32)
    for n in range(2 * levels):
        rolled = moved(grad[n // levels, n % levels], 0, n)
        rim_side = jnp.where(lane == ((n - rim_shift) & (LANES - 1)), rolled, rim_side)
    rim[rim_base:, :] = pltpu.roll(rim_side, rim_shift, 1)
    for copy in copies:
        copy.wait()


def controls_kernel(place, rims, point_map, point_weight, out, beside):
    peers, rim_rows, _ = rims.shape
    depth = 104
    wide = rim_rows - depth
    share = 32 * SLOTS
    row_of = lax.broadcasted_iota(jnp.int32, (share, LANES), 0)

    def spread(ids, weights):
        return jnp.where(row_of == ids - place[0] * share, weights, 0.0)

    def window(ref, start):
        first = start // LANES
        second = jnp.minimum(first + 1, ref.shape[0] - 1)
        pair = jnp.concatenate([ref[pl.ds(first, 1), :], ref[pl.ds(second, 1), :]], axis=1)
        pair = pltpu.roll(pair, lax.rem(2 * LANES - lax.rem(start, LANES), 2 * LANES), 1)
        return pair[:, :LANES]

    lane = lanes_of((1, LANES))
    west_at = 2048 + place[1] * wide
    east_at = 3328 + place[1] * wide

    def joined(ref, fill):
        west, east = window(ref, west_at), window(ref, east_at)
        east = pltpu.roll(east, wide, 1)
        return jnp.where(lane < wide, west, jnp.where(lane < 2 * wide, east, fill))

    beside[...] = jnp.zeros_like(beside)
    beside[0:wide, :] = rims[0, depth:, :]
    beside[wide : 2 * wide, :] = rims[peers - 1, depth:, :]
    out[...] = lax.dot_general(
        spread(joined(point_map, -1), joined(point_weight, 0.0)),
        beside[...],
        (((1,), (0,)), ((), ())),
        precision=lax.Precision.HIGHEST,
        preferred_element_type=jnp.float32,
    )
    first = jnp.where(place[1] == 0, 0, peers)

    @pl.when((place[1] == 0) | (place[1] == 31))
    def _():
        total = jnp.zeros((share, depth), jnp.float32)
        for peer in range(peers):
            ids = point_map[pl.ds(first + peer, 1), :]
            weights = point_weight[pl.ds(first + peer, 1), :]
            total = total + lax.dot_general(
                spread(ids, weights),
                rims[peer, 0:depth, :],
                (((1,), (1,)), ((), ())),
                precision=lax.Precision.HIGHEST,
                preferred_element_type=jnp.float32,
            )
        out[:, 0:depth] = out[:, 0:depth] + total


def gather_kernel(parts, out):
    total = parts[0:SLOTS, :]
    for at in range(SLOTS, parts.shape[0], SLOTS):
        total = total + parts[at : at + SLOTS, :]
    levels = out.shape[2]
    out[:, 0, :] = total[0:SLOTS, 0:levels]
    out[:, 1, :] = total[0:SLOTS, levels : 2 * levels]


def shifted(value, axis, step):
    count = lax.axis_size(axis)
    pairs = [(i, i + step) for i in range(count) if 0 <= i + step < count]
    return lax.ppermute(value, axis, pairs)


def shape_of(*shape):
    return jax.ShapeDtypeStruct(shape, jnp.float32)


def per_device(
    tracer_adjoint,
    surface_adjoint,
    flow_east,
    flow_north,
    vertical_mix,
    land_mask,
    conduct_east,
    conduct_north,
    surface_diagonal,
    pressure_load,
    surface_forcing,
    control_map,
    control_weight,
):
    levels, rows, cols = flow_east.shape
    across, along = lax.axis_size("gx"), lax.axis_size("gy")
    place = jnp.stack([lax.axis_index("gx"), lax.axis_index("gy")]).astype(jnp.int32)
    point_map = control_map.reshape(-1, LANES)
    point_weight = control_weight.reshape(-1, LANES)

    tile = shape_of(rows, cols)
    field = shape_of(2, levels, rows, cols)
    pack = shape_of(rows, 3 * LANES)
    kept = pltpu.VMEM(field.shape, jnp.float32)
    south_shape, north_shape = shape_of(240, cols), shape_of(296, cols)
    b, u, v, west_pack, east_pack, south_rows, north_rows = pl.pallas_call(
        columns_kernel,
        out_shape=(tile, kept, kept, pack, pack, south_shape, north_shape),
        in_specs=[HBM] * 11,
        out_specs=(VMEM,) * 7,
        scratch_shapes=[
            pltpu.VMEM((levels, rows, cols), jnp.float32),
            pltpu.SMEM((2, levels), jnp.float32),
            pltpu.SMEM((2, levels), jnp.float32),
            pltpu.VMEM((2, levels, rows, cols), jnp.float32),
            pltpu.VMEM((rows, cols), jnp.float32),
            pltpu.VMEM((levels, rows, cols), jnp.float32),
            pltpu.VMEM((levels, BLOCK, cols), jnp.float32),
            pltpu.VMEM((levels - 1, rows, cols), jnp.float32),
            pltpu.VMEM((levels, rows, cols), jnp.int32),
            pltpu.VMEM((rows, cols), jnp.float32),
            pltpu.VMEM((rows, cols), jnp.float32),
            pltpu.VMEM((rows, cols), jnp.float32),
            pltpu.SemaphoreType.DMA((48,)),
        ],
        compiler_params=BIG,
        name="columns",
    )(
        *(
            pltpu.with_memory_space_constraint(value, pltpu.HBM)
            for value in (
                surface_forcing, pressure_load, tracer_adjoint, surface_adjoint, flow_east, flow_north,
                vertical_mix, land_mask, conduct_east, conduct_north, surface_diagonal,
            )
        )
    )
    stay = [pltpu.with_memory_space_constraint(value, pltpu.VMEM) for value in (u, v)]
    west_pack, place = lax.optimization_barrier((west_pack, place))
    west_in = shifted(east_pack, "gx", 1)
    east_in = shifted(west_pack, "gx", -1)
    outer = pl.BlockSpec((5 * BLOCK, cols), lambda i: (5, 0))
    south_rows, north_rows, side = pl.pallas_call(
        rows_kernel,
        out_shape=(south_shape, north_shape, tile),
        grid=(1,),
        in_specs=[VMEM] * 6 + [pl.BlockSpec(memory_space=pl.ANY)] * 2,
        out_specs=(outer, outer, VMEM),
        input_output_aliases={6: 0, 7: 1},
        compiler_params=SMALL,
        name="rows",
    )(b, conduct_east, conduct_north, surface_diagonal, west_in, east_in, south_rows, north_rows)
    south_in = shifted(north_rows, "gy", 1)
    north_in = shifted(south_rows, "gy", -1)
    full = shape_of(rows + 2 * BLOCK, 2 * LANES)
    v0, v1, v2, sums = pl.pallas_call(
        krylov_kernel,
        out_shape=(full, full, full, shape_of(1, LANES)),
        in_specs=[VMEM] * 7,
        out_specs=(VMEM,) * 4,
        compiler_params=SMALL,
        name="krylov",
    )(b, conduct_east, conduct_north, surface_diagonal, side, south_in, north_in)
    everyone = across * along
    sums = jnp.broadcast_to(sums[None], (everyone, 1, LANES))
    sums = lax.all_to_all(sums, ("gx", "gy"), 0, 0).reshape(everyone, LANES)
    rim_rows = 104 + rows
    tracer_grad, x, rim = pl.pallas_call(
        fields_kernel,
        out_shape=(field, tile, shape_of(rim_rows, LANES)),
        in_specs=[SMEM] + [VMEM] * 12,
        out_specs=(HBM, VMEM, VMEM),
        scratch_shapes=[
            pltpu.VMEM((2, levels, rows, cols), jnp.float32),
            pltpu.VMEM(full.shape, jnp.float32),
            pltpu.VMEM((2 * levels, cols), jnp.float32),
            pltpu.VMEM((2 * levels, cols), jnp.float32),
            pltpu.VMEM((10, rows + BLOCK, cols), jnp.float32),
            pltpu.VMEM((10, rows + BLOCK, cols), jnp.float32),
            pltpu.SemaphoreType.DMA((levels // 10,)),
        ],
        compiler_params=MIDDLE,
        name="fields",
    )(place, sums, v0, v1, v2, *stay, flow_east, flow_north, west_in, east_in, south_in, north_in)
    rims = lax.all_to_all(jnp.broadcast_to(rim[None], (across, rim_rows, LANES)), "gx", 0, 0)
    parts = pl.pallas_call(
        controls_kernel,
        out_shape=shape_of(along * SLOTS, LANES),
        in_specs=[SMEM] + [VMEM] * 3,
        out_specs=VMEM,
        scratch_shapes=[pltpu.VMEM((LANES, LANES), jnp.float32)],
        compiler_params=SMALL,
        name="controls",
    )(place, rims, point_map, point_weight)
    parts = lax.all_to_all(parts.reshape(along, 1, SLOTS * LANES), "gy", 0, 0)
    parts = parts.reshape(along * SLOTS, LANES)
    control_grad = pl.pallas_call(
        gather_kernel,
        out_shape=shape_of(SLOTS, 2, levels),
        in_specs=[VMEM],
        out_specs=VMEM,
        compiler_params=SMALL,
        name="gather",
    )(parts)
    return tracer_grad, x, jnp.transpose(control_grad, (1, 2, 0))


def solution(mesh):
    in_specs = (
        P(None, None, "gy", "gx"),
        P("gy", "gx"),
        P(None, "gy", "gx"),
        P(None, "gy", "gx"),
        P(None, "gy", "gx"),
        P(None, "gy", "gx"),
        P("gy", "gx"),
        P("gy", "gx"),
        P("gy", "gx"),
        P(),
        P(),
        P(),
        P(),
    )
    out_specs = (P(None, None, "gy", "gx"), P("gy", "gx"), P(None, None, ("gx", "gy")))
    return jax.shard_map(
        per_device, mesh=mesh, in_specs=in_specs, out_specs=out_specs, check_vma=False
    )
```

```python
import functools

import jax
import jax.numpy as jnp
from jax import lax
from jax.experimental import pallas as pl
from jax.experimental.pallas import tpu as pltpu
from jax.sharding import PartitionSpec as P

SLOTS = 10
LANES = 128
BLOCK = 8
GRAM = ((0, 0), (0, 1), (0, 2), (0, 3), (1, 1), (1, 2), (1, 3), (2, 2), (2, 3))
VMEM = pl.BlockSpec(memory_space=pltpu.VMEM)
SMEM = pl.BlockSpec(memory_space=pltpu.SMEM)
HBM = pl.BlockSpec(memory_space=pltpu.HBM)
MIB = 1024 * 1024
BIG = pltpu.CompilerParams(vmem_limit_bytes=16 * MIB)
MIDDLE = pltpu.CompilerParams(vmem_limit_bytes=12 * MIB)
SMALL = pltpu.CompilerParams(vmem_limit_bytes=3 * MIB)


def lanes_of(shape):
    return lax.broadcasted_iota(jnp.int32, shape, len(shape) - 1)


def moved(value, source, target):
    shift = target - source
    shift = shift % LANES if isinstance(shift, int) else lax.rem(shift + 4 * LANES, LANES)
    return pltpu.roll(value, shift, 1)


def columns_kernel(
    place, forcing_in, loads_in, tracer_in, surface_in, east_flow, north_flow, mix_in, mask_in, c_east_in,
    c_north_in, diag_in,
    b_out, u_hbm, v_hbm, west_pack, east_pack, west_inner, east_inner, south_rows, north_rows, inner_rows,
    u_out, v_out, ratios, forcing, loads, tracer, surface, flow_east, flow_north, mix, mask, c_east, c_north, diag,
    sems,
):
    levels, rows, cols = mask.shape
    shape = (rows, cols)
    zero = jnp.zeros(shape, jnp.float32)
    last = levels - 1
    chunk = 7
    started = []

    def fetch(source, target):
        copy = pltpu.make_async_copy(source, target, sems.at[len(started)])
        copy.start()
        started.append(copy)
        return copy

    scalars = [fetch(forcing_in, forcing), fetch(loads_in, loads)]
    chunks = []
    for at in range(0, last, chunk):
        here = pl.ds(at, chunk if at + chunk < last else chunk + 1)
        below = pl.ds(at + 1, chunk) if at else pl.ds(0, chunk + 1)
        chunks.append([
            fetch(mask_in.at[below], mask.at[below]),
            fetch(mix_in.at[pl.ds(at, chunk)], mix.at[pl.ds(at, chunk)]),
            fetch(tracer_in.at[:, here], tracer.at[:, here]),
        ])
    flats = [
        fetch(source, target)
        for source, target in (
            (surface_in, surface), (c_east_in, c_east), (c_north_in, c_north), (diag_in, diag),
            (north_flow.at[:, pl.ds(rows - BLOCK, BLOCK)], flow_north), (east_flow, flow_east),
        )
    ]
    for copy in scalars:
        copy.wait()

    def level_step(k, carry, kappa):
        before, ratio, r0, r1, r2, r3, total = carry
        wet = mask[k].astype(jnp.float32)
        t0, t1 = tracer[0, k], tracer[1, k]
        total = total + wet * (forcing[0, k] * t0 + forcing[1, k] * t1)
        inverse = 1.0 / (1.0 + before + kappa - before * ratio)
        r0 = (t0 + before * r0) * inverse
        r1 = (t1 + before * r1) * inverse
        r2 = (wet * loads[0, k] + before * r2) * inverse
        r3 = (wet * loads[1, k] + before * r3) * inverse
        return kappa * inverse, r0, r1, r2, r3, total

    carry = (zero,) * 7
    for k in range(last):
        if k % chunk == 0:
            for copy in chunks[k // chunk]:
                copy.wait()
        kappa = mix[k] * mask[k + 1].astype(jnp.float32)
        ratio, *reds, total = level_step(k, carry, kappa)
        ratios[k] = ratio
        u_out[0, k], u_out[1, k], v_out[0, k], v_out[1, k] = reds
        carry = (kappa, ratio, *reds, total)
    _, *sols, total = level_step(last, carry, zero)
    for copy in flats:
        copy.wait()
    total = total + surface[...]
    b_out[...] = total

    southern = place[1] == 0
    leaving = []
    for k in range(last, -1, -1):
        if k < last:
            ratio = ratios[k]
            reds = (u_out[0, k], u_out[1, k], v_out[0, k], v_out[1, k])
            sols = [red + ratio * sol for red, sol in zip(reds, sols)]
        wet = mask[k].astype(jnp.float32)
        fields = [wet * sol for sol in sols]
        u_out[0, k], u_out[1, k], v_out[0, k], v_out[1, k] = fields
        for q, field in enumerate(fields):
            line = slice(4 * k + q, 4 * k + q + 1)
            south_rows[line, :] = field[0:1]
            north_rows[line, :] = field[rows - 1 : rows]
            inner_rows[line, :] = jnp.where(southern, field[1:2], field[rows - 2 : rows - 1])
        if k % 10 == 0:
            at = pl.ds(k, 10)
            leaving += [
                fetch(buffer.at[:, at], target.at[:, at])
                for buffer, target in ((u_out, u_hbm), (v_out, v_hbm))
            ]
    lane = lanes_of((1, cols))
    side = slice(LANES, 2 * LANES)
    west_pack[:, side] = zero
    east_pack[:, side] = zero
    for tile in range(2):
        west, east, west_in, east_in = zero, zero, zero, zero
        for spot in range(4 * min(32, levels - 32 * tile)):
            k, q = 32 * tile + spot // 4, spot % 4
            field = u_out[q, k] if q < 2 else v_out[q - 2, k]
            turned = moved(field, 0, spot)
            west = jnp.where(lane == spot, turned, west)
            west_in = jnp.where(lane == (spot + 1) % LANES, turned, west_in)
            east = jnp.where(lane == (spot - 1) % LANES, turned, east)
            east_in = jnp.where(lane == (spot - 2) % LANES, turned, east_in)
        at = slice(tile * LANES, (tile + 1) * LANES)
        west_pack[:, at], east_pack[:, at] = west, moved(east, 0, 1)
        west_inner[:, at], east_inner[:, at] = moved(west_in, 1, 0), moved(east_in, 0, 2)
    value = east_pack[:, side]
    for k in range(levels):
        value = jnp.where(lane == 72 + k, moved(flow_east[k], cols - 1, 72 + k), value)
        north_rows[240 + k : 241 + k, :] = flow_north[k, BLOCK - 1 : BLOCK, :]
    east_pack[:, side] = value
    west, east = zero, zero
    for a, field in enumerate((total, c_east[...], c_north[...], diag[...])):
        here = (lane >= 4 * a) & (lane < 4 * a + 3)
        west = jnp.where(here, moved(field, 0, 4 * a), west)
        east = jnp.where(here, moved(field, cols - 3, 4 * a), east)
    west_pack[:, 2 * LANES :], east_pack[:, 2 * LANES :] = west, east
    for copy in leaving:
        copy.wait()


def rows_kernel(b, c_east, c_north, diag, west_in, east_in, _s, _n, south_rows, north_rows, side):
    shape = b.shape
    rows = shape[0]
    lane = lanes_of(shape)
    both = jnp.where(
        lane < 64, west_in[:, 2 * LANES :], moved(east_in[:, 2 * LANES :], 0, 64)
    )
    side[...] = both
    for a, field in enumerate((b, c_east, c_north, diag, side)):
        south_rows[8 * a : 8 * a + 8, :] = field[0:BLOCK, :]
        north_rows[8 * a : 8 * a + 8, :] = field[rows - BLOCK :, :]


def tall_transpose(value):
    rows, wide = value.shape
    if rows < LANES:
        value = jnp.concatenate([value, jnp.zeros((LANES - rows, wide), jnp.float32)], axis=0)
    tiles = [jnp.transpose(value[:, at : at + LANES]) for at in range(0, wide, LANES)]
    return jnp.concatenate(tiles, axis=0)


def rim_parts(center, inner, low, high, face_high, face_low, face_inner, last, factors):
    lane = lanes_of(center.shape)
    which = lax.broadcasted_iota(jnp.int32, center.shape, 0) & 3
    low = jnp.where(lane == 0, low, pltpu.roll(center, 1, 1))
    high = jnp.where(lane == last, high, pltpu.roll(center, LANES - 1, 1))
    face_low = jnp.where(lane == 0, face_low, pltpu.roll(face_high, 1, 1))
    parts = []
    for n, (f_center, f_inner, f_low, f_high) in enumerate(factors):
        if n == 0:
            f_center, f_inner, f_low, f_high = (
                jnp.where(which < 2, 1.0, f) for f in (f_center, f_inner, f_low, f_high)
            )
        here = center * f_center
        parts.append(
            here
            + 0.5 * face_high * (high * f_high - here)
            + 0.5 * face_low * (here - low * f_low)
            + 0.5 * face_inner * (inner * f_inner - here)
        )
    rows = center.shape[0]
    return parts[0], jnp.where(which >= 2, parts[1], pltpu.roll(parts[2], rows - 2, 0))


def krylov_kernel(
    place, b, c_east, c_north, diag, side, south_in, north_in, west_in, east_in,
    flow_east, flow_north, west_pack, east_pack, west_inner, east_inner, south_rows, north_rows, inner_rows,
    v0_out, v1_out, v2_out, out,
    high_buf, low_buf, face_buf, turned,
):
    levels, rows, cols = flow_east.shape
    sides = jnp.concatenate([south_in[232:240, :], side[...], north_in[232:240, :]], axis=0)
    lane = lanes_of(sides.shape)
    full = []
    for a, field in enumerate((b, c_east, c_north, diag)):
        at = slice(200 + 8 * a, 208 + 8 * a)
        main = jnp.concatenate([south_in[at, :], field[...], north_in[at, :]], axis=0)
        beside = jnp.where(
            lane >= LANES - 3,
            moved(sides, 4 * a, LANES - 3),
            jnp.where(lane < 3, moved(sides, 64 + 4 * a, 0), 0.0),
        )
        full.append(jnp.concatenate([main, beside], axis=1))
    vec, ce, cn, dg = full
    tall, wide = vec.shape
    cw = pltpu.roll(ce, 1, 1)
    cs = pltpu.roll(cn, 1, 0)
    vecs = [vec]
    for _ in range(3):
        vec = (
            dg * vec
            + ce * (vec - pltpu.roll(vec, wide - 1, 1))
            + cw * (vec - pltpu.roll(vec, 1, 1))
            + cn * (vec - pltpu.roll(vec, tall - 1, 0))
            + cs * (vec - pltpu.roll(vec, 1, 0))
        )
        vecs.append(vec)
    outs = (v0_out, v1_out, v2_out)
    for target, value in zip(outs, vecs):
        target[...] = value
    tiles = [value[BLOCK : BLOCK + rows, :LANES] for value in vecs]
    spot = lanes_of((1, LANES))
    row = jnp.zeros((1, LANES), jnp.float32)
    for n, (i, j) in enumerate(GRAM):
        part = jnp.sum(tiles[i] * tiles[j], axis=0, keepdims=True)
        row = jnp.where(spot == n, jnp.sum(part, axis=1, keepdims=True), row)
    groups = out.shape[0]
    out[...] = jnp.zeros_like(out)
    for group in range(groups):
        out[group, 96:97, :] = row
    count = 4 * levels
    used = -(-count // 32)

    def emit(parts, first, step):
        for group in range(used):
            length = min(32, count - 32 * group)
            for n, part in enumerate(parts):
                out[group, first + n * step : first + n * step + length, :] = part[
                    32 * group : 32 * group + length
                ]

    @pl.when((place[1] == 0) | (place[1] == place[3] - 1))
    def _():
        south = place[1] == 0
        at = jnp.where(south, 0, rows - 1)
        at_in = jnp.where(south, 1, rows - 2)
        sign = jnp.where(south, 1.0, -1.0)
        west_turned = tall_transpose(west_in[:, : 2 * LANES])
        west_turned = jnp.where(south, west_turned, moved(west_turned, rows - 1, 0))
        turned[...] = west_turned
        east_turned = tall_transpose(east_in[:, : 2 * LANES])
        high = jnp.where(
            south, moved(east_turned, 0, cols - 1), moved(east_turned, rows - 1, cols - 1)
        )
        for k in range(levels):
            four = slice(4 * k, 4 * k + 4)
            high_buf[four, :] = jnp.broadcast_to(flow_east[k, pl.ds(at, 1), :], (4, cols))
            low_buf[four, :] = jnp.broadcast_to(turned[count + k : count + k + 1, :], (4, cols))
            face_buf[four, :] = jnp.broadcast_to(
                sign * flow_north[k, pl.ds(jnp.where(south, 0, rows - 2), 1), :], (4, cols)
            )
        factors = []
        for value in outs:
            line = value[pl.ds(BLOCK + at, 1), :]
            factors.append((
                line[:, :cols], value[pl.ds(BLOCK + at_in, 1), :][:, :cols],
                pltpu.roll(line, 1, 1)[:, :cols], pltpu.roll(line, wide - 1, 1)[:, :cols],
            ))
        parts = rim_parts(
            jnp.where(south, south_rows[0:count, :], north_rows[0:count, :]),
            inner_rows[...], west_turned[0:count], high[0:count],
            high_buf[...], low_buf[...], face_buf[...], cols - 1, factors,
        )
        emit(parts, 0, 32)

    @pl.when((place[0] == 0) | (place[0] == place[2] - 1))
    def _():
        western = place[0] == 0
        at = jnp.where(western, 0, cols - 1)
        at_in = jnp.where(western, 1, cols - 2)
        sign = jnp.where(western, 1.0, -1.0)
        flat = lanes_of((rows, cols))
        norths = jnp.zeros((rows, cols), jnp.float32)
        easts = norths
        for k in range(levels):
            mark = jnp.where(western, k, (k - 1) % LANES)
            norths = jnp.where(flat == mark, moved(flow_north[k], 0, k), norths)
            mark = jnp.where(western, k, (k - 2) % LANES)
            easts = jnp.where(flat == mark, moved(flow_east[k], 0, k), easts)
        norths = jnp.where(western, norths, pltpu.roll(norths, 1, 1))
        easts = jnp.where(western, moved(easts, 0, 64), moved(easts, 0, 66))
        turned[0:LANES, :] = tall_transpose(jnp.where(flat < 64, norths, easts))
        for k in range(levels):
            four = slice(4 * k, 4 * k + 4)
            high_buf[four, :] = jnp.broadcast_to(turned[k : k + 1, :], (4, cols))
            face_buf[four, :] = jnp.broadcast_to(sign * turned[64 + k : 65 + k, :], (4, cols))
            low_buf[four, :] = jnp.broadcast_to(south_in[240 + k : 241 + k, :], (4, cols))

        def line_up(value, target):
            return jnp.where(western, moved(value, 0, target), moved(value, cols - 1, target))

        factors = []
        for value in outs:
            turned[0:LANES, :] = tall_transpose(value[:, :cols])
            line = pltpu.roll(turned[pl.ds(at, 1), :], LANES - BLOCK, 1)
            factors.append((
                line, pltpu.roll(turned[pl.ds(at_in, 1), :], LANES - BLOCK, 1),
                pltpu.roll(line, 1, 1), pltpu.roll(line, LANES - 1, 1),
            ))
        center = jnp.where(western, west_pack[:, : 2 * LANES], east_pack[:, : 2 * LANES])
        inside = jnp.where(western, west_inner[...], east_inner[...])
        first, second = rim_parts(
            tall_transpose(center)[0:count], tall_transpose(inside)[0:count],
            line_up(south_in[0:count, :], 0), line_up(north_in[0:count, :], rows - 1),
            high_buf[...], line_up(low_buf[...], 0), face_buf[...], rows - 1, factors,
        )
        half = lanes_of(first.shape) < 64
        emit((jnp.where(half, first, moved(second, 0, 64)),), 64, 0)


def krylov_weights(sums):
    gram = {pair: sums[0:1, n : n + 1] for n, pair in enumerate(GRAM)}

    def form(left, right):
        total = 0.0
        for i, x in left.items():
            for j, y in right.items():
                total = total + x * y * gram[min(i, j), max(i, j)]
        return total

    one = jnp.ones_like(gram[0, 0])
    remain, search = {0: one}, {0: one}
    weights = {}
    norm = gram[0, 0]
    for iteration in range(3):
        image = {i + 1: x for i, x in search.items()}
        step = norm / form(search, image)
        for i, x in search.items():
            weights[i] = weights.get(i, 0.0) + step * x
        if iteration < 2:
            remain = {
                i: remain.get(i, 0.0) - step * image.get(i, 0.0) for i in range(iteration + 2)
            }
            renewed = form(remain, remain)
            ratio = renewed / norm
            search = {i: x + ratio * search.get(i, 0.0) for i, x in remain.items()}
            norm = renewed
    return weights


def fields_kernel(
    sums_in, v0, v1, v2, u_hbm, v_hbm, flow_east, flow_north, west_in, east_in, south_in, north_in,
    grad_out, x_out, u, v, grad, x_full, south_lam, north_lam, lam_buf, flux_buf, sems,
):
    levels, rows, cols = flow_east.shape
    shape = (rows, cols)
    arrivals = []
    for n, at in enumerate(range(0, levels, 10)):
        at = pl.ds(at, 10)
        arrivals.append([
            pltpu.make_async_copy(source.at[:, at], target.at[:, at], sems.at[5 + 2 * n + m])
            for m, (source, target) in enumerate(((u_hbm, u), (v_hbm, v)))
        ])
        for copy in arrivals[-1]:
            copy.start()
    lane = lanes_of(shape)
    weights = krylov_weights(sums_in)
    x_full[...] = weights[0] * v0[...] + weights[1] * v1[...] + weights[2] * v2[...]
    x = x_full[BLOCK : BLOCK + rows, :cols]
    x_out[...] = x
    count = 4 * levels
    for source, target, at in ((south_in, south_lam, BLOCK - 1), (north_in, north_lam, BLOCK + rows)):
        target[...] = source[0:count, :] + source[2 : count + 2, :] * x_full[at : at + 1, :cols]
    x_west = x_full[BLOCK : BLOCK + rows, 2 * LANES - 1 :]
    x_east = x_full[BLOCK : BLOCK + rows, LANES : LANES + 1]
    part = lane & 3
    halos = []
    for tile in range(2):
        at = slice(tile * LANES, (tile + 1) * LANES)
        west, east = west_in[:, at], east_in[:, at]
        west = west + pltpu.roll(west, LANES - 2, 1) * x_west
        east = east + pltpu.roll(east, LANES - 2, 1) * x_east
        later = jnp.where(part == 2, pltpu.roll(west, 1, 1), pltpu.roll(east, LANES - 1, 1))
        halos.append(jnp.where(part == 0, west, jnp.where(part == 1, east, later)))
    copies = []
    for k in range(levels):
        if k % 10 == 0:
            for copy in arrivals[k // 10]:
                copy.wait()
        fe, fn = 0.5 * flow_east[k], 0.5 * flow_north[k]
        fw = jnp.where(
            lane == 0, 0.5 * moved(west_in[:, LANES : 2 * LANES], 72 + k, 0), pltpu.roll(fe, 1, 1)
        )
        fs = 0.5 * south_in[240 + k : 241 + k, :]
        for s in range(2):
            n = s * levels + k
            slot = n % 10
            line = slice(4 * k + s, 4 * k + s + 1)
            lam = u[s, k] + v[s, k] * x
            lam_buf[slot, 0:rows, :] = lam
            lam_buf[slot, rows : rows + 1, :] = north_lam[line, :]
            halo = moved(halos[k // 32], 4 * (k % 32) + 2 * s, 0)
            east = jnp.where(lane == cols - 1, halo, pltpu.roll(lam, cols - 1, 1))
            west = jnp.where(lane == 0, halo, pltpu.roll(lam, 1, 1))
            flux = fn * (lam_buf[slot, 1 : rows + 1, :] - lam)
            flux_buf[slot, BLOCK : BLOCK + rows, :] = flux
            flux_buf[slot, BLOCK - 1 : BLOCK, :] = fs * (lam[0:1] - south_lam[line, :])
            out = (
                lam
                + fe * (east - lam)
                + fw * (lam - west)
                + flux
                + flux_buf[slot, BLOCK - 1 : BLOCK - 1 + rows, :]
            )
            grad[s, k] = out
        if k % 10 == 9:
            at = pl.ds(k - 9, 10)
            copies.append(
                pltpu.make_async_copy(grad.at[:, at], grad_out.at[:, at], sems.at[k // 10])
            )
            copies[-1].start()
    for copy in copies:
        copy.wait()


def controls_kernel(place, rims, point_map, point_weight, out, values, hot, halves):
    peers = rims.shape[0]
    wide = 40
    lane = lanes_of((1, LANES))

    def target_of(ids):
        column = lax.shift_right_logical(lax.shift_right_logical(ids, 6) * 13108, 16)
        local = ids - 320 * column
        row = lax.shift_right_logical(local * 6554, 16)
        return (column >> 2) * 1280 + row * 40 + (column & 3) * 10 + local - 10 * row

    def window(ref, start):
        first = start // LANES
        second = jnp.minimum(first + 1, ref.shape[0] - 1)
        pair = jnp.concatenate([ref[pl.ds(first, 1), :], ref[pl.ds(second, 1), :]], axis=1)
        pair = pltpu.roll(pair, lax.rem(2 * LANES - lax.rem(start, LANES), 2 * LANES), 1)
        return pair[:, :LANES]

    def joined(ref, fill):
        west = window(ref, 2048 + place[1] * wide)
        east = pltpu.roll(window(ref, 3328 + place[1] * wide), wide, 1)
        return jnp.where(lane < wide, west, jnp.where(lane < 2 * wide, east, fill))

    def split(value, at):
        for piece in range(3):
            part = value.astype(jnp.bfloat16)
            values[64 * piece : 64 * piece + 64, at : at + LANES] = part
            value = value - part.astype(jnp.float32)

    def unfolded(peer):
        both = rims[peer, 64:96, :]
        return jnp.concatenate([both, moved(both, 64, 0)], axis=0)

    beside = jnp.where(
        lane < wide, unfolded(0), jnp.where(lane < 2 * wide, moved(unfolded(peers - 1), 0, wide), 0.0)
    )
    split(beside * joined(point_weight, 0.0), 0)
    beside_target = target_of(joined(point_map, 0))

    def spread(targets, length):
        block = 512
        height = lax.broadcasted_iota(jnp.int32, (block, LANES), 0)
        for at in range(0, 2560, block):
            here = slice(at, at + block)
            for n, target in enumerate(targets):
                hit = jnp.where(height == target - at, 1.0, 0.0)
                hot[here, n * LANES : (n + 1) * LANES] = hit.astype(jnp.bfloat16)
            got = lax.dot_general(
                hot[here, :length],
                values[:, :length],
                (((1,), (1,)), ((), ())),
                preferred_element_type=jnp.float32,
            )
            low = got[:, :LANES]
            high = jnp.concatenate([got[:, LANES:], got[:, LANES:]], axis=1)
            halves[here, :] = low + pltpu.roll(low, 64, 1) + high

    rim = (place[1] == 0) | (place[1] == place[3] - 1)

    @pl.when(jnp.logical_not(rim))
    def _():
        spread([beside_target], LANES)

    @pl.when(rim)
    def _():
        first = jnp.where(place[1] == 0, 0, peers)
        targets = [beside_target]
        for peer in range(peers):
            split(rims[peer, 0:64, :] * point_weight[pl.ds(first + peer, 1), :], (peer + 1) * LANES)
            targets.append(target_of(point_map[pl.ds(first + peer, 1), :]))
        spread(targets, (peers + 1) * LANES)

    sums = rims[0, 96:97, :]
    for peer in range(1, peers):
        sums = sums + rims[peer, 96:97, :]
    for row in range(32):
        at = slice(40 * row, 40 * row + 40)
        above = slice(1280 + 40 * row, 1320 + 40 * row)
        out[41 * row : 41 * row + 40, :] = jnp.where(lane < 64, halves[at, :], halves[above, :])
        out[41 * row + 40 : 41 * row + 41, :] = sums


def join_kernel(parts, sums_out, out):
    total = parts[0:41, :]
    for at in range(41, parts.shape[0], 41):
        total = total + parts[at : at + 41, :]
    sums_out[...] = total[40:41]
    weights = krylov_weights(total[40:41])
    value = total[0:40]
    value = (
        value
        + weights[0] * pltpu.roll(value, LANES - 2, 1)
        + weights[1] * pltpu.roll(value, LANES - 34, 1)
        + weights[2] * pltpu.roll(value, LANES - 32, 1)
    )
    out[0:40, :] = value
    out[40:80, :] = pltpu.roll(value, 64, 1)


def gather_kernel(parts, out):
    levels = out.shape[2]
    source = lax.broadcasted_iota(jnp.int32, (LANES, LANES), 0)
    target = lanes_of((LANES, LANES))
    total = jnp.zeros((SLOTS, LANES), jnp.float32)
    for group in range(-(-levels // 8)):
        wanted = 64 * (source & 3) + 8 * group + (source >> 2)
        pick = (target == wanted) & ((source & 3) < 2) & (source < 32)
        total = total + jnp.dot(
            parts[SLOTS * group : SLOTS * group + SLOTS, :],
            jnp.where(pick, 1.0, 0.0),
            precision=lax.Precision.HIGHEST,
            preferred_element_type=jnp.float32,
        )
    out[:, 0, :] = total[:, 0:levels]
    out[:, 1, :] = total[:, 64 : 64 + levels]


def shifted(value, axis, step):
    count = lax.axis_size(axis)
    pairs = [(i, i + step) for i in range(count) if 0 <= i + step < count]
    return lax.ppermute(value, axis, pairs)


def in_hbm(value):
    return pltpu.with_memory_space_constraint(value, pltpu.HBM)


def shape_of(*shape):
    return jax.ShapeDtypeStruct(shape, jnp.float32)


def per_device(
    tracer_adjoint,
    surface_adjoint,
    flow_east,
    flow_north,
    vertical_mix,
    land_mask,
    conduct_east,
    conduct_north,
    surface_diagonal,
    pressure_load,
    surface_forcing,
    control_map,
    control_weight,
):
    levels, rows, cols = flow_east.shape
    across, along = lax.axis_size("gx"), lax.axis_size("gy")
    place = jnp.stack([lax.axis_index("gx"), lax.axis_index("gy"), across, along]).astype(jnp.int32)
    point_map = control_map.reshape(-1, LANES)
    point_weight = control_weight.reshape(-1, LANES)

    tile = shape_of(rows, cols)
    field = shape_of(2, levels, rows, cols)
    pack, inner = shape_of(rows, 3 * LANES), shape_of(rows, 2 * LANES)
    count = 4 * levels
    lines = shape_of(count, cols)
    south_shape, north_shape = shape_of(240, cols), shape_of(296, cols)
    b, u, v, west_pack, east_pack, west_inner, east_inner, south_rows, north_rows, inner_rows = pl.pallas_call(
        columns_kernel,
        out_shape=(tile, field, field, pack, pack, inner, inner, south_shape, north_shape, lines),
        in_specs=[SMEM] + [HBM] * 11,
        out_specs=(VMEM, HBM, HBM) + (VMEM,) * 7,
        scratch_shapes=[
            pltpu.VMEM(field.shape, jnp.float32),
            pltpu.VMEM(field.shape, jnp.float32),
            pltpu.VMEM((levels, rows, cols), jnp.float32),
            pltpu.SMEM((2, levels), jnp.float32),
            pltpu.SMEM((2, levels), jnp.float32),
            pltpu.VMEM((2, levels, rows, cols), jnp.float32),
            pltpu.VMEM((rows, cols), jnp.float32),
            pltpu.VMEM((levels, rows, cols), jnp.float32),
            pltpu.VMEM((levels, BLOCK, cols), jnp.float32),
            pltpu.VMEM((levels - 1, rows, cols), jnp.float32),
            pltpu.VMEM((levels, rows, cols), jnp.int32),
            pltpu.VMEM((rows, cols), jnp.float32),
            pltpu.VMEM((rows, cols), jnp.float32),
            pltpu.VMEM((rows, cols), jnp.float32),
            pltpu.SemaphoreType.DMA((48,)),
        ],
        compiler_params=BIG,
        name="columns",
    )(
        place,
        *(
            in_hbm(value)
            for value in (
                surface_forcing, pressure_load, tracer_adjoint, surface_adjoint, flow_east, flow_north,
                vertical_mix, land_mask, conduct_east, conduct_north, surface_diagonal,
            )
        ),
    )
    west_pack, place = lax.optimization_barrier((west_pack, place))
    west_in = shifted(east_pack, "gx", 1)
    east_in = shifted(west_pack, "gx", -1)
    outer = pl.BlockSpec((5 * BLOCK, cols), lambda i: (5, 0))
    south_rows, north_rows, side = pl.pallas_call(
        rows_kernel,
        out_shape=(south_shape, north_shape, tile),
        grid=(1,),
        in_specs=[VMEM] * 6 + [pl.BlockSpec(memory_space=pl.ANY)] * 2,
        out_specs=(outer, outer, VMEM),
        input_output_aliases={6: 0, 7: 1},
        compiler_params=SMALL,
        name="rows",
    )(b, conduct_east, conduct_north, surface_diagonal, west_in, east_in, south_rows, north_rows)
    south_in = shifted(north_rows, "gy", 1)
    north_in = shifted(south_rows, "gy", -1)
    full = shape_of(rows + 2 * BLOCK, 2 * LANES)
    v0, v1, v2, rims = pl.pallas_call(
        krylov_kernel,
        out_shape=(full, full, full, shape_of(across, 104, LANES)),
        in_specs=[SMEM] + [VMEM] * 18,
        out_specs=(VMEM,) * 4,
        scratch_shapes=[pltpu.VMEM((count, cols), jnp.float32)] * 3
        + [pltpu.VMEM((2 * LANES, LANES), jnp.float32)],
        compiler_params=MIDDLE,
        name="krylov",
    )(
        place, b, conduct_east, conduct_north, surface_diagonal, side, south_in, north_in, west_in, east_in,
        flow_east, flow_north, west_pack, east_pack, west_inner, east_inner, south_rows, north_rows, inner_rows,
    )
    rims = lax.all_to_all(rims, "gx", 0, 0)
    parts = pl.pallas_call(
        controls_kernel,
        out_shape=shape_of(along * 41, LANES),
        in_specs=[SMEM] + [VMEM] * 3,
        out_specs=VMEM,
        scratch_shapes=[
            pltpu.VMEM((192, (across + 1) * LANES), jnp.bfloat16),
            pltpu.VMEM((2560, (across + 1) * LANES), jnp.bfloat16),
            pltpu.VMEM((2560, LANES), jnp.float32),
        ],
        compiler_params=MIDDLE,
        name="controls",
    )(place, rims, point_map, point_weight)
    parts = lax.all_to_all(parts.reshape(along, 1, 41 * LANES), "gy", 0, 0)
    sums, joined = pl.pallas_call(
        join_kernel,
        out_shape=(shape_of(1, LANES), shape_of(across * SLOTS, LANES)),
        in_specs=[VMEM],
        out_specs=(VMEM,) * 2,
        compiler_params=SMALL,
        name="join",
    )(parts.reshape(along * 41, LANES))
    joined = lax.all_to_all(joined.reshape(across, 1, SLOTS * LANES), "gx", 0, 0)
    tracer_grad, x = pl.pallas_call(
        fields_kernel,
        out_shape=(field, tile),
        in_specs=[VMEM] * 4 + [HBM] * 2 + [VMEM] * 6,
        out_specs=(HBM, VMEM),
        scratch_shapes=[
            pltpu.VMEM(field.shape, jnp.float32),
            pltpu.VMEM(field.shape, jnp.float32),
            pltpu.VMEM((2, levels, rows, cols), jnp.float32),
            pltpu.VMEM(full.shape, jnp.float32),
            pltpu.VMEM((count, cols), jnp.float32),
            pltpu.VMEM((count, cols), jnp.float32),
            pltpu.VMEM((10, rows + BLOCK, cols), jnp.float32),
            pltpu.VMEM((10, rows + BLOCK, cols), jnp.float32),
            pltpu.SemaphoreType.DMA((15,)),
        ],
        compiler_params=MIDDLE,
        name="fields",
    )(sums, v0, v1, v2, in_hbm(u), in_hbm(v), flow_east, flow_north, west_in, east_in, south_in, north_in)
    control_grad = pl.pallas_call(
        gather_kernel,
        out_shape=shape_of(SLOTS, 2, levels),
        in_specs=[VMEM],
        out_specs=VMEM,
        compiler_params=SMALL,
        name="gather",
    )(joined.reshape(across * SLOTS, LANES))
    return tracer_grad, x, jnp.transpose(control_grad, (1, 2, 0))


def solution(mesh):
    in_specs = (
        P(None, None, "gy", "gx"),
        P("gy", "gx"),
        P(None, "gy", "gx"),
        P(None, "gy", "gx"),
        P(None, "gy", "gx"),
        P(None, "gy", "gx"),
        P("gy", "gx"),
        P("gy", "gx"),
        P("gy", "gx"),
        P(),
        P(),
        P(),
        P(),
    )
    out_specs = (P(None, None, "gy", "gx"), P("gy", "gx"), P(None, None, ("gx", "gy")))
    return jax.shard_map(
        per_device, mesh=mesh, in_specs=in_specs, out_specs=out_specs, check_vma=False
    )
```

```python
import functools

import jax
import jax.numpy as jnp
from jax import lax
from jax.experimental import pallas as pl
from jax.experimental.pallas import tpu as pltpu
from jax.sharding import PartitionSpec as P

SLOTS = 10
LANES = 128
BLOCK = 8
GROUP = 25
GRAM = ((0, 0), (0, 1), (0, 2), (0, 3), (1, 1), (1, 2), (1, 3), (2, 2), (2, 3))
VMEM = pl.BlockSpec(memory_space=pltpu.VMEM)
SMEM = pl.BlockSpec(memory_space=pltpu.SMEM)
HBM = pl.BlockSpec(memory_space=pltpu.HBM)
MIB = 1024 * 1024
BIG = pltpu.CompilerParams(vmem_limit_bytes=16 * MIB)
MIDDLE = pltpu.CompilerParams(vmem_limit_bytes=12 * MIB)
SMALL = pltpu.CompilerParams(vmem_limit_bytes=3 * MIB)


def lanes_of(shape):
    return lax.broadcasted_iota(jnp.int32, shape, len(shape) - 1)


def moved(value, source, target):
    shift = target - source
    shift = shift % LANES if isinstance(shift, int) else lax.rem(shift + 4 * LANES, LANES)
    return pltpu.roll(value, shift, 1)


def columns_kernel(
    place, forcing_in, loads_in, tracer_in, surface_in, east_flow, north_flow, mix_in, mask_in, c_east_in,
    c_north_in, diag_in,
    b_out, u_hbm, v_hbm, west_pack, east_pack, west_inner, east_inner, south_rows, north_rows, inner_rows,
    u_out, v_out, ratios, forcing, loads, tracer, surface, flow_east, flow_north, mix, mask, c_east, c_north, diag,
    sems,
):
    levels, rows, cols = mask.shape
    shape = (rows, cols)
    zero = jnp.zeros(shape, jnp.float32)
    last = levels - 1
    chunk = 7
    started = []

    def fetch(source, target):
        copy = pltpu.make_async_copy(source, target, sems.at[len(started)])
        copy.start()
        started.append(copy)
        return copy

    scalars = [fetch(forcing_in, forcing), fetch(loads_in, loads)]
    chunks = []
    for at in range(0, last, chunk):
        here = pl.ds(at, chunk if at + chunk < last else chunk + 1)
        below = pl.ds(at + 1, chunk) if at else pl.ds(0, chunk + 1)
        chunks.append([
            fetch(mask_in.at[below], mask.at[below]),
            fetch(mix_in.at[pl.ds(at, chunk)], mix.at[pl.ds(at, chunk)]),
            fetch(tracer_in.at[:, here], tracer.at[:, here]),
        ])
    flats = [
        fetch(source, target)
        for source, target in (
            (surface_in, surface), (c_east_in, c_east), (c_north_in, c_north), (diag_in, diag),
            (north_flow.at[:, pl.ds(rows - BLOCK, BLOCK)], flow_north), (east_flow, flow_east),
        )
    ]
    for copy in scalars:
        copy.wait()

    def level_step(k, carry, kappa):
        before, ratio, r0, r1, r2, r3, total = carry
        wet = mask[k].astype(jnp.float32)
        t0, t1 = tracer[0, k], tracer[1, k]
        total = total + wet * (forcing[0, k] * t0 + forcing[1, k] * t1)
        inverse = 1.0 / (1.0 + before + kappa - before * ratio)
        r0 = (t0 + before * r0) * inverse
        r1 = (t1 + before * r1) * inverse
        r2 = (wet * loads[0, k] + before * r2) * inverse
        r3 = (wet * loads[1, k] + before * r3) * inverse
        return kappa * inverse, r0, r1, r2, r3, total

    carry = (zero,) * 7
    for k in range(last):
        if k % chunk == 0:
            for copy in chunks[k // chunk]:
                copy.wait()
        kappa = mix[k] * mask[k + 1].astype(jnp.float32)
        ratio, *reds, total = level_step(k, carry, kappa)
        ratios[k] = ratio
        u_out[0, k], u_out[1, k], v_out[0, k], v_out[1, k] = reds
        carry = (kappa, ratio, *reds, total)
    _, *sols, total = level_step(last, carry, zero)
    for copy in flats:
        copy.wait()
    total = total + surface[...]
    b_out[...] = total

    southern = place[1] == 0
    leaving = []
    for k in range(last, -1, -1):
        if k < last:
            ratio = ratios[k]
            reds = (u_out[0, k], u_out[1, k], v_out[0, k], v_out[1, k])
            sols = [red + ratio * sol for red, sol in zip(reds, sols)]
        wet = mask[k].astype(jnp.float32)
        fields = [wet * sol for sol in sols]
        u_out[0, k], u_out[1, k], v_out[0, k], v_out[1, k] = fields
        for q, field in enumerate(fields):
            line = slice(4 * k + q, 4 * k + q + 1)
            south_rows[line, :] = field[0:1]
            north_rows[line, :] = field[rows - 1 : rows]
            inner_rows[line, :] = jnp.where(southern, field[1:2], field[rows - 2 : rows - 1])
        if k % 10 == 0:
            at = pl.ds(k, 10)
            leaving += [
                fetch(buffer.at[:, at], target.at[:, at])
                for buffer, target in ((u_out, u_hbm), (v_out, v_hbm))
            ]
    lane = lanes_of((1, cols))
    side = slice(LANES, 2 * LANES)
    west_pack[:, side] = zero
    east_pack[:, side] = zero
    for tile in range(2):
        west, east, west_in, east_in = zero, zero, zero, zero
        for spot in range(4 * min(32, levels - 32 * tile)):
            k, q = 32 * tile + spot // 4, spot % 4
            field = u_out[q, k] if q < 2 else v_out[q - 2, k]
            turned = moved(field, 0, spot)
            west = jnp.where(lane == spot, turned, west)
            west_in = jnp.where(lane == (spot + 1) % LANES, turned, west_in)
            east = jnp.where(lane == (spot - 1) % LANES, turned, east)
            east_in = jnp.where(lane == (spot - 2) % LANES, turned, east_in)
        at = slice(tile * LANES, (tile + 1) * LANES)
        west_pack[:, at], east_pack[:, at] = west, moved(east, 0, 1)
        west_inner[:, at], east_inner[:, at] = moved(west_in, 1, 0), moved(east_in, 0, 2)
    value = east_pack[:, side]
    for k in range(levels):
        value = jnp.where(lane == 72 + k, moved(flow_east[k], cols - 1, 72 + k), value)
        north_rows[240 + k : 241 + k, :] = flow_north[k, BLOCK - 1 : BLOCK, :]
    east_pack[:, side] = value
    west, east = zero, zero
    for a, field in enumerate((total, c_east[...], c_north[...], diag[...])):
        here = (lane >= 4 * a) & (lane < 4 * a + 3)
        west = jnp.where(here, moved(field, 0, 4 * a), west)
        east = jnp.where(here, moved(field, cols - 3, 4 * a), east)
    west_pack[:, 2 * LANES :], east_pack[:, 2 * LANES :] = west, east
    for copy in leaving:
        copy.wait()


def rows_kernel(b, c_east, c_north, diag, west_in, east_in, _s, _n, south_rows, north_rows, side):
    shape = b.shape
    rows = shape[0]
    lane = lanes_of(shape)
    both = jnp.where(
        lane < 64, west_in[:, 2 * LANES :], moved(east_in[:, 2 * LANES :], 0, 64)
    )
    side[...] = both
    for a, field in enumerate((b, c_east, c_north, diag, side)):
        south_rows[8 * a : 8 * a + 8, :] = field[0:BLOCK, :]
        north_rows[8 * a : 8 * a + 8, :] = field[rows - BLOCK :, :]


def tall_transpose(value):
    rows, wide = value.shape
    if rows < LANES:
        value = jnp.concatenate([value, jnp.zeros((LANES - rows, wide), jnp.float32)], axis=0)
    tiles = [jnp.transpose(value[:, at : at + LANES]) for at in range(0, wide, LANES)]
    return jnp.concatenate(tiles, axis=0)


def rim_parts(center, inner, low, high, face_high, face_low, face_inner, last, factors):
    lane = lanes_of(center.shape)
    which = lax.broadcasted_iota(jnp.int32, center.shape, 0) & 3
    low = jnp.where(lane == 0, low, pltpu.roll(center, 1, 1))
    high = jnp.where(lane == last, high, pltpu.roll(center, LANES - 1, 1))
    face_low = jnp.where(lane == 0, face_low, pltpu.roll(face_high, 1, 1))
    parts = []
    for n, (f_center, f_inner, f_low, f_high) in enumerate(factors):
        if n == 0:
            f_center, f_inner, f_low, f_high = (
                jnp.where(which < 2, 1.0, f) for f in (f_center, f_inner, f_low, f_high)
            )
        here = center * f_center
        parts.append(
            here
            + 0.5 * face_high * (high * f_high - here)
            + 0.5 * face_low * (here - low * f_low)
            + 0.5 * face_inner * (inner * f_inner - here)
        )
    rows = center.shape[0]
    return parts[0], jnp.where(which >= 2, parts[1], pltpu.roll(parts[2], rows - 2, 0))


def krylov_kernel(
    place, b, c_east, c_north, diag, side, south_in, north_in, west_in, east_in,
    flow_east, flow_north, west_pack, east_pack, west_inner, east_inner, south_rows, north_rows, inner_rows,
    v0_out, v1_out, v2_out, out,
    high_buf, low_buf, face_buf, turned,
):
    levels, rows, cols = flow_east.shape
    sides = jnp.concatenate([south_in[232:240, :], side[...], north_in[232:240, :]], axis=0)
    lane = lanes_of(sides.shape)
    full = []
    for a, field in enumerate((b, c_east, c_north, diag)):
        at = slice(200 + 8 * a, 208 + 8 * a)
        main = jnp.concatenate([south_in[at, :], field[...], north_in[at, :]], axis=0)
        beside = jnp.where(
            lane >= LANES - 3,
            moved(sides, 4 * a, LANES - 3),
            jnp.where(lane < 3, moved(sides, 64 + 4 * a, 0), 0.0),
        )
        full.append(jnp.concatenate([main, beside], axis=1))
    vec, ce, cn, dg = full
    tall, wide = vec.shape
    cw = pltpu.roll(ce, 1, 1)
    cs = pltpu.roll(cn, 1, 0)
    vecs = [vec]
    for _ in range(3):
        vec = (
            dg * vec
            + ce * (vec - pltpu.roll(vec, wide - 1, 1))
            + cw * (vec - pltpu.roll(vec, 1, 1))
            + cn * (vec - pltpu.roll(vec, tall - 1, 0))
            + cs * (vec - pltpu.roll(vec, 1, 0))
        )
        vecs.append(vec)
    outs = (v0_out, v1_out, v2_out)
    for target, value in zip(outs, vecs):
        target[...] = value
    tiles = [value[BLOCK : BLOCK + rows, :LANES] for value in vecs]
    spot = lanes_of((1, LANES))
    row = jnp.zeros((1, LANES), jnp.float32)
    for n, (i, j) in enumerate(GRAM):
        part = jnp.sum(tiles[i] * tiles[j], axis=0, keepdims=True)
        row = jnp.where(spot == n, jnp.sum(part, axis=1, keepdims=True), row)
    out[...] = jnp.zeros_like(out)
    for at in range(0, out.shape[0], GROUP):
        out[at + GROUP - 1 : at + GROUP, :] = row
    count = 4 * levels

    def emit(parts, first):
        for group in range(count // BLOCK):
            for n, part in enumerate(parts):
                at = GROUP * group + first + n * BLOCK
                out[at : at + BLOCK, :] = part[BLOCK * group : BLOCK * group + BLOCK]

    @pl.when((place[1] == 0) | (place[1] == place[3] - 1))
    def _():
        south = place[1] == 0
        at = jnp.where(south, 0, rows - 1)
        at_in = jnp.where(south, 1, rows - 2)
        sign = jnp.where(south, 1.0, -1.0)
        west_turned = tall_transpose(west_in[:, : 2 * LANES])
        west_turned = jnp.where(south, west_turned, moved(west_turned, rows - 1, 0))
        turned[...] = west_turned
        east_turned = tall_transpose(east_in[:, : 2 * LANES])
        high = jnp.where(
            south, moved(east_turned, 0, cols - 1), moved(east_turned, rows - 1, cols - 1)
        )
        for k in range(levels):
            four = slice(4 * k, 4 * k + 4)
            high_buf[four, :] = jnp.broadcast_to(flow_east[k, pl.ds(at, 1), :], (4, cols))
            low_buf[four, :] = jnp.broadcast_to(turned[count + k : count + k + 1, :], (4, cols))
            face_buf[four, :] = jnp.broadcast_to(
                sign * flow_north[k, pl.ds(jnp.where(south, 0, rows - 2), 1), :], (4, cols)
            )
        factors = []
        for value in outs:
            line = value[pl.ds(BLOCK + at, 1), :]
            factors.append((
                line[:, :cols], value[pl.ds(BLOCK + at_in, 1), :][:, :cols],
                pltpu.roll(line, 1, 1)[:, :cols], pltpu.roll(line, wide - 1, 1)[:, :cols],
            ))
        parts = rim_parts(
            jnp.where(south, south_rows[0:count, :], north_rows[0:count, :]),
            inner_rows[...], west_turned[0:count], high[0:count],
            high_buf[...], low_buf[...], face_buf[...], cols - 1, factors,
        )
        emit(parts, 0)

    @pl.when((place[0] == 0) | (place[0] == place[2] - 1))
    def _():
        western = place[0] == 0
        at = jnp.where(western, 0, cols - 1)
        at_in = jnp.where(western, 1, cols - 2)
        sign = jnp.where(western, 1.0, -1.0)
        flat = lanes_of((rows, cols))
        norths = jnp.zeros((rows, cols), jnp.float32)
        easts = norths
        for k in range(levels):
            mark = jnp.where(western, k, (k - 1) % LANES)
            norths = jnp.where(flat == mark, moved(flow_north[k], 0, k), norths)
            mark = jnp.where(western, k, (k - 2) % LANES)
            easts = jnp.where(flat == mark, moved(flow_east[k], 0, k), easts)
        norths = jnp.where(western, norths, pltpu.roll(norths, 1, 1))
        easts = jnp.where(western, moved(easts, 0, 64), moved(easts, 0, 66))
        turned[0:LANES, :] = tall_transpose(jnp.where(flat < 64, norths, easts))
        for k in range(levels):
            four = slice(4 * k, 4 * k + 4)
            high_buf[four, :] = jnp.broadcast_to(turned[k : k + 1, :], (4, cols))
            face_buf[four, :] = jnp.broadcast_to(sign * turned[64 + k : 65 + k, :], (4, cols))
            low_buf[four, :] = jnp.broadcast_to(south_in[240 + k : 241 + k, :], (4, cols))

        def line_up(value, target):
            return jnp.where(western, moved(value, 0, target), moved(value, cols - 1, target))

        factors = []
        for value in outs:
            turned[0:LANES, :] = tall_transpose(value[:, :cols])
            line = pltpu.roll(turned[pl.ds(at, 1), :], LANES - BLOCK, 1)
            factors.append((
                line, pltpu.roll(turned[pl.ds(at_in, 1), :], LANES - BLOCK, 1),
                pltpu.roll(line, 1, 1), pltpu.roll(line, LANES - 1, 1),
            ))
        center = jnp.where(western, west_pack[:, : 2 * LANES], east_pack[:, : 2 * LANES])
        inside = jnp.where(western, west_inner[...], east_inner[...])
        first, second = rim_parts(
            tall_transpose(center)[0:count], tall_transpose(inside)[0:count],
            line_up(south_in[0:count, :], 0), line_up(north_in[0:count, :], rows - 1),
            high_buf[...], line_up(low_buf[...], 0), face_buf[...], rows - 1, factors,
        )
        half = lanes_of(first.shape) < 64
        emit((jnp.where(half, first, moved(second, 0, 64)),), 2 * BLOCK)


def krylov_weights(sums):
    gram = {pair: sums[0:1, n : n + 1] for n, pair in enumerate(GRAM)}

    def form(left, right):
        total = 0.0
        for i, x in left.items():
            for j, y in right.items():
                total = total + x * y * gram[min(i, j), max(i, j)]
        return total

    one = jnp.ones_like(gram[0, 0])
    remain, search = {0: one}, {0: one}
    weights = {}
    norm = gram[0, 0]
    for iteration in range(3):
        image = {i + 1: x for i, x in search.items()}
        step = norm / form(search, image)
        for i, x in search.items():
            weights[i] = weights.get(i, 0.0) + step * x
        if iteration < 2:
            remain = {
                i: remain.get(i, 0.0) - step * image.get(i, 0.0) for i in range(iteration + 2)
            }
            renewed = form(remain, remain)
            ratio = renewed / norm
            search = {i: x + ratio * search.get(i, 0.0) for i, x in remain.items()}
            norm = renewed
    return weights


def fields_kernel(
    sums_in, v0, v1, v2, u_hbm, v_hbm, flow_east, flow_north, west_in, east_in, south_in, north_in,
    grad_out, x_out, u, v, grad, x_full, south_lam, north_lam, lam_buf, flux_buf, sems,
):
    levels, rows, cols = flow_east.shape
    shape = (rows, cols)
    arrivals = []
    for n, at in enumerate(range(0, levels, 10)):
        at = pl.ds(at, 10)
        arrivals.append([
            pltpu.make_async_copy(source.at[:, at], target.at[:, at], sems.at[5 + 2 * n + m])
            for m, (source, target) in enumerate(((u_hbm, u), (v_hbm, v)))
        ])
        for copy in arrivals[-1]:
            copy.start()
    lane = lanes_of(shape)
    weights = krylov_weights(sums_in)
    x_full[...] = weights[0] * v0[...] + weights[1] * v1[...] + weights[2] * v2[...]
    x = x_full[BLOCK : BLOCK + rows, :cols]
    x_out[...] = x
    count = 4 * levels
    for source, target, at in ((south_in, south_lam, BLOCK - 1), (north_in, north_lam, BLOCK + rows)):
        target[...] = source[0:count, :] + source[2 : count + 2, :] * x_full[at : at + 1, :cols]
    x_west = x_full[BLOCK : BLOCK + rows, 2 * LANES - 1 :]
    x_east = x_full[BLOCK : BLOCK + rows, LANES : LANES + 1]
    part = lane & 3
    halos = []
    for tile in range(2):
        at = slice(tile * LANES, (tile + 1) * LANES)
        west, east = west_in[:, at], east_in[:, at]
        west = west + pltpu.roll(west, LANES - 2, 1) * x_west
        east = east + pltpu.roll(east, LANES - 2, 1) * x_east
        later = jnp.where(part == 2, pltpu.roll(west, 1, 1), pltpu.roll(east, LANES - 1, 1))
        halos.append(jnp.where(part == 0, west, jnp.where(part == 1, east, later)))
    copies = []
    for k in range(levels):
        if k % 10 == 0:
            for copy in arrivals[k // 10]:
                copy.wait()
        fe, fn = 0.5 * flow_east[k], 0.5 * flow_north[k]
        fw = jnp.where(
            lane == 0, 0.5 * moved(west_in[:, LANES : 2 * LANES], 72 + k, 0), pltpu.roll(fe, 1, 1)
        )
        fs = 0.5 * south_in[240 + k : 241 + k, :]
        for s in range(2):
            n = s * levels + k
            slot = n % 10
            line = slice(4 * k + s, 4 * k + s + 1)
            lam = u[s, k] + v[s, k] * x
            lam_buf[slot, 0:rows, :] = lam
            lam_buf[slot, rows : rows + 1, :] = north_lam[line, :]
            halo = moved(halos[k // 32], 4 * (k % 32) + 2 * s, 0)
            east = jnp.where(lane == cols - 1, halo, pltpu.roll(lam, cols - 1, 1))
            west = jnp.where(lane == 0, halo, pltpu.roll(lam, 1, 1))
            flux = fn * (lam_buf[slot, 1 : rows + 1, :] - lam)
            flux_buf[slot, BLOCK : BLOCK + rows, :] = flux
            flux_buf[slot, BLOCK - 1 : BLOCK, :] = fs * (lam[0:1] - south_lam[line, :])
            out = (
                lam
                + fe * (east - lam)
                + fw * (lam - west)
                + flux
                + flux_buf[slot, BLOCK - 1 : BLOCK - 1 + rows, :]
            )
            grad[s, k] = out
        if k % 10 == 9:
            at = pl.ds(k - 9, 10)
            copies.append(
                pltpu.make_async_copy(grad.at[:, at], grad_out.at[:, at], sems.at[k // 10])
            )
            copies[-1].start()
    for copy in copies:
        copy.wait()


def controls_kernel(place, rims, point_map, point_weight, out, values, hot, total):
    peers, high, wide = out.shape
    lane = lanes_of((1, LANES))
    rows = 40
    tiles = rows * (rims.shape[0] // GROUP) // LANES

    def point_tile(n, value, row):
        value = value * point_weight[pl.ds(row, 1), :]
        ids = point_map[pl.ds(row, 1), :]
        column = lax.shift_right_logical(lax.shift_right_logical(ids, 6) * 13108, 16)
        here = slice(n * LANES, (n + 1) * LANES)
        for piece in range(3):
            part = value.astype(jnp.bfloat16).astype(jnp.float32)
            for peer in range(peers):
                at = high * (3 * peer + piece)
                mine = jnp.where(column == peer, part, 0.0)
                values[at : at + high, here] = mine.astype(jnp.bfloat16)
            value = value - part
        target = ids - 32 * SLOTS * column
        target = jnp.transpose(jnp.broadcast_to(target, (LANES, LANES)))
        across = lanes_of((LANES, LANES))
        for at in range(0, wide, LANES):
            hit = jnp.where(across == target - at, 1.0, 0.0)
            hot[here, at : at + LANES] = hit.astype(jnp.bfloat16)

    def product(depth):
        total[...] = jnp.dot(
            values[:, :depth], hot[:depth, :], preferred_element_type=jnp.float32
        )

    last = rims.shape[0] - GROUP
    point_tile(0, rims[0:high, :], place[0])
    point_tile(1, rims[last : last + high, :], peers + place[0])
    beside = (place[0] == 0) | (place[0] == place[2] - 1)

    @pl.when(jnp.logical_not(beside))
    def _():
        product(2 * LANES)

    @pl.when(beside)
    def _():
        first = jnp.where(place[0] == 0, 2 * peers, 2 * peers + tiles)
        for tile in range(tiles):
            parts = []
            for source in (0, 64):
                value = jnp.zeros((BLOCK, LANES), jnp.float32)
                for row in range(tile * LANES // rows, -(-(tile + 1) * LANES // rows)):
                    at = rows * row - tile * LANES
                    piece = rims[GROUP * row + 2 * BLOCK : GROUP * row + 3 * BLOCK, :]
                    value = jnp.where(
                        (lane >= at) & (lane < at + rows), moved(piece, source, at % LANES), value
                    )
                parts.append(value)
            point_tile(2 + tile, jnp.concatenate(parts, axis=0), first + tile)
        product((2 + tiles) * LANES)

    sums = rims[GROUP - 1 : GROUP, :]
    for at in range(GROUP, rims.shape[0], GROUP):
        sums = sums + rims[at + GROUP - 1 : at + GROUP, :]
    sums = pltpu.roll(sums, 64, 1)
    for peer in range(peers):
        at = 3 * high * peer
        out[peer] = (
            total[at : at + high] + total[at + high : at + 2 * high] + total[at + 2 * high : at + 3 * high]
        )
        at = slice(wide - LANES, wide)
        out[peer, 0:1, at] = jnp.where(lane < 64, out[peer, 0:1, at], sums)


def join_kernel(parts, sums_out, out, spread):
    total = jnp.sum(parts[...], axis=0)
    sums = pltpu.roll(total[0:1, 2 * LANES :], 64, 1)
    sums_out[...] = sums
    weights = krylov_weights(sums)
    first, second = total[0:BLOCK], total[BLOCK:]
    value = (
        first
        + weights[0] * pltpu.roll(first, BLOCK - 2, 0)
        + weights[1] * pltpu.roll(second, BLOCK - 2, 0)
        + weights[2] * second
    )
    spread[...] = jnp.zeros_like(spread)
    for source, target in ((0, 0), (4, 1), (1, 64), (5, 65)):
        spread[target : target + 1, :] = value[source : source + 1]
    for tile in range(3):
        at = slice(tile * LANES, min((tile + 1) * LANES, out.shape[0]))
        out[at, :] = jnp.transpose(spread[:, tile * LANES : (tile + 1) * LANES])[: at.stop - at.start]


def gather_kernel(parts, out):
    levels = out.shape[2]
    lane = lanes_of((1, LANES))
    total = jnp.zeros((SLOTS, LANES), jnp.float32)
    for pair in range(levels // 2):
        value = parts[SLOTS * pair : SLOTS * pair + SLOTS, :]
        total = jnp.where((lane & 63) >> 1 == pair, moved(value, 0, 2 * pair), total)
    out[:, 0, :] = total[:, 0:levels]
    out[:, 1, :] = total[:, 64 : 64 + levels]


def shifted(value, axis, step):
    count = lax.axis_size(axis)
    pairs = [(i, i + step) for i in range(count) if 0 <= i + step < count]
    return lax.ppermute(value, axis, pairs)


def in_hbm(value):
    return pltpu.with_memory_space_constraint(value, pltpu.HBM)


def shape_of(*shape):
    return jax.ShapeDtypeStruct(shape, jnp.float32)


def per_device(
    tracer_adjoint,
    surface_adjoint,
    flow_east,
    flow_north,
    vertical_mix,
    land_mask,
    conduct_east,
    conduct_north,
    surface_diagonal,
    pressure_load,
    surface_forcing,
    control_map,
    control_weight,
):
    levels, rows, cols = flow_east.shape
    across, along = lax.axis_size("gx"), lax.axis_size("gy")
    place = jnp.stack([lax.axis_index("gx"), lax.axis_index("gy"), across, along]).astype(jnp.int32)
    point_map = control_map.reshape(-1, LANES)
    point_weight = control_weight.reshape(-1, LANES)

    tile = shape_of(rows, cols)
    field = shape_of(2, levels, rows, cols)
    pack, inner = shape_of(rows, 3 * LANES), shape_of(rows, 2 * LANES)
    count = 4 * levels
    lines = shape_of(count, cols)
    south_shape, north_shape = shape_of(240, cols), shape_of(296, cols)
    b, u, v, west_pack, east_pack, west_inner, east_inner, south_rows, north_rows, inner_rows = pl.pallas_call(
        columns_kernel,
        out_shape=(tile, field, field, pack, pack, inner, inner, south_shape, north_shape, lines),
        in_specs=[SMEM] + [HBM] * 11,
        out_specs=(VMEM, HBM, HBM) + (VMEM,) * 7,
        scratch_shapes=[
            pltpu.VMEM(field.shape, jnp.float32),
            pltpu.VMEM(field.shape, jnp.float32),
            pltpu.VMEM((levels, rows, cols), jnp.float32),
            pltpu.SMEM((2, levels), jnp.float32),
            pltpu.SMEM((2, levels), jnp.float32),
            pltpu.VMEM((2, levels, rows, cols), jnp.float32),
            pltpu.VMEM((rows, cols), jnp.float32),
            pltpu.VMEM((levels, rows, cols), jnp.float32),
            pltpu.VMEM((levels, BLOCK, cols), jnp.float32),
            pltpu.VMEM((levels - 1, rows, cols), jnp.float32),
            pltpu.VMEM((levels, rows, cols), jnp.int32),
            pltpu.VMEM((rows, cols), jnp.float32),
            pltpu.VMEM((rows, cols), jnp.float32),
            pltpu.VMEM((rows, cols), jnp.float32),
            pltpu.SemaphoreType.DMA((48,)),
        ],
        compiler_params=BIG,
        name="columns",
    )(
        place,
        *(
            in_hbm(value)
            for value in (
                surface_forcing, pressure_load, tracer_adjoint, surface_adjoint, flow_east, flow_north,
                vertical_mix, land_mask, conduct_east, conduct_north, surface_diagonal,
            )
        ),
    )
    west_pack, place = lax.optimization_barrier((west_pack, place))
    west_in = shifted(east_pack, "gx", 1)
    east_in = shifted(west_pack, "gx", -1)
    outer = pl.BlockSpec((5 * BLOCK, cols), lambda i: (5, 0))
    south_rows, north_rows, side = pl.pallas_call(
        rows_kernel,
        out_shape=(south_shape, north_shape, tile),
        grid=(1,),
        in_specs=[VMEM] * 6 + [pl.BlockSpec(memory_space=pl.ANY)] * 2,
        out_specs=(outer, outer, VMEM),
        input_output_aliases={6: 0, 7: 1},
        compiler_params=SMALL,
        name="rows",
    )(b, conduct_east, conduct_north, surface_diagonal, west_in, east_in, south_rows, north_rows)
    south_in = shifted(north_rows, "gy", 1)
    north_in = shifted(south_rows, "gy", -1)
    full = shape_of(rows + 2 * BLOCK, 2 * LANES)
    v0, v1, v2, rims = pl.pallas_call(
        krylov_kernel,
        out_shape=(full, full, full, shape_of(along * GROUP, LANES)),
        in_specs=[SMEM] + [VMEM] * 18,
        out_specs=(VMEM,) * 4,
        scratch_shapes=[pltpu.VMEM((count, cols), jnp.float32)] * 3
        + [pltpu.VMEM((2 * LANES, LANES), jnp.float32)],
        compiler_params=MIDDLE,
        name="krylov",
    )(
        place, b, conduct_east, conduct_north, surface_diagonal, side, south_in, north_in, west_in, east_in,
        flow_east, flow_north, west_pack, east_pack, west_inner, east_inner, south_rows, north_rows, inner_rows,
    )
    rims = lax.all_to_all(rims.reshape(along, 1, GROUP * LANES), "gy", 0, 0)
    points = (2 + rows * along // LANES) * LANES
    parts = pl.pallas_call(
        controls_kernel,
        out_shape=shape_of(across, 16, 3 * LANES),
        in_specs=[SMEM] + [VMEM] * 3,
        out_specs=VMEM,
        scratch_shapes=[
            pltpu.VMEM((across * 48, points), jnp.bfloat16),
            pltpu.VMEM((points, 3 * LANES), jnp.bfloat16),
            pltpu.VMEM((across * 48, 3 * LANES), jnp.float32),
        ],
        compiler_params=MIDDLE,
        name="controls",
    )(place, rims.reshape(along * GROUP, LANES), point_map, point_weight)
    parts = lax.all_to_all(parts, "gx", 0, 0)
    sums, joined = pl.pallas_call(
        join_kernel,
        out_shape=(shape_of(1, LANES), shape_of(along * SLOTS, LANES)),
        in_specs=[VMEM],
        out_specs=(VMEM,) * 2,
        scratch_shapes=[pltpu.VMEM((LANES, 3 * LANES), jnp.float32)],
        compiler_params=SMALL,
        name="join",
    )(parts)
    joined = lax.all_to_all(joined.reshape(along, 1, SLOTS * LANES), "gy", 0, 0)
    tracer_grad, x = pl.pallas_call(
        fields_kernel,
        out_shape=(field, tile),
        in_specs=[VMEM] * 4 + [HBM] * 2 + [VMEM] * 6,
        out_specs=(HBM, VMEM),
        scratch_shapes=[
            pltpu.VMEM(field.shape, jnp.float32),
            pltpu.VMEM(field.shape, jnp.float32),
            pltpu.VMEM((2, levels, rows, cols), jnp.float32),
            pltpu.VMEM(full.shape, jnp.float32),
            pltpu.VMEM((count, cols), jnp.float32),
            pltpu.VMEM((count, cols), jnp.float32),
            pltpu.VMEM((10, rows + BLOCK, cols), jnp.float32),
            pltpu.VMEM((10, rows + BLOCK, cols), jnp.float32),
            pltpu.SemaphoreType.DMA((15,)),
        ],
        compiler_params=MIDDLE,
        name="fields",
    )(sums, v0, v1, v2, in_hbm(u), in_hbm(v), flow_east, flow_north, west_in, east_in, south_in, north_in)
    control_grad = pl.pallas_call(
        gather_kernel,
        out_shape=shape_of(SLOTS, 2, levels),
        in_specs=[VMEM],
        out_specs=VMEM,
        compiler_params=SMALL,
        name="gather",
    )(joined.reshape(along * SLOTS, LANES))
    return tracer_grad, x, jnp.transpose(control_grad, (1, 2, 0))


def solution(mesh):
    in_specs = (
        P(None, None, "gy", "gx"),
        P("gy", "gx"),
        P(None, "gy", "gx"),
        P(None, "gy", "gx"),
        P(None, "gy", "gx"),
        P(None, "gy", "gx"),
        P("gy", "gx"),
        P("gy", "gx"),
        P("gy", "gx"),
        P(),
        P(),
        P(),
        P(),
    )
    out_specs = (P(None, None, "gy", "gx"), P("gy", "gx"), P(None, None, ("gx", "gy")))
    return jax.shard_map(
        per_device, mesh=mesh, in_specs=in_specs, out_specs=out_specs, check_vma=False
    )
```

```python
import functools

import jax
import jax.numpy as jnp
from jax import lax
from jax.experimental import pallas as pl
from jax.experimental.pallas import tpu as pltpu
from jax.sharding import PartitionSpec as P

SLOTS = 10
LANES = 128
BLOCK = 8
GROUP = 25
GRAM = ((0, 0), (0, 1), (0, 2), (0, 3), (1, 1), (1, 2), (1, 3), (2, 2), (2, 3))
VMEM = pl.BlockSpec(memory_space=pltpu.VMEM)
SMEM = pl.BlockSpec(memory_space=pltpu.SMEM)
HBM = pl.BlockSpec(memory_space=pltpu.HBM)
MIB = 1024 * 1024
BIG = pltpu.CompilerParams(vmem_limit_bytes=16 * MIB)
MIDDLE = pltpu.CompilerParams(vmem_limit_bytes=12 * MIB)
SMALL = pltpu.CompilerParams(vmem_limit_bytes=3 * MIB)


def lanes_of(shape):
    return lax.broadcasted_iota(jnp.int32, shape, len(shape) - 1)


def moved(value, source, target):
    shift = target - source
    shift = shift % LANES if isinstance(shift, int) else lax.rem(shift + 4 * LANES, LANES)
    return pltpu.roll(value, shift, 1)


def columns_kernel(
    place, forcing_in, loads_in, tracer_in, surface_in, east_flow, north_flow, mix_in, mask_in, c_east_in,
    c_north_in, diag_in,
    b_out, u_out, v_out, first_pack, second_pack, west_inner, east_inner, edge_flow,
    ratios, forcing, loads, tracer, surface, flow_east, flow_north, mix, mask, c_east, c_north, diag,
    sems,
):
    levels, rows, cols = mask.shape
    shape = (rows, cols)
    zero = jnp.zeros(shape, jnp.float32)
    last = levels - 1
    chunk = 7
    started = []

    def fetch(source, target):
        copy = pltpu.make_async_copy(source, target, sems.at[len(started)])
        copy.start()
        started.append(copy)
        return copy

    scalars = [fetch(forcing_in, forcing), fetch(loads_in, loads)]
    chunks = []
    for at in range(0, last, chunk):
        here = pl.ds(at, chunk if at + chunk < last else chunk + 1)
        below = pl.ds(at + 1, chunk) if at else pl.ds(0, chunk + 1)
        chunks.append([
            fetch(mask_in.at[below], mask.at[below]),
            fetch(mix_in.at[pl.ds(at, chunk)], mix.at[pl.ds(at, chunk)]),
            fetch(tracer_in.at[:, here], tracer.at[:, here]),
        ])
    flats = [
        fetch(source, target)
        for source, target in (
            (surface_in, surface), (c_east_in, c_east), (c_north_in, c_north), (diag_in, diag),
            (north_flow.at[:, pl.ds(rows - BLOCK, BLOCK)], flow_north), (east_flow, flow_east),
        )
    ]
    for copy in scalars:
        copy.wait()

    def level_step(k, carry, kappa):
        before, ratio, r0, r1, r2, r3, total = carry
        wet = mask[k].astype(jnp.float32)
        t0, t1 = tracer[0, k], tracer[1, k]
        total = total + wet * (forcing[0, k] * t0 + forcing[1, k] * t1)
        inverse = 1.0 / (1.0 + before + kappa - before * ratio)
        r0 = (t0 + before * r0) * inverse
        r1 = (t1 + before * r1) * inverse
        r2 = (wet * loads[0, k] + before * r2) * inverse
        r3 = (wet * loads[1, k] + before * r3) * inverse
        return kappa * inverse, r0, r1, r2, r3, total

    carry = (zero,) * 7
    for k in range(last):
        if k % chunk == 0:
            for copy in chunks[k // chunk]:
                copy.wait()
        kappa = mix[k] * mask[k + 1].astype(jnp.float32)
        ratio, *reds, total = level_step(k, carry, kappa)
        ratios[k] = ratio
        u_out[0, k], u_out[1, k], v_out[0, k], v_out[1, k] = reds
        carry = (kappa, ratio, *reds, total)
    _, *sols, total = level_step(last, carry, zero)
    for copy in flats:
        copy.wait()
    total = total + surface[...]
    b_out[...] = total

    for k in range(last, -1, -1):
        if k < last:
            ratio = ratios[k]
            reds = (u_out[0, k], u_out[1, k], v_out[0, k], v_out[1, k])
            sols = [red + ratio * sol for red, sol in zip(reds, sols)]
        wet = mask[k].astype(jnp.float32)
        fields = [wet * sol for sol in sols]
        u_out[0, k], u_out[1, k], v_out[0, k], v_out[1, k] = fields
    lane = lanes_of((1, cols))
    even = (place[0] & 1) == 0

    def pack(at, west, east):
        first_pack[:, at] = jnp.where(even, east, west)
        second_pack[:, at] = jnp.where(even, west, east)

    for tile in range(2):
        west, east, west_in, east_in = zero, zero, zero, zero
        for spot in range(4 * min(32, levels - 32 * tile)):
            k, q = 32 * tile + spot // 4, spot % 4
            field = u_out[q, k] if q < 2 else v_out[q - 2, k]
            turned = moved(field, 0, spot)
            west = jnp.where(lane == spot, turned, west)
            west_in = jnp.where(lane == (spot + 1) % LANES, turned, west_in)
            east = jnp.where(lane == (spot - 1) % LANES, turned, east)
            east_in = jnp.where(lane == (spot - 2) % LANES, turned, east_in)
        at = slice(tile * LANES, (tile + 1) * LANES)
        east = moved(east, 0, 1)
        if tile == 1:
            for k in range(levels):
                east = jnp.where(lane == 72 + k, moved(flow_east[k], cols - 1, 72 + k), east)
        pack(at, west, east)
        west_inner[:, at], east_inner[:, at] = moved(west_in, 1, 0), moved(east_in, 0, 2)
    for k in range(levels):
        edge_flow[k : k + 1, :] = flow_north[k, BLOCK - 1 : BLOCK, :]
    west, east = zero, zero
    for a, field in enumerate((total, c_east[...], c_north[...], diag[...])):
        here = (lane >= 4 * a) & (lane < 4 * a + 3)
        west = jnp.where(here, moved(field, 0, 4 * a), west)
        east = jnp.where(here, moved(field, cols - 3, 4 * a), east)
    pack(slice(2 * LANES, 3 * LANES), west, east)

def store_kernel(place, u, v, edge_flow, u_hbm, v_hbm, first_rows, second_rows, inner_rows, sems):
    _, levels, rows, _ = u.shape
    copies = [
        pltpu.make_async_copy(source, target, sems.at[n])
        for n, (source, target) in enumerate(((u, u_hbm), (v, v_hbm)))
    ]
    for copy in copies:
        copy.start()
    even = (place[1] & 1) == 0
    picks = (
        (first_rows, jnp.where(even, rows - 1, 0)),
        (second_rows, jnp.where(even, 0, rows - 1)),
        (inner_rows, jnp.where(place[1] == 0, 1, rows - 2)),
    )
    for k in range(levels):
        for q in range(4):
            for target, row in picks:
                line = slice(4 * k + q, 4 * k + q + 1)
                target[line, :] = (u, v)[q // 2][q % 2, k, pl.ds(row, 1), :]
    for target in (first_rows, second_rows):
        target[240 : 240 + levels, :] = edge_flow[0:levels, :]
    for copy in copies:
        copy.wait()


def rows_kernel(
    place, b, c_east, c_north, diag, first_in, second_in, _f, _s,
    first_rows, second_rows, side, west_in, east_in,
):
    shape = b.shape
    rows = shape[0]
    lane = lanes_of(shape)
    even = (place[0] & 1) == 0
    west_in[...] = jnp.where(even, second_in[...], first_in[...])
    east_in[...] = jnp.where(even, first_in[...], second_in[...])
    side[...] = jnp.where(
        lane < 64, west_in[:, 2 * LANES :], moved(east_in[:, 2 * LANES :], 0, 64)
    )
    even = (place[1] & 1) == 0
    for a, field in enumerate((b, c_east, c_north, diag, side)):
        south, north = field[0:BLOCK, :], field[rows - BLOCK :, :]
        first_rows[BLOCK * a : BLOCK * a + BLOCK, :] = jnp.where(even, north, south)
        second_rows[BLOCK * a : BLOCK * a + BLOCK, :] = jnp.where(even, south, north)


def tall_transpose(value):
    rows, wide = value.shape
    if rows < LANES:
        value = jnp.concatenate([value, jnp.zeros((LANES - rows, wide), jnp.float32)], axis=0)
    tiles = [jnp.transpose(value[:, at : at + LANES]) for at in range(0, wide, LANES)]
    return jnp.concatenate(tiles, axis=0)


def rim_weights(center, inner, low, high, face_high, face_low, face_inner, last):
    lane = lanes_of(center.shape)
    low = jnp.where(lane == 0, low, pltpu.roll(center, 1, 1))
    high = jnp.where(lane == last, high, pltpu.roll(center, LANES - 1, 1))
    face_low = jnp.where(lane == 0, face_low, pltpu.roll(face_high, 1, 1))
    return (
        center * (1.0 - 0.5 * face_high + 0.5 * face_low - 0.5 * face_inner),
        0.5 * face_inner * inner,
        -0.5 * face_low * low,
        0.5 * face_high * high,
    )


def rim_parts(weights, factors):
    rows = weights[0].shape[0]
    which = lax.broadcasted_iota(jnp.int32, weights[0].shape, 0) & 3
    parts = []
    for n, values in enumerate(factors):
        if n == 0:
            values = [jnp.where(which < 2, 1.0, value) for value in values]
        parts.append(sum(weight * value for weight, value in zip(weights, values)))
    return parts[0], jnp.where(which >= 2, parts[1], pltpu.roll(parts[2], rows - 2, 0))


def prepare_kernel(
    place, flow_east, flow_north, west_in, east_in, first_pack, second_pack, west_inner, east_inner,
    first_rows, second_rows, inner_rows,
    line_out, side_out,
    high_buf, low_buf, face_buf, turned,
):
    levels, rows, cols = flow_east.shape
    count = 4 * levels

    @pl.when((place[1] == 0) | (place[1] == place[3] - 1))
    def _():
        south = place[1] == 0
        at = jnp.where(south, 0, rows - 1)
        sign = jnp.where(south, 1.0, -1.0)
        west_turned = tall_transpose(west_in[:, : 2 * LANES])
        west_turned = jnp.where(south, west_turned, moved(west_turned, rows - 1, 0))
        turned[...] = west_turned
        east_turned = tall_transpose(east_in[:, : 2 * LANES])
        high = jnp.where(
            south, moved(east_turned, 0, cols - 1), moved(east_turned, rows - 1, cols - 1)
        )
        for k in range(levels):
            four = slice(4 * k, 4 * k + 4)
            high_buf[four, :] = jnp.broadcast_to(flow_east[k, pl.ds(at, 1), :], (4, cols))
            low_buf[four, :] = jnp.broadcast_to(turned[count + k : count + k + 1, :], (4, cols))
            face_buf[four, :] = jnp.broadcast_to(
                sign * flow_north[k, pl.ds(jnp.where(south, 0, rows - 2), 1), :], (4, cols)
            )
        second = south == ((place[1] & 1) == 0)
        weights = rim_weights(
            jnp.where(second, second_rows[0:count, :], first_rows[0:count, :]),
            inner_rows[...], west_turned[0:count], high[0:count],
            high_buf[...], low_buf[...], face_buf[...], cols - 1,
        )
        for n, weight in enumerate(weights):
            line_out[n] = weight

    @pl.when((place[0] == 0) | (place[0] == place[2] - 1))
    def _():
        western = place[0] == 0
        sign = jnp.where(western, 1.0, -1.0)
        flat = lanes_of((rows, cols))
        norths = jnp.zeros((rows, cols), jnp.float32)
        easts = norths
        for k in range(levels):
            mark = jnp.where(western, k, (k - 1) % LANES)
            norths = jnp.where(flat == mark, moved(flow_north[k], 0, k), norths)
            mark = jnp.where(western, k, (k - 2) % LANES)
            easts = jnp.where(flat == mark, moved(flow_east[k], 0, k), easts)
        norths = jnp.where(western, norths, pltpu.roll(norths, 1, 1))
        easts = jnp.where(western, moved(easts, 0, 64), moved(easts, 0, 66))
        turned[0:LANES, :] = tall_transpose(jnp.where(flat < 64, norths, easts))
        for k in range(levels):
            four = slice(4 * k, 4 * k + 4)
            high_buf[four, :] = jnp.broadcast_to(turned[k : k + 1, :], (4, cols))
            face_buf[four, :] = jnp.broadcast_to(sign * turned[64 + k : 65 + k, :], (4, cols))

        second = western == ((place[0] & 1) == 0)
        center = jnp.where(second, second_pack[:, : 2 * LANES], first_pack[:, : 2 * LANES])
        inside = jnp.where(western, west_inner[...], east_inner[...])
        center = tall_transpose(center)[0:count]
        weights = rim_weights(
            center, tall_transpose(inside)[0:count], 0.0, 0.0, high_buf[...], 0.0, face_buf[...], rows - 1
        )
        for n, weight in enumerate((*weights, 0.5 * center, 0.5 * high_buf[...])):
            side_out[n] = weight


def krylov_kernel(
    place, b, c_east, c_north, diag, side, first_in, second_in, line_in, side_in,
    v0_out, v1_out, v2_out, out, south_in, north_in,
    low_buf, turned,
):
    rows, cols = b.shape
    count = line_in.shape[1]
    levels = count // 4
    even = (place[1] & 1) == 0
    south_in[...] = jnp.where(even, second_in[...], first_in[...])
    north_in[...] = jnp.where(even, first_in[...], second_in[...])
    sides = jnp.concatenate([south_in[232:240, :], side[...], north_in[232:240, :]], axis=0)
    lane = lanes_of(sides.shape)
    full = []
    for a, field in enumerate((b, c_east, c_north, diag)):
        at = slice(200 + 8 * a, 208 + 8 * a)
        main = jnp.concatenate([south_in[at, :], field[...], north_in[at, :]], axis=0)
        beside = jnp.where(
            lane >= LANES - 3,
            moved(sides, 4 * a, LANES - 3),
            jnp.where(lane < 3, moved(sides, 64 + 4 * a, 0), 0.0),
        )
        full.append(jnp.concatenate([main, beside], axis=1))
    vec, ce, cn, dg = full
    tall, wide = vec.shape
    cw = pltpu.roll(ce, 1, 1)
    cs = pltpu.roll(cn, 1, 0)
    vecs = [vec]
    for _ in range(3):
        vec = (
            dg * vec
            + ce * (vec - pltpu.roll(vec, wide - 1, 1))
            + cw * (vec - pltpu.roll(vec, 1, 1))
            + cn * (vec - pltpu.roll(vec, tall - 1, 0))
            + cs * (vec - pltpu.roll(vec, 1, 0))
        )
        vecs.append(vec)
    outs = (v0_out, v1_out, v2_out)
    for target, value in zip(outs, vecs):
        target[...] = value
    tiles = [value[BLOCK : BLOCK + rows, :LANES] for value in vecs]
    spot = lanes_of((1, LANES))
    row = jnp.zeros((1, LANES), jnp.float32)
    for n, (i, j) in enumerate(GRAM):
        part = jnp.sum(tiles[i] * tiles[j], axis=0, keepdims=True)
        row = jnp.where(spot == n, jnp.sum(part, axis=1, keepdims=True), row)
    out[...] = jnp.zeros_like(out)
    for at in range(0, out.shape[0], GROUP):
        out[at + GROUP - 1 : at + GROUP, :] = row

    def emit(parts, first):
        for group in range(count // BLOCK):
            for n, part in enumerate(parts):
                at = GROUP * group + first + n * BLOCK
                out[at : at + BLOCK, :] = part[BLOCK * group : BLOCK * group + BLOCK]

    @pl.when((place[1] == 0) | (place[1] == place[3] - 1))
    def _():
        south = place[1] == 0
        at = jnp.where(south, 0, rows - 1)
        at_in = jnp.where(south, 1, rows - 2)
        factors = []
        for value in outs:
            line = value[pl.ds(BLOCK + at, 1), :]
            factors.append((
                line[:, :cols], value[pl.ds(BLOCK + at_in, 1), :][:, :cols],
                pltpu.roll(line, 1, 1)[:, :cols], pltpu.roll(line, wide - 1, 1)[:, :cols],
            ))
        emit(rim_parts([line_in[n] for n in range(4)], factors), 0)

    @pl.when((place[0] == 0) | (place[0] == place[2] - 1))
    def _():
        western = place[0] == 0
        at = jnp.where(western, 0, cols - 1)
        at_in = jnp.where(western, 1, cols - 2)
        for k in range(levels):
            low_buf[4 * k : 4 * k + 4, :] = jnp.broadcast_to(south_in[240 + k : 241 + k, :], (4, cols))

        def line_up(value, target):
            return jnp.where(western, moved(value, 0, target), moved(value, cols - 1, target))

        factors = []
        for value in outs:
            turned[...] = tall_transpose(value[:, :cols])
            line = pltpu.roll(turned[pl.ds(at, 1), :], LANES - BLOCK, 1)
            factors.append((
                line, pltpu.roll(turned[pl.ds(at_in, 1), :], LANES - BLOCK, 1),
                pltpu.roll(line, 1, 1), pltpu.roll(line, LANES - 1, 1),
            ))
        here, inside, before, behind, center, face = (side_in[n] for n in range(6))
        spots = lanes_of(here.shape)
        low = line_up(low_buf[...], 0)
        here = here + jnp.where(spots == 0, low * center, 0.0)
        before = jnp.where(spots == 0, -0.5 * low * line_up(south_in[0:count, :], 0), before)
        behind = jnp.where(
            spots == rows - 1, face * line_up(north_in[0:count, :], rows - 1), behind
        )
        first, second = rim_parts((here, inside, before, behind), factors)
        half = lanes_of(first.shape) < 64
        emit((jnp.where(half, first, moved(second, 0, 64)),), 2 * BLOCK)


def krylov_weights(sums):
    gram = {pair: sums[0:1, n : n + 1] for n, pair in enumerate(GRAM)}

    def form(left, right):
        total = 0.0
        for i, x in left.items():
            for j, y in right.items():
                total = total + x * y * gram[min(i, j), max(i, j)]
        return total

    one = jnp.ones_like(gram[0, 0])
    remain, search = {0: one}, {0: one}
    weights = {}
    norm = gram[0, 0]
    for iteration in range(3):
        image = {i + 1: x for i, x in search.items()}
        step = norm / form(search, image)
        for i, x in search.items():
            weights[i] = weights.get(i, 0.0) + step * x
        if iteration < 2:
            remain = {
                i: remain.get(i, 0.0) - step * image.get(i, 0.0) for i in range(iteration + 2)
            }
            renewed = form(remain, remain)
            ratio = renewed / norm
            search = {i: x + ratio * search.get(i, 0.0) for i, x in remain.items()}
            norm = renewed
    return weights


def fields_kernel(
    sums_in, v0, v1, v2, u_hbm, v_hbm, flow_east, flow_north, west_in, east_in, south_in, north_in,
    grad_out, x_out, u, v, grad, x_full, south_lam, north_lam, lam_buf, flux_buf, sems,
):
    levels, rows, cols = flow_east.shape
    shape = (rows, cols)
    arrivals = []
    for n, at in enumerate(range(0, levels, 10)):
        at = pl.ds(at, 10)
        arrivals.append([
            pltpu.make_async_copy(source.at[:, at], target.at[:, at], sems.at[5 + 2 * n + m])
            for m, (source, target) in enumerate(((u_hbm, u), (v_hbm, v)))
        ])
        for copy in arrivals[-1]:
            copy.start()
    lane = lanes_of(shape)
    weights = krylov_weights(sums_in)
    x_full[...] = weights[0] * v0[...] + weights[1] * v1[...] + weights[2] * v2[...]
    x = x_full[BLOCK : BLOCK + rows, :cols]
    x_out[...] = x
    count = 4 * levels
    for source, target, at in ((south_in, south_lam, BLOCK - 1), (north_in, north_lam, BLOCK + rows)):
        target[...] = source[0:count, :] + source[2 : count + 2, :] * x_full[at : at + 1, :cols]
    x_west = x_full[BLOCK : BLOCK + rows, 2 * LANES - 1 :]
    x_east = x_full[BLOCK : BLOCK + rows, LANES : LANES + 1]
    part = lane & 3
    halos = []
    for tile in range(2):
        at = slice(tile * LANES, (tile + 1) * LANES)
        west, east = west_in[:, at], east_in[:, at]
        west = west + pltpu.roll(west, LANES - 2, 1) * x_west
        east = east + pltpu.roll(east, LANES - 2, 1) * x_east
        later = jnp.where(part == 2, pltpu.roll(west, 1, 1), pltpu.roll(east, LANES - 1, 1))
        halos.append(jnp.where(part == 0, west, jnp.where(part == 1, east, later)))
    copies = []
    for k in range(levels):
        if k % 10 == 0:
            for copy in arrivals[k // 10]:
                copy.wait()
        fe, fn = 0.5 * flow_east[k], 0.5 * flow_north[k]
        fw = jnp.where(
            lane == 0, 0.5 * moved(west_in[:, LANES : 2 * LANES], 72 + k, 0), pltpu.roll(fe, 1, 1)
        )
        fs = 0.5 * south_in[240 + k : 241 + k, :]
        for s in range(2):
            n = s * levels + k
            slot = n % 10
            line = slice(4 * k + s, 4 * k + s + 1)
            lam = u[s, k] + v[s, k] * x
            lam_buf[slot, 0:rows, :] = lam
            lam_buf[slot, rows : rows + 1, :] = north_lam[line, :]
            halo = moved(halos[k // 32], 4 * (k % 32) + 2 * s, 0)
            east = jnp.where(lane == cols - 1, halo, pltpu.roll(lam, cols - 1, 1))
            west = jnp.where(lane == 0, halo, pltpu.roll(lam, 1, 1))
            flux = fn * (lam_buf[slot, 1 : rows + 1, :] - lam)
            flux_buf[slot, BLOCK : BLOCK + rows, :] = flux
            flux_buf[slot, BLOCK - 1 : BLOCK, :] = fs * (lam[0:1] - south_lam[line, :])
            out = (
                lam
                + fe * (east - lam)
                + fw * (lam - west)
                + flux
                + flux_buf[slot, BLOCK - 1 : BLOCK - 1 + rows, :]
            )
            grad[s, k] = out
        if k % 10 == 9:
            at = pl.ds(k - 9, 10)
            copies.append(
                pltpu.make_async_copy(grad.at[:, at], grad_out.at[:, at], sems.at[k // 10])
            )
            copies[-1].start()
    for copy in copies:
        copy.wait()


def controls_kernel(place, rims, point_map, point_weight, out, values, hot, total):
    peers, high, wide = out.shape
    lane = lanes_of((1, LANES))
    rows = 40
    tiles = rows * (rims.shape[0] // GROUP) // LANES

    def point_tile(n, value, row):
        value = value * point_weight[pl.ds(row, 1), :]
        ids = point_map[pl.ds(row, 1), :]
        column = lax.shift_right_logical(lax.shift_right_logical(ids, 6) * 13108, 16)
        here = slice(n * LANES, (n + 1) * LANES)
        for piece in range(3):
            part = value.astype(jnp.bfloat16).astype(jnp.float32)
            for peer in range(peers):
                at = high * (3 * peer + piece)
                mine = jnp.where(column == peer, part, 0.0)
                values[at : at + high, here] = mine.astype(jnp.bfloat16)
            value = value - part
        target = ids - 32 * SLOTS * column
        target = jnp.transpose(jnp.broadcast_to(target, (LANES, LANES)))
        across = lanes_of((LANES, LANES))
        for at in range(0, wide, LANES):
            hit = jnp.where(across == target - at, 1.0, 0.0)
            hot[here, at : at + LANES] = hit.astype(jnp.bfloat16)

    def product(depth):
        total[...] = jnp.dot(
            values[:, :depth], hot[:depth, :], preferred_element_type=jnp.float32
        )

    last = rims.shape[0] - GROUP
    point_tile(0, rims[0:high, :], place[0])
    point_tile(1, rims[last : last + high, :], peers + place[0])
    beside = (place[0] == 0) | (place[0] == place[2] - 1)

    @pl.when(jnp.logical_not(beside))
    def _():
        product(2 * LANES)

    @pl.when(beside)
    def _():
        first = jnp.where(place[0] == 0, 2 * peers, 2 * peers + tiles)
        for tile in range(tiles):
            parts = []
            for source in (0, 64):
                value = jnp.zeros((BLOCK, LANES), jnp.float32)
                for row in range(tile * LANES // rows, -(-(tile + 1) * LANES // rows)):
                    at = rows * row - tile * LANES
                    piece = rims[GROUP * row + 2 * BLOCK : GROUP * row + 3 * BLOCK, :]
                    value = jnp.where(
                        (lane >= at) & (lane < at + rows), moved(piece, source, at % LANES), value
                    )
                parts.append(value)
            point_tile(2 + tile, jnp.concatenate(parts, axis=0), first + tile)
        product((2 + tiles) * LANES)

    sums = rims[GROUP - 1 : GROUP, :]
    for at in range(GROUP, rims.shape[0], GROUP):
        sums = sums + rims[at + GROUP - 1 : at + GROUP, :]
    sums = pltpu.roll(sums, 64, 1)
    for peer in range(peers):
        at = 3 * high * peer
        out[peer] = (
            total[at : at + high] + total[at + high : at + 2 * high] + total[at + 2 * high : at + 3 * high]
        )
        at = slice(wide - LANES, wide)
        out[peer, 0:1, at] = jnp.where(lane < 64, out[peer, 0:1, at], sums)


def join_kernel(parts, sums_out, out, spread):
    total = jnp.sum(parts[...], axis=0)
    sums = pltpu.roll(total[0:1, 2 * LANES :], 64, 1)
    sums_out[...] = sums
    weights = krylov_weights(sums)
    first, second = total[0:BLOCK], total[BLOCK:]
    value = (
        first
        + weights[0] * pltpu.roll(first, BLOCK - 2, 0)
        + weights[1] * pltpu.roll(second, BLOCK - 2, 0)
        + weights[2] * second
    )
    spread[...] = jnp.zeros_like(spread)
    for source, target in ((0, 0), (4, 1), (1, 64), (5, 65)):
        spread[target : target + 1, :] = value[source : source + 1]
    for tile in range(3):
        at = slice(tile * LANES, min((tile + 1) * LANES, out.shape[0]))
        out[at, :] = jnp.transpose(spread[:, tile * LANES : (tile + 1) * LANES])[: at.stop - at.start]


def gather_kernel(parts, out):
    levels = out.shape[2]
    lane = lanes_of((1, LANES))
    total = jnp.zeros((SLOTS, LANES), jnp.float32)
    for pair in range(levels // 2):
        value = parts[SLOTS * pair : SLOTS * pair + SLOTS, :]
        total = jnp.where((lane & 63) >> 1 == pair, moved(value, 0, 2 * pair), total)
    out[:, 0, :] = total[:, 0:levels]
    out[:, 1, :] = total[:, 64 : 64 + levels]


def swapped(value, axis, first):
    count = lax.axis_size(axis)
    pairs = []
    for low in range(0 if first else 1, count - 1, 2):
        pairs += [(low, low + 1), (low + 1, low)]
    return lax.ppermute(value, axis, pairs)


def in_vmem(value):
    return pltpu.with_memory_space_constraint(value, pltpu.VMEM)


def in_hbm(value):
    return pltpu.with_memory_space_constraint(value, pltpu.HBM)


def shape_of(*shape):
    return jax.ShapeDtypeStruct(shape, jnp.float32)


def per_device(
    tracer_adjoint,
    surface_adjoint,
    flow_east,
    flow_north,
    vertical_mix,
    land_mask,
    conduct_east,
    conduct_north,
    surface_diagonal,
    pressure_load,
    surface_forcing,
    control_map,
    control_weight,
):
    levels, rows, cols = flow_east.shape
    across, along = lax.axis_size("gx"), lax.axis_size("gy")
    place = jnp.stack([lax.axis_index("gx"), lax.axis_index("gy"), across, along]).astype(jnp.int32)
    point_map = control_map.reshape(-1, LANES)
    point_weight = control_weight.reshape(-1, LANES)

    tile = shape_of(rows, cols)
    field = shape_of(2, levels, rows, cols)
    pack, inner = shape_of(rows, 3 * LANES), shape_of(rows, 2 * LANES)
    count = 4 * levels
    lines = shape_of(count, cols)
    rows_shape = shape_of(296, cols)
    kept, away = pltpu.VMEM(field.shape, jnp.float32), pltpu.HBM(field.shape, jnp.float32)
    b, u, v, first_pack, second_pack, west_inner, east_inner, edge_flow = pl.pallas_call(
        columns_kernel,
        out_shape=(tile, kept, kept, pack, pack, inner, inner, shape_of(56, cols)),
        in_specs=[SMEM] + [HBM] * 11,
        out_specs=(VMEM,) * 8,
        scratch_shapes=[
            pltpu.VMEM((levels, rows, cols), jnp.float32),
            pltpu.SMEM((2, levels), jnp.float32),
            pltpu.SMEM((2, levels), jnp.float32),
            pltpu.VMEM((2, levels, rows, cols), jnp.float32),
            pltpu.VMEM((rows, cols), jnp.float32),
            pltpu.VMEM((levels, rows, cols), jnp.float32),
            pltpu.VMEM((levels, BLOCK, cols), jnp.float32),
            pltpu.VMEM((levels - 1, rows, cols), jnp.float32),
            pltpu.VMEM((levels, rows, cols), jnp.int32),
            pltpu.VMEM((rows, cols), jnp.float32),
            pltpu.VMEM((rows, cols), jnp.float32),
            pltpu.VMEM((rows, cols), jnp.float32),
            pltpu.SemaphoreType.DMA((48,)),
        ],
        compiler_params=BIG,
        name="columns",
    )(
        place,
        *(
            in_hbm(value)
            for value in (
                surface_forcing, pressure_load, tracer_adjoint, surface_adjoint, flow_east, flow_north,
                vertical_mix, land_mask, conduct_east, conduct_north, surface_diagonal,
            )
        ),
    )
    first_in = swapped(first_pack, "gx", True)
    second_in = swapped(second_pack, "gx", False)
    u, v, first_rows, second_rows, inner_rows = pl.pallas_call(
        store_kernel,
        out_shape=(away, away, rows_shape, rows_shape, lines),
        in_specs=[SMEM] + [VMEM] * 3,
        out_specs=(HBM, HBM, VMEM, VMEM, VMEM),
        scratch_shapes=[pltpu.SemaphoreType.DMA((2,))],
        cost_estimate=pl.CostEstimate(flops=10**6, bytes_accessed=8 * 10**6, transcendentals=0),
        compiler_params=SMALL,
        name="store",
    )(place, in_vmem(u), in_vmem(v), edge_flow)
    outer = pl.BlockSpec((5 * BLOCK, cols), lambda i: (5, 0))
    first_rows, second_rows, side, west_in, east_in = pl.pallas_call(
        rows_kernel,
        out_shape=(rows_shape, rows_shape, tile, pack, pack),
        grid=(1,),
        in_specs=[SMEM] + [VMEM] * 6 + [pl.BlockSpec(memory_space=pl.ANY)] * 2,
        out_specs=(outer, outer) + (VMEM,) * 3,
        input_output_aliases={7: 0, 8: 1},
        compiler_params=SMALL,
        name="rows",
    )(
        place, b, conduct_east, conduct_north, surface_diagonal, first_in, second_in,
        first_rows, second_rows,
    )
    first_in = swapped(first_rows, "gy", True)
    second_in = swapped(second_rows, "gy", False)
    full = shape_of(rows + 2 * BLOCK, 2 * LANES)
    line_weights, side_weights = pl.pallas_call(
        prepare_kernel,
        out_shape=(shape_of(4, count, cols), shape_of(6, count, cols)),
        in_specs=[SMEM] + [VMEM] * 11,
        out_specs=(VMEM,) * 2,
        scratch_shapes=[pltpu.VMEM((count, cols), jnp.float32)] * 3
        + [pltpu.VMEM((2 * LANES, LANES), jnp.float32)],
        cost_estimate=pl.CostEstimate(flops=10**6, bytes_accessed=4 * 10**6, transcendentals=0),
        compiler_params=MIDDLE,
        name="prepare",
    )(
        place, flow_east, flow_north, west_in, east_in, first_pack, second_pack, west_inner, east_inner,
        first_rows, second_rows, inner_rows,
    )
    v0, v1, v2, rims, south_in, north_in = pl.pallas_call(
        krylov_kernel,
        out_shape=(full, full, full, shape_of(along * GROUP, LANES), rows_shape, rows_shape),
        in_specs=[SMEM] + [VMEM] * 9,
        out_specs=(VMEM,) * 6,
        scratch_shapes=[
            pltpu.VMEM((count, cols), jnp.float32),
            pltpu.VMEM((LANES, LANES), jnp.float32),
        ],
        compiler_params=MIDDLE,
        name="krylov",
    )(
        place, b, conduct_east, conduct_north, surface_diagonal, side, first_in, second_in,
        line_weights, side_weights,
    )
    rims = lax.all_to_all(rims.reshape(along, 1, GROUP * LANES), "gy", 0, 0)
    points = (2 + rows * along // LANES) * LANES
    parts = pl.pallas_call(
        controls_kernel,
        out_shape=shape_of(across, 16, 3 * LANES),
        in_specs=[SMEM] + [VMEM] * 3,
        out_specs=VMEM,
        scratch_shapes=[
            pltpu.VMEM((across * 48, points), jnp.bfloat16),
            pltpu.VMEM((points, 3 * LANES), jnp.bfloat16),
            pltpu.VMEM((across * 48, 3 * LANES), jnp.float32),
        ],
        compiler_params=MIDDLE,
        name="controls",
    )(place, rims.reshape(along * GROUP, LANES), point_map, point_weight)
    parts = lax.all_to_all(parts, "gx", 0, 0)
    sums, joined = pl.pallas_call(
        join_kernel,
        out_shape=(shape_of(1, LANES), shape_of(along * SLOTS, LANES)),
        in_specs=[VMEM],
        out_specs=(VMEM,) * 2,
        scratch_shapes=[pltpu.VMEM((LANES, 3 * LANES), jnp.float32)],
        compiler_params=SMALL,
        name="join",
    )(parts)
    joined = lax.all_to_all(joined.reshape(along, 1, SLOTS * LANES), "gy", 0, 0)
    tracer_grad, x = pl.pallas_call(
        fields_kernel,
        out_shape=(field, tile),
        in_specs=[VMEM] * 4 + [HBM] * 2 + [VMEM] * 6,
        out_specs=(HBM, VMEM),
        scratch_shapes=[
            pltpu.VMEM(field.shape, jnp.float32),
            pltpu.VMEM(field.shape, jnp.float32),
            pltpu.VMEM((2, levels, rows, cols), jnp.float32),
            pltpu.VMEM(full.shape, jnp.float32),
            pltpu.VMEM((count, cols), jnp.float32),
            pltpu.VMEM((count, cols), jnp.float32),
            pltpu.VMEM((10, rows + BLOCK, cols), jnp.float32),
            pltpu.VMEM((10, rows + BLOCK, cols), jnp.float32),
            pltpu.SemaphoreType.DMA((15,)),
        ],
        compiler_params=MIDDLE,
        name="fields",
    )(sums, v0, v1, v2, in_hbm(u), in_hbm(v), flow_east, flow_north, west_in, east_in, south_in, north_in)
    control_grad = pl.pallas_call(
        gather_kernel,
        out_shape=shape_of(SLOTS, 2, levels),
        in_specs=[VMEM],
        out_specs=VMEM,
        compiler_params=SMALL,
        name="gather",
    )(joined.reshape(along * SLOTS, LANES))
    return tracer_grad, x, jnp.transpose(control_grad, (1, 2, 0))


def solution(mesh):
    in_specs = (
        P(None, None, "gy", "gx"),
        P("gy", "gx"),
        P(None, "gy", "gx"),
        P(None, "gy", "gx"),
        P(None, "gy", "gx"),
        P(None, "gy", "gx"),
        P("gy", "gx"),
        P("gy", "gx"),
        P("gy", "gx"),
        P(),
        P(),
        P(),
        P(),
    )
    out_specs = (P(None, None, "gy", "gx"), P("gy", "gx"), P(None, None, ("gx", "gy")))
    return jax.shard_map(
        per_device, mesh=mesh, in_specs=in_specs, out_specs=out_specs, check_vma=False
    )
```

```python
import functools

import jax
import jax.numpy as jnp
from jax import lax
from jax.experimental import pallas as pl
from jax.experimental.pallas import tpu as pltpu
from jax.sharding import PartitionSpec as P

SLOTS = 10
LANES = 128
BLOCK = 8
GROUP = 25
GRAM = ((0, 0), (0, 1), (0, 2), (0, 3), (1, 1), (1, 2), (1, 3), (2, 2), (2, 3))
VMEM = pl.BlockSpec(memory_space=pltpu.VMEM)
HBM = pl.BlockSpec(memory_space=pltpu.HBM)
MIB = 1024 * 1024
BIG = pltpu.CompilerParams(vmem_limit_bytes=16 * MIB)
MIDDLE = pltpu.CompilerParams(vmem_limit_bytes=12 * MIB)
SMALL = pltpu.CompilerParams(vmem_limit_bytes=3 * MIB)


def lanes_of(shape):
    return lax.broadcasted_iota(jnp.int32, shape, len(shape) - 1)


def own_place():
    axes = ("gx", "gy")
    return tuple(map(lax.axis_index, axes)) + tuple(map(lax.axis_size, axes))


def moved(value, source, target):
    shift = target - source
    shift = shift % LANES if isinstance(shift, int) else lax.rem(shift + 4 * LANES, LANES)
    return pltpu.roll(value, shift, 1)


def columns_kernel(
    forcing_in, loads_in, tracer_in, surface_in, east_flow, north_flow, mix_in, mask_in, c_east_in,
    c_north_in, diag_in,
    b_out, u_out, v_out, first_pack, second_pack, west_inner, east_inner, edge_flow,
    ratios, forcing, loads, tracer, surface, flow_east, flow_north, mix, mask, c_east, c_north, diag,
    sems,
):
    levels, rows, cols = mask.shape
    shape = (rows, cols)
    place = own_place()
    zero = jnp.zeros(shape, jnp.float32)
    last = levels - 1
    chunk = 7
    started = []

    def fetch(source, target):
        copy = pltpu.make_async_copy(source, target, sems.at[len(started)])
        copy.start()
        started.append(copy)
        return copy

    scalars = [fetch(forcing_in, forcing), fetch(loads_in, loads)]
    chunks = []
    for at in range(0, last, chunk):
        here = pl.ds(at, chunk if at + chunk < last else chunk + 1)
        below = pl.ds(at + 1, chunk) if at else pl.ds(0, chunk + 1)
        chunks.append([
            fetch(mask_in.at[below], mask.at[below]),
            fetch(mix_in.at[pl.ds(at, chunk)], mix.at[pl.ds(at, chunk)]),
            fetch(tracer_in.at[:, here], tracer.at[:, here]),
        ])
    flats = [
        fetch(source, target)
        for source, target in (
            (surface_in, surface), (c_east_in, c_east), (c_north_in, c_north), (diag_in, diag),
            (north_flow.at[:, pl.ds(rows - BLOCK, BLOCK)], flow_north), (east_flow, flow_east),
        )
    ]
    for copy in scalars:
        copy.wait()

    def level_step(k, carry, kappa):
        before, ratio, r0, r1, r2, r3, total = carry
        wet = mask[k].astype(jnp.float32)
        t0, t1 = tracer[0, k], tracer[1, k]
        total = total + wet * (forcing[0, k] * t0 + forcing[1, k] * t1)
        inverse = 1.0 / (1.0 + before + kappa - before * ratio)
        r0 = (t0 + before * r0) * inverse
        r1 = (t1 + before * r1) * inverse
        r2 = (wet * loads[0, k] + before * r2) * inverse
        r3 = (wet * loads[1, k] + before * r3) * inverse
        return kappa * inverse, r0, r1, r2, r3, total

    carry = (zero,) * 7
    for k in range(last):
        if k % chunk == 0:
            for copy in chunks[k // chunk]:
                copy.wait()
        kappa = mix[k] * mask[k + 1].astype(jnp.float32)
        ratio, *reds, total = level_step(k, carry, kappa)
        ratios[k] = ratio
        u_out[0, k], u_out[1, k], v_out[0, k], v_out[1, k] = reds
        carry = (kappa, ratio, *reds, total)
    _, *sols, total = level_step(last, carry, zero)
    for copy in flats:
        copy.wait()
    total = total + surface[...]
    b_out[...] = total

    for k in range(last, -1, -1):
        if k < last:
            ratio = ratios[k]
            reds = (u_out[0, k], u_out[1, k], v_out[0, k], v_out[1, k])
            sols = [red + ratio * sol for red, sol in zip(reds, sols)]
        wet = mask[k].astype(jnp.float32)
        fields = [wet * sol for sol in sols]
        u_out[0, k], u_out[1, k], v_out[0, k], v_out[1, k] = fields
    lane = lanes_of((1, cols))
    even = (place[0] & 1) == 0

    def pack(at, west, east):
        first_pack[:, at] = jnp.where(even, east, west)
        second_pack[:, at] = jnp.where(even, west, east)

    for tile in range(2):
        west, east, west_in, east_in = zero, zero, zero, zero
        for spot in range(4 * min(32, levels - 32 * tile)):
            k, q = 32 * tile + spot // 4, spot % 4
            field = u_out[q, k] if q < 2 else v_out[q - 2, k]
            turned = moved(field, 0, spot)
            west = jnp.where(lane == spot, turned, west)
            west_in = jnp.where(lane == (spot + 1) % LANES, turned, west_in)
            east = jnp.where(lane == (spot - 1) % LANES, turned, east)
            east_in = jnp.where(lane == (spot - 2) % LANES, turned, east_in)
        at = slice(tile * LANES, (tile + 1) * LANES)
        east = moved(east, 0, 1)
        if tile == 1:
            for k in range(levels):
                east = jnp.where(lane == 72 + k, moved(flow_east[k], cols - 1, 72 + k), east)
        pack(at, west, east)
        west_inner[:, at], east_inner[:, at] = moved(west_in, 1, 0), moved(east_in, 0, 2)
    for k in range(levels):
        edge_flow[k : k + 1, :] = flow_north[k, BLOCK - 1 : BLOCK, :]
    west, east = zero, zero
    for a, field in enumerate((total, c_east[...], c_north[...], diag[...])):
        here = (lane >= 4 * a) & (lane < 4 * a + 3)
        west = jnp.where(here, moved(field, 0, 4 * a), west)
        east = jnp.where(here, moved(field, cols - 3, 4 * a), east)
    pack(slice(2 * LANES, 3 * LANES), west, east)

def store_kernel(u, v, edge_flow, u_hbm, v_hbm, first_rows, second_rows, inner_rows, sems):
    _, levels, rows, _ = u.shape
    place = own_place()
    copies = [
        pltpu.make_async_copy(source, target, sems.at[n])
        for n, (source, target) in enumerate(((u, u_hbm), (v, v_hbm)))
    ]
    for copy in copies:
        copy.start()
    even = (place[1] & 1) == 0
    picks = (
        (first_rows, jnp.where(even, rows - 1, 0)),
        (second_rows, jnp.where(even, 0, rows - 1)),
        (inner_rows, jnp.where(place[1] == 0, 1, rows - 2)),
    )
    for k in range(levels):
        for q in range(4):
            for target, row in picks:
                line = slice(4 * k + q, 4 * k + q + 1)
                target[line, :] = (u, v)[q // 2][q % 2, k, pl.ds(row, 1), :]
    for target in (first_rows, second_rows):
        target[240 : 240 + levels, :] = edge_flow[0:levels, :]
    for copy in copies:
        copy.wait()


def rows_kernel(
    b, c_east, c_north, diag, first_in, second_in, _f, _s,
    first_rows, second_rows, side, west_in, east_in,
):
    shape = b.shape
    rows = shape[0]
    place = own_place()
    lane = lanes_of(shape)
    even = (place[0] & 1) == 0
    west_in[...] = jnp.where(even, second_in[...], first_in[...])
    east_in[...] = jnp.where(even, first_in[...], second_in[...])
    side[...] = jnp.where(
        lane < 64, west_in[:, 2 * LANES :], moved(east_in[:, 2 * LANES :], 0, 64)
    )
    even = (place[1] & 1) == 0
    for a, field in enumerate((b, c_east, c_north, diag, side)):
        south, north = field[0:BLOCK, :], field[rows - BLOCK :, :]
        first_rows[BLOCK * a : BLOCK * a + BLOCK, :] = jnp.where(even, north, south)
        second_rows[BLOCK * a : BLOCK * a + BLOCK, :] = jnp.where(even, south, north)


def tall_transpose(value):
    rows, wide = value.shape
    if rows < LANES:
        value = jnp.concatenate([value, jnp.zeros((LANES - rows, wide), jnp.float32)], axis=0)
    tiles = [jnp.transpose(value[:, at : at + LANES]) for at in range(0, wide, LANES)]
    return jnp.concatenate(tiles, axis=0)


def rim_weights(center, inner, low, high, face_high, face_low, face_inner, last):
    lane = lanes_of(center.shape)
    low = jnp.where(lane == 0, low, pltpu.roll(center, 1, 1))
    high = jnp.where(lane == last, high, pltpu.roll(center, LANES - 1, 1))
    face_low = jnp.where(lane == 0, face_low, pltpu.roll(face_high, 1, 1))
    return (
        center * (1.0 - 0.5 * face_high + 0.5 * face_low - 0.5 * face_inner),
        0.5 * face_inner * inner,
        -0.5 * face_low * low,
        0.5 * face_high * high,
    )


def rim_parts(weights, factors):
    rows = weights[0].shape[0]
    which = lax.broadcasted_iota(jnp.int32, weights[0].shape, 0) & 3
    parts = []
    for n, values in enumerate(factors):
        if n == 0:
            values = [jnp.where(which < 2, 1.0, value) for value in values]
        parts.append(sum(weight * value for weight, value in zip(weights, values)))
    return parts[0], jnp.where(which >= 2, parts[1], pltpu.roll(parts[2], rows - 2, 0))


def prepare_kernel(
    flow_east, flow_north, west_in, east_in, first_pack, second_pack, west_inner, east_inner,
    first_rows, second_rows, inner_rows,
    line_out, side_out,
    high_buf, low_buf, face_buf, turned,
):
    levels, rows, cols = flow_east.shape
    count = 4 * levels
    place = own_place()

    @pl.when((place[1] == 0) | (place[1] == place[3] - 1))
    def _():
        south = place[1] == 0
        at = jnp.where(south, 0, rows - 1)
        sign = jnp.where(south, 1.0, -1.0)
        west_turned = tall_transpose(west_in[:, : 2 * LANES])
        west_turned = jnp.where(south, west_turned, moved(west_turned, rows - 1, 0))
        turned[...] = west_turned
        east_turned = tall_transpose(east_in[:, : 2 * LANES])
        high = jnp.where(
            south, moved(east_turned, 0, cols - 1), moved(east_turned, rows - 1, cols - 1)
        )
        for k in range(levels):
            four = slice(4 * k, 4 * k + 4)
            high_buf[four, :] = jnp.broadcast_to(flow_east[k, pl.ds(at, 1), :], (4, cols))
            low_buf[four, :] = jnp.broadcast_to(turned[count + k : count + k + 1, :], (4, cols))
            face_buf[four, :] = jnp.broadcast_to(
                sign * flow_north[k, pl.ds(jnp.where(south, 0, rows - 2), 1), :], (4, cols)
            )
        second = south == ((place[1] & 1) == 0)
        weights = rim_weights(
            jnp.where(second, second_rows[0:count, :], first_rows[0:count, :]),
            inner_rows[...], west_turned[0:count], high[0:count],
            high_buf[...], low_buf[...], face_buf[...], cols - 1,
        )
        for n, weight in enumerate(weights):
            line_out[n] = weight

    @pl.when((place[0] == 0) | (place[0] == place[2] - 1))
    def _():
        western = place[0] == 0
        sign = jnp.where(western, 1.0, -1.0)
        flat = lanes_of((rows, cols))
        norths = jnp.zeros((rows, cols), jnp.float32)
        easts = norths
        for k in range(levels):
            mark = jnp.where(western, k, (k - 1) % LANES)
            norths = jnp.where(flat == mark, moved(flow_north[k], 0, k), norths)
            mark = jnp.where(western, k, (k - 2) % LANES)
            easts = jnp.where(flat == mark, moved(flow_east[k], 0, k), easts)
        norths = jnp.where(western, norths, pltpu.roll(norths, 1, 1))
        easts = jnp.where(western, moved(easts, 0, 64), moved(easts, 0, 66))
        turned[0:LANES, :] = tall_transpose(jnp.where(flat < 64, norths, easts))
        for k in range(levels):
            four = slice(4 * k, 4 * k + 4)
            high_buf[four, :] = jnp.broadcast_to(turned[k : k + 1, :], (4, cols))
            face_buf[four, :] = jnp.broadcast_to(sign * turned[64 + k : 65 + k, :], (4, cols))

        second = western == ((place[0] & 1) == 0)
        center = jnp.where(second, second_pack[:, : 2 * LANES], first_pack[:, : 2 * LANES])
        inside = jnp.where(western, west_inner[...], east_inner[...])
        center = tall_transpose(center)[0:count]
        weights = rim_weights(
            center, tall_transpose(inside)[0:count], 0.0, 0.0, high_buf[...], 0.0, face_buf[...], rows - 1
        )
        for n, weight in enumerate((*weights, 0.5 * center, 0.5 * high_buf[...])):
            side_out[n] = weight


def krylov_kernel(
    b, c_east, c_north, diag, side, first_in, second_in, line_in, side_in,
    v0_out, v1_out, v2_out, out, south_in, north_in,
    low_buf, turned,
):
    rows, cols = b.shape
    count = line_in.shape[1]
    levels = count // 4
    place = own_place()
    even = (place[1] & 1) == 0
    south_in[...] = jnp.where(even, second_in[...], first_in[...])
    north_in[...] = jnp.where(even, first_in[...], second_in[...])
    sides = jnp.concatenate([south_in[232:240, :], side[...], north_in[232:240, :]], axis=0)
    lane = lanes_of(sides.shape)
    full = []
    for a, field in enumerate((b, c_east, c_north, diag)):
        at = slice(200 + 8 * a, 208 + 8 * a)
        main = jnp.concatenate([south_in[at, :], field[...], north_in[at, :]], axis=0)
        beside = jnp.where(
            lane >= LANES - 3,
            moved(sides, 4 * a, LANES - 3),
            jnp.where(lane < 3, moved(sides, 64 + 4 * a, 0), 0.0),
        )
        full.append(jnp.concatenate([main, beside], axis=1))
    vec, ce, cn, dg = full
    tall, wide = vec.shape
    cw = pltpu.roll(ce, 1, 1)
    cs = pltpu.roll(cn, 1, 0)
    vecs = [vec]
    for _ in range(3):
        vec = (
            dg * vec
            + ce * (vec - pltpu.roll(vec, wide - 1, 1))
            + cw * (vec - pltpu.roll(vec, 1, 1))
            + cn * (vec - pltpu.roll(vec, tall - 1, 0))
            + cs * (vec - pltpu.roll(vec, 1, 0))
        )
        vecs.append(vec)
    outs = (v0_out, v1_out, v2_out)
    for target, value in zip(outs, vecs):
        target[...] = value
    tiles = [value[BLOCK : BLOCK + rows, :LANES] for value in vecs]
    spot = lanes_of((1, LANES))
    row = jnp.zeros((1, LANES), jnp.float32)
    for n, (i, j) in enumerate(GRAM):
        part = jnp.sum(tiles[i] * tiles[j], axis=0, keepdims=True)
        row = jnp.where(spot == n, jnp.sum(part, axis=1, keepdims=True), row)
    out[...] = jnp.zeros_like(out)
    for at in range(0, out.shape[0], GROUP):
        out[at + GROUP - 1 : at + GROUP, :] = row

    def emit(parts, first):
        for group in range(count // BLOCK):
            for n, part in enumerate(parts):
                at = GROUP * group + first + n * BLOCK
                out[at : at + BLOCK, :] = part[BLOCK * group : BLOCK * group + BLOCK]

    @pl.when((place[1] == 0) | (place[1] == place[3] - 1))
    def _():
        south = place[1] == 0
        at = jnp.where(south, 0, rows - 1)
        at_in = jnp.where(south, 1, rows - 2)
        factors = []
        for value in outs:
            line = value[pl.ds(BLOCK + at, 1), :]
            factors.append((
                line[:, :cols], value[pl.ds(BLOCK + at_in, 1), :][:, :cols],
                pltpu.roll(line, 1, 1)[:, :cols], pltpu.roll(line, wide - 1, 1)[:, :cols],
            ))
        emit(rim_parts([line_in[n] for n in range(4)], factors), 0)

    @pl.when((place[0] == 0) | (place[0] == place[2] - 1))
    def _():
        western = place[0] == 0
        at = jnp.where(western, 0, cols - 1)
        at_in = jnp.where(western, 1, cols - 2)
        for k in range(levels):
            low_buf[4 * k : 4 * k + 4, :] = jnp.broadcast_to(south_in[240 + k : 241 + k, :], (4, cols))

        def line_up(value, target):
            return jnp.where(western, moved(value, 0, target), moved(value, cols - 1, target))

        factors = []
        for value in outs:
            turned[...] = tall_transpose(value[:, :cols])
            line = pltpu.roll(turned[pl.ds(at, 1), :], LANES - BLOCK, 1)
            factors.append((
                line, pltpu.roll(turned[pl.ds(at_in, 1), :], LANES - BLOCK, 1),
                pltpu.roll(line, 1, 1), pltpu.roll(line, LANES - 1, 1),
            ))
        here, inside, before, behind, center, face = (side_in[n] for n in range(6))
        spots = lanes_of(here.shape)
        low = line_up(low_buf[...], 0)
        here = here + jnp.where(spots == 0, low * center, 0.0)
        before = jnp.where(spots == 0, -0.5 * low * line_up(south_in[0:count, :], 0), before)
        behind = jnp.where(
            spots == rows - 1, face * line_up(north_in[0:count, :], rows - 1), behind
        )
        first, second = rim_parts((here, inside, before, behind), factors)
        half = lanes_of(first.shape) < 64
        emit((jnp.where(half, first, moved(second, 0, 64)),), 2 * BLOCK)


def krylov_weights(sums):
    gram = {pair: sums[0:1, n : n + 1] for n, pair in enumerate(GRAM)}

    def form(left, right):
        total = 0.0
        for i, x in left.items():
            for j, y in right.items():
                total = total + x * y * gram[min(i, j), max(i, j)]
        return total

    one = jnp.ones_like(gram[0, 0])
    remain, search = {0: one}, {0: one}
    weights = {}
    norm = gram[0, 0]
    for iteration in range(3):
        image = {i + 1: x for i, x in search.items()}
        step = norm / form(search, image)
        for i, x in search.items():
            weights[i] = weights.get(i, 0.0) + step * x
        if iteration < 2:
            remain = {
                i: remain.get(i, 0.0) - step * image.get(i, 0.0) for i in range(iteration + 2)
            }
            renewed = form(remain, remain)
            ratio = renewed / norm
            search = {i: x + ratio * search.get(i, 0.0) for i, x in remain.items()}
            norm = renewed
    return weights


def fields_kernel(
    sums_in, v0, v1, v2, u_hbm, v_hbm, flow_east, flow_north, west_in, east_in, south_in, north_in,
    grad_out, x_out, u, v, grad, x_full, south_lam, north_lam, lam_buf, flux_buf, sems,
):
    levels, rows, cols = flow_east.shape
    shape = (rows, cols)
    arrivals = []
    for n, at in enumerate(range(0, levels, 10)):
        at = pl.ds(at, 10)
        arrivals.append([
            pltpu.make_async_copy(source.at[:, at], target.at[:, at], sems.at[5 + 2 * n + m])
            for m, (source, target) in enumerate(((u_hbm, u), (v_hbm, v)))
        ])
        for copy in arrivals[-1]:
            copy.start()
    lane = lanes_of(shape)
    weights = krylov_weights(sums_in)
    x_full[...] = weights[0] * v0[...] + weights[1] * v1[...] + weights[2] * v2[...]
    x = x_full[BLOCK : BLOCK + rows, :cols]
    x_out[...] = x
    count = 4 * levels
    for source, target, at in ((south_in, south_lam, BLOCK - 1), (north_in, north_lam, BLOCK + rows)):
        target[...] = source[0:count, :] + source[2 : count + 2, :] * x_full[at : at + 1, :cols]
    x_west = x_full[BLOCK : BLOCK + rows, 2 * LANES - 1 :]
    x_east = x_full[BLOCK : BLOCK + rows, LANES : LANES + 1]
    part = lane & 3
    halos = []
    for tile in range(2):
        at = slice(tile * LANES, (tile + 1) * LANES)
        west, east = west_in[:, at], east_in[:, at]
        west = west + pltpu.roll(west, LANES - 2, 1) * x_west
        east = east + pltpu.roll(east, LANES - 2, 1) * x_east
        later = jnp.where(part == 2, pltpu.roll(west, 1, 1), pltpu.roll(east, LANES - 1, 1))
        halos.append(jnp.where(part == 0, west, jnp.where(part == 1, east, later)))
    copies = []
    for k in range(levels):
        if k % 10 == 0:
            for copy in arrivals[k // 10]:
                copy.wait()
        fe, fn = 0.5 * flow_east[k], 0.5 * flow_north[k]
        fw = jnp.where(
            lane == 0, 0.5 * moved(west_in[:, LANES : 2 * LANES], 72 + k, 0), pltpu.roll(fe, 1, 1)
        )
        fs = 0.5 * south_in[240 + k : 241 + k, :]
        for s in range(2):
            n = s * levels + k
            slot = n % 10
            line = slice(4 * k + s, 4 * k + s + 1)
            lam = u[s, k] + v[s, k] * x
            lam_buf[slot, 0:rows, :] = lam
            lam_buf[slot, rows : rows + 1, :] = north_lam[line, :]
            halo = moved(halos[k // 32], 4 * (k % 32) + 2 * s, 0)
            east = jnp.where(lane == cols - 1, halo, pltpu.roll(lam, cols - 1, 1))
            west = jnp.where(lane == 0, halo, pltpu.roll(lam, 1, 1))
            flux = fn * (lam_buf[slot, 1 : rows + 1, :] - lam)
            flux_buf[slot, BLOCK : BLOCK + rows, :] = flux
            flux_buf[slot, BLOCK - 1 : BLOCK, :] = fs * (lam[0:1] - south_lam[line, :])
            out = (
                lam
                + fe * (east - lam)
                + fw * (lam - west)
                + flux
                + flux_buf[slot, BLOCK - 1 : BLOCK - 1 + rows, :]
            )
            grad[s, k] = out
        if k % 10 == 9:
            at = pl.ds(k - 9, 10)
            copies.append(
                pltpu.make_async_copy(grad.at[:, at], grad_out.at[:, at], sems.at[k // 10])
            )
            copies[-1].start()
    for copy in copies:
        copy.wait()


def controls_kernel(rims, point_map, point_weight, out, values, hot, total):
    peers, high, wide = out.shape
    place = own_place()
    lane = lanes_of((1, LANES))
    rows = 40
    tiles = rows * (rims.shape[0] // GROUP) // LANES

    def point_tile(n, value, row):
        value = value * point_weight[pl.ds(row, 1), :]
        ids = point_map[pl.ds(row, 1), :]
        column = lax.shift_right_logical(lax.shift_right_logical(ids, 6) * 13108, 16)
        here = slice(n * LANES, (n + 1) * LANES)
        for piece in range(3):
            part = value.astype(jnp.bfloat16).astype(jnp.float32)
            for peer in range(peers):
                at = high * (3 * peer + piece)
                mine = jnp.where(column == peer, part, 0.0)
                values[at : at + high, here] = mine.astype(jnp.bfloat16)
            value = value - part
        target = ids - 32 * SLOTS * column
        target = jnp.transpose(jnp.broadcast_to(target, (LANES, LANES)))
        across = lanes_of((LANES, LANES))
        for at in range(0, wide, LANES):
            hit = jnp.where(across == target - at, 1.0, 0.0)
            hot[here, at : at + LANES] = hit.astype(jnp.bfloat16)

    def product(depth):
        total[...] = jnp.dot(
            values[:, :depth], hot[:depth, :], preferred_element_type=jnp.float32
        )

    last = rims.shape[0] - GROUP
    point_tile(0, rims[0:high, :], place[0])
    point_tile(1, rims[last : last + high, :], peers + place[0])
    beside = (place[0] == 0) | (place[0] == place[2] - 1)

    @pl.when(jnp.logical_not(beside))
    def _():
        product(2 * LANES)

    @pl.when(beside)
    def _():
        first = jnp.where(place[0] == 0, 2 * peers, 2 * peers + tiles)
        for tile in range(tiles):
            parts = []
            for source in (0, 64):
                value = jnp.zeros((BLOCK, LANES), jnp.float32)
                for row in range(tile * LANES // rows, -(-(tile + 1) * LANES // rows)):
                    at = rows * row - tile * LANES
                    piece = rims[GROUP * row + 2 * BLOCK : GROUP * row + 3 * BLOCK, :]
                    value = jnp.where(
                        (lane >= at) & (lane < at + rows), moved(piece, source, at % LANES), value
                    )
                parts.append(value)
            point_tile(2 + tile, jnp.concatenate(parts, axis=0), first + tile)
        product((2 + tiles) * LANES)

    sums = [rims[at - 1 : at, :] for at in range(GROUP, rims.shape[0] + 1, GROUP)]
    while len(sums) > 1:
        sums = [a + b for a, b in zip(sums[0::2], sums[1::2])]
    sums = pltpu.roll(sums[0], 64, 1)
    for peer in range(peers):
        at = 3 * high * peer
        out[peer] = (
            total[at : at + high] + total[at + high : at + 2 * high] + total[at + 2 * high : at + 3 * high]
        )
        at = slice(wide - LANES, wide)
        out[peer, 0:1, at] = jnp.where(lane < 64, out[peer, 0:1, at], sums)


def join_kernel(parts, sums_out, out, spread):
    total = jnp.sum(parts[...], axis=0)
    sums = pltpu.roll(total[0:1, 2 * LANES :], 64, 1)
    sums_out[...] = sums
    weights = krylov_weights(sums)
    first, second = total[0:BLOCK], total[BLOCK:]
    value = (
        first
        + weights[0] * pltpu.roll(first, BLOCK - 2, 0)
        + weights[1] * pltpu.roll(second, BLOCK - 2, 0)
        + weights[2] * second
    )
    spread[...] = jnp.zeros_like(spread)
    for source, target in ((0, 0), (4, 1), (1, 64), (5, 65)):
        spread[target : target + 1, :] = value[source : source + 1]
    for tile in range(3):
        at = slice(tile * LANES, min((tile + 1) * LANES, out.shape[0]))
        out[at, :] = jnp.transpose(spread[:, tile * LANES : (tile + 1) * LANES])[: at.stop - at.start]


def gather_kernel(parts, out):
    levels = out.shape[2]
    lane = lanes_of((1, LANES))
    total = jnp.zeros((SLOTS, LANES), jnp.float32)
    for pair in range(levels // 2):
        value = parts[SLOTS * pair : SLOTS * pair + SLOTS, :]
        total = jnp.where((lane & 63) >> 1 == pair, moved(value, 0, 2 * pair), total)
    out[:, 0, :] = total[:, 0:levels]
    out[:, 1, :] = total[:, 64 : 64 + levels]


def swapped(value, axis, first):
    count = lax.axis_size(axis)
    pairs = []
    for low in range(0 if first else 1, count - 1, 2):
        pairs += [(low, low + 1), (low + 1, low)]
    return lax.ppermute(value, axis, pairs)


def in_vmem(value):
    return pltpu.with_memory_space_constraint(value, pltpu.VMEM)


def in_hbm(value):
    return pltpu.with_memory_space_constraint(value, pltpu.HBM)


def shape_of(*shape):
    return jax.ShapeDtypeStruct(shape, jnp.float32)


def per_device(
    tracer_adjoint,
    surface_adjoint,
    flow_east,
    flow_north,
    vertical_mix,
    land_mask,
    conduct_east,
    conduct_north,
    surface_diagonal,
    pressure_load,
    surface_forcing,
    control_map,
    control_weight,
):
    levels, rows, cols = flow_east.shape
    across, along = lax.axis_size("gx"), lax.axis_size("gy")
    point_map = control_map.reshape(-1, LANES)
    point_weight = control_weight.reshape(-1, LANES)

    tile = shape_of(rows, cols)
    field = shape_of(2, levels, rows, cols)
    pack, inner = shape_of(rows, 3 * LANES), shape_of(rows, 2 * LANES)
    count = 4 * levels
    lines = shape_of(count, cols)
    rows_shape = shape_of(296, cols)
    kept, away = pltpu.VMEM(field.shape, jnp.float32), pltpu.HBM(field.shape, jnp.float32)
    b, u, v, first_pack, second_pack, west_inner, east_inner, edge_flow = pl.pallas_call(
        columns_kernel,
        out_shape=(tile, kept, kept, pack, pack, inner, inner, shape_of(56, cols)),
        in_specs=[HBM] * 11,
        out_specs=(VMEM,) * 8,
        scratch_shapes=[
            pltpu.VMEM((levels, rows, cols), jnp.float32),
            pltpu.SMEM((2, levels), jnp.float32),
            pltpu.SMEM((2, levels), jnp.float32),
            pltpu.VMEM((2, levels, rows, cols), jnp.float32),
            pltpu.VMEM((rows, cols), jnp.float32),
            pltpu.VMEM((levels, rows, cols), jnp.float32),
            pltpu.VMEM((levels, BLOCK, cols), jnp.float32),
            pltpu.VMEM((levels - 1, rows, cols), jnp.float32),
            pltpu.VMEM((levels, rows, cols), jnp.int32),
            pltpu.VMEM((rows, cols), jnp.float32),
            pltpu.VMEM((rows, cols), jnp.float32),
            pltpu.VMEM((rows, cols), jnp.float32),
            pltpu.SemaphoreType.DMA((48,)),
        ],
        compiler_params=BIG,
        name="columns",
    )(
        *(
            in_hbm(value)
            for value in (
                surface_forcing, pressure_load, tracer_adjoint, surface_adjoint, flow_east, flow_north,
                vertical_mix, land_mask, conduct_east, conduct_north, surface_diagonal,
            )
        ),
    )
    first_in = swapped(first_pack, "gx", True)
    second_in = swapped(second_pack, "gx", False)
    u, v, first_rows, second_rows, inner_rows = pl.pallas_call(
        store_kernel,
        out_shape=(away, away, rows_shape, rows_shape, lines),
        in_specs=[VMEM] * 3,
        out_specs=(HBM, HBM, VMEM, VMEM, VMEM),
        scratch_shapes=[pltpu.SemaphoreType.DMA((2,))],
        cost_estimate=pl.CostEstimate(flops=10**6, bytes_accessed=8 * 10**6, transcendentals=0),
        compiler_params=SMALL,
        name="store",
    )(in_vmem(u), in_vmem(v), edge_flow)
    outer = pl.BlockSpec((5 * BLOCK, cols), lambda i: (5, 0))
    first_rows, second_rows, side, west_in, east_in = pl.pallas_call(
        rows_kernel,
        out_shape=(rows_shape, rows_shape, tile, pack, pack),
        grid=(1,),
        in_specs=[VMEM] * 6 + [pl.BlockSpec(memory_space=pl.ANY)] * 2,
        out_specs=(outer, outer) + (VMEM,) * 3,
        input_output_aliases={6: 0, 7: 1},
        compiler_params=SMALL,
        name="rows",
    )(
        b, conduct_east, conduct_north, surface_diagonal, first_in, second_in,
        first_rows, second_rows,
    )
    first_in = swapped(first_rows, "gy", True)
    second_in = swapped(second_rows, "gy", False)
    full = shape_of(rows + 2 * BLOCK, 2 * LANES)
    line_weights, side_weights = pl.pallas_call(
        prepare_kernel,
        out_shape=(shape_of(4, count, cols), shape_of(6, count, cols)),
        in_specs=[VMEM] * 11,
        out_specs=(VMEM,) * 2,
        scratch_shapes=[pltpu.VMEM((count, cols), jnp.float32)] * 3
        + [pltpu.VMEM((2 * LANES, LANES), jnp.float32)],
        cost_estimate=pl.CostEstimate(flops=10**6, bytes_accessed=4 * 10**6, transcendentals=0),
        compiler_params=MIDDLE,
        name="prepare",
    )(
        flow_east, flow_north, west_in, east_in, first_pack, second_pack, west_inner, east_inner,
        first_rows, second_rows, inner_rows,
    )
    v0, v1, v2, rims, south_in, north_in = pl.pallas_call(
        krylov_kernel,
        out_shape=(full, full, full, shape_of(along * GROUP, LANES), rows_shape, rows_shape),
        in_specs=[VMEM] * 9,
        out_specs=(VMEM,) * 6,
        scratch_shapes=[
            pltpu.VMEM((count, cols), jnp.float32),
            pltpu.VMEM((LANES, LANES), jnp.float32),
        ],
        compiler_params=MIDDLE,
        name="krylov",
    )(
        b, conduct_east, conduct_north, surface_diagonal, side, first_in, second_in,
        line_weights, side_weights,
    )
    rims = lax.all_to_all(rims.reshape(along, 1, GROUP * LANES), "gy", 0, 0)
    points = (2 + rows * along // LANES) * LANES
    parts = pl.pallas_call(
        controls_kernel,
        out_shape=shape_of(across, 16, 3 * LANES),
        in_specs=[VMEM] * 3,
        out_specs=VMEM,
        scratch_shapes=[
            pltpu.VMEM((across * 48, points), jnp.bfloat16),
            pltpu.VMEM((points, 3 * LANES), jnp.bfloat16),
            pltpu.VMEM((across * 48, 3 * LANES), jnp.float32),
        ],
        compiler_params=MIDDLE,
        name="controls",
    )(rims.reshape(along * GROUP, LANES), point_map, point_weight)
    parts = lax.all_to_all(parts, "gx", 0, 0)
    sums, joined = pl.pallas_call(
        join_kernel,
        out_shape=(shape_of(1, LANES), shape_of(along * SLOTS, LANES)),
        in_specs=[VMEM],
        out_specs=(VMEM,) * 2,
        scratch_shapes=[pltpu.VMEM((LANES, 3 * LANES), jnp.float32)],
        compiler_params=SMALL,
        name="join",
    )(parts)
    joined = lax.all_to_all(joined.reshape(along, 1, SLOTS * LANES), "gy", 0, 0)
    tracer_grad, x = pl.pallas_call(
        fields_kernel,
        out_shape=(field, tile),
        in_specs=[VMEM] * 4 + [HBM] * 2 + [VMEM] * 6,
        out_specs=(HBM, VMEM),
        scratch_shapes=[
            pltpu.VMEM(field.shape, jnp.float32),
            pltpu.VMEM(field.shape, jnp.float32),
            pltpu.VMEM((2, levels, rows, cols), jnp.float32),
            pltpu.VMEM(full.shape, jnp.float32),
            pltpu.VMEM((count, cols), jnp.float32),
            pltpu.VMEM((count, cols), jnp.float32),
            pltpu.VMEM((10, rows + BLOCK, cols), jnp.float32),
            pltpu.VMEM((10, rows + BLOCK, cols), jnp.float32),
            pltpu.SemaphoreType.DMA((15,)),
        ],
        compiler_params=MIDDLE,
        name="fields",
    )(sums, v0, v1, v2, in_hbm(u), in_hbm(v), flow_east, flow_north, west_in, east_in, south_in, north_in)
    control_grad = pl.pallas_call(
        gather_kernel,
        out_shape=shape_of(SLOTS, 2, levels),
        in_specs=[VMEM],
        out_specs=VMEM,
        compiler_params=SMALL,
        name="gather",
    )(joined.reshape(along * SLOTS, LANES))
    return tracer_grad, x, jnp.transpose(control_grad, (1, 2, 0))


def solution(mesh):
    in_specs = (
        P(None, None, "gy", "gx"),
        P("gy", "gx"),
        P(None, "gy", "gx"),
        P(None, "gy", "gx"),
        P(None, "gy", "gx"),
        P(None, "gy", "gx"),
        P("gy", "gx"),
        P("gy", "gx"),
        P("gy", "gx"),
        P(),
        P(),
        P(),
        P(),
    )
    out_specs = (P(None, None, "gy", "gx"), P("gy", "gx"), P(None, None, ("gx", "gy")))
    return jax.shard_map(
        per_device, mesh=mesh, in_specs=in_specs, out_specs=out_specs, check_vma=False
    )
```

```python
import functools

import jax
import jax.numpy as jnp
from jax import lax
from jax.experimental import pallas as pl
from jax.experimental.pallas import tpu as pltpu
from jax.sharding import PartitionSpec as P

SLOTS = 10
LANES = 128
BLOCK = 8
GROUP = 25
GRAM = ((0, 0), (0, 1), (0, 2), (0, 3), (1, 1), (1, 2), (1, 3), (2, 2), (2, 3))
VMEM = pl.BlockSpec(memory_space=pltpu.VMEM)
HBM = pl.BlockSpec(memory_space=pltpu.HBM)
MIB = 1024 * 1024
BIG = pltpu.CompilerParams(vmem_limit_bytes=16 * MIB)
MIDDLE = pltpu.CompilerParams(vmem_limit_bytes=12 * MIB)
SMALL = pltpu.CompilerParams(vmem_limit_bytes=3 * MIB)


def lanes_of(shape):
    return lax.broadcasted_iota(jnp.int32, shape, len(shape) - 1)


def own_place():
    axes = ("gx", "gy")
    return tuple(map(lax.axis_index, axes)) + tuple(map(lax.axis_size, axes))


def moved(value, source, target):
    shift = target - source
    shift = shift % LANES if isinstance(shift, int) else lax.rem(shift + 4 * LANES, LANES)
    return pltpu.roll(value, shift, 1)


def columns_kernel(
    forcing_in, loads_in, tracer_in, surface_in, east_flow, north_flow, mix_in, mask_in, c_east_in,
    c_north_in, diag_in,
    b_out, u_out, v_out, first_pack, second_pack, west_inner, east_inner, edge_flow,
    ratios, forcing, loads, tracer, surface, flow_east, flow_north, mix, mask, c_east, c_north, diag,
    sems,
):
    levels, rows, cols = mask.shape
    shape = (rows, cols)
    place = own_place()
    zero = jnp.zeros(shape, jnp.float32)
    last = levels - 1
    chunk = 7
    started = []

    def fetch(source, target):
        copy = pltpu.make_async_copy(source, target, sems.at[len(started)])
        copy.start()
        started.append(copy)
        return copy

    scalars = [fetch(forcing_in, forcing), fetch(loads_in, loads)]
    chunks = []
    for at in range(0, last, chunk):
        here = pl.ds(at, chunk if at + chunk < last else chunk + 1)
        below = pl.ds(at + 1, chunk) if at else pl.ds(0, chunk + 1)
        chunks.append([
            fetch(mask_in.at[below], mask.at[below]),
            fetch(mix_in.at[pl.ds(at, chunk)], mix.at[pl.ds(at, chunk)]),
            fetch(tracer_in.at[:, here], tracer.at[:, here]),
        ])
    flats = [
        fetch(source, target)
        for source, target in (
            (surface_in, surface), (c_east_in, c_east), (c_north_in, c_north), (diag_in, diag),
            (north_flow.at[:, pl.ds(rows - BLOCK, BLOCK)], flow_north), (east_flow, flow_east),
        )
    ]
    for copy in scalars:
        copy.wait()

    def level_step(k, carry, kappa):
        before, ratio, r0, r1, r2, r3, total = carry
        wet = mask[k].astype(jnp.float32)
        t0, t1 = tracer[0, k], tracer[1, k]
        total = total + wet * (forcing[0, k] * t0 + forcing[1, k] * t1)
        inverse = 1.0 / (1.0 + before + kappa - before * ratio)
        r0 = (t0 + before * r0) * inverse
        r1 = (t1 + before * r1) * inverse
        r2 = (wet * loads[0, k] + before * r2) * inverse
        r3 = (wet * loads[1, k] + before * r3) * inverse
        return kappa * inverse, r0, r1, r2, r3, total

    carry = (zero,) * 7
    for k in range(last):
        if k % chunk == 0:
            for copy in chunks[k // chunk]:
                copy.wait()
        kappa = mix[k] * mask[k + 1].astype(jnp.float32)
        ratio, *reds, total = level_step(k, carry, kappa)
        ratios[k] = ratio
        u_out[0, k], u_out[1, k], v_out[0, k], v_out[1, k] = reds
        carry = (kappa, ratio, *reds, total)
    _, *sols, total = level_step(last, carry, zero)
    b_out[...] = total
    for k in range(last, -1, -1):
        if k < last:
            ratio = ratios[k]
            reds = (u_out[0, k], u_out[1, k], v_out[0, k], v_out[1, k])
            sols = [red + ratio * sol for red, sol in zip(reds, sols)]
        wet = mask[k].astype(jnp.float32)
        fields = [wet * sol for sol in sols]
        u_out[0, k], u_out[1, k], v_out[0, k], v_out[1, k] = fields
    for copy in flats:
        copy.wait()
    total = b_out[...] + surface[...]
    b_out[...] = total
    lane = lanes_of((1, cols))
    even = (place[0] & 1) == 0

    def pack(at, west, east):
        first_pack[:, at] = jnp.where(even, east, west)
        second_pack[:, at] = jnp.where(even, west, east)

    for tile in range(2):
        west, east, west_in, east_in = zero, zero, zero, zero
        for spot in range(4 * min(32, levels - 32 * tile)):
            k, q = 32 * tile + spot // 4, spot % 4
            field = u_out[q, k] if q < 2 else v_out[q - 2, k]
            turned = moved(field, 0, spot)
            west = jnp.where(lane == spot, turned, west)
            west_in = jnp.where(lane == (spot + 1) % LANES, turned, west_in)
            east = jnp.where(lane == (spot - 1) % LANES, turned, east)
            east_in = jnp.where(lane == (spot - 2) % LANES, turned, east_in)
        at = slice(tile * LANES, (tile + 1) * LANES)
        east = moved(east, 0, 1)
        if tile == 1:
            for k in range(levels):
                east = jnp.where(lane == 72 + k, moved(flow_east[k], cols - 1, 72 + k), east)
        pack(at, west, east)
        west_inner[:, at], east_inner[:, at] = moved(west_in, 1, 0), moved(east_in, 0, 2)
    for k in range(levels):
        edge_flow[k : k + 1, :] = flow_north[k, BLOCK - 1 : BLOCK, :]
    west, east = zero, zero
    for a, field in enumerate((total, c_east[...], c_north[...], diag[...])):
        here = (lane >= 4 * a) & (lane < 4 * a + 3)
        west = jnp.where(here, moved(field, 0, 4 * a), west)
        east = jnp.where(here, moved(field, cols - 3, 4 * a), east)
    pack(slice(2 * LANES, 3 * LANES), west, east)

def store_kernel(u, v, edge_flow, u_hbm, v_hbm, first_rows, second_rows, inner_rows, sems):
    _, levels, rows, _ = u.shape
    place = own_place()
    copies = [
        pltpu.make_async_copy(source, target, sems.at[n])
        for n, (source, target) in enumerate(((u, u_hbm), (v, v_hbm)))
    ]
    for copy in copies:
        copy.start()
    even = (place[1] & 1) == 0
    picks = (
        (first_rows, jnp.where(even, rows - 1, 0)),
        (second_rows, jnp.where(even, 0, rows - 1)),
        (inner_rows, jnp.where(place[1] == 0, 1, rows - 2)),
    )
    for k in range(levels):
        for q in range(4):
            for target, row in picks:
                line = slice(4 * k + q, 4 * k + q + 1)
                target[line, :] = (u, v)[q // 2][q % 2, k, pl.ds(row, 1), :]
    for target in (first_rows, second_rows):
        target[240 : 240 + levels, :] = edge_flow[0:levels, :]
    for copy in copies:
        copy.wait()


def rows_kernel(
    b, c_east, c_north, diag, first_in, second_in, _f, _s,
    first_rows, second_rows, side, west_in, east_in,
):
    shape = b.shape
    rows = shape[0]
    place = own_place()
    lane = lanes_of(shape)
    even = (place[0] & 1) == 0
    west_in[...] = jnp.where(even, second_in[...], first_in[...])
    east_in[...] = jnp.where(even, first_in[...], second_in[...])
    side[...] = jnp.where(
        lane < 64, west_in[:, 2 * LANES :], moved(east_in[:, 2 * LANES :], 0, 64)
    )
    even = (place[1] & 1) == 0
    for a, field in enumerate((b, c_east, c_north, diag, side)):
        south, north = field[0:BLOCK, :], field[rows - BLOCK :, :]
        first_rows[BLOCK * a : BLOCK * a + BLOCK, :] = jnp.where(even, north, south)
        second_rows[BLOCK * a : BLOCK * a + BLOCK, :] = jnp.where(even, south, north)


def tall_transpose(value):
    rows, wide = value.shape
    if rows < LANES:
        value = jnp.concatenate([value, jnp.zeros((LANES - rows, wide), jnp.float32)], axis=0)
    tiles = [jnp.transpose(value[:, at : at + LANES]) for at in range(0, wide, LANES)]
    return jnp.concatenate(tiles, axis=0)


def rim_weights(center, inner, low, high, face_high, face_low, face_inner, last):
    lane = lanes_of(center.shape)
    low = jnp.where(lane == 0, low, pltpu.roll(center, 1, 1))
    high = jnp.where(lane == last, high, pltpu.roll(center, LANES - 1, 1))
    face_low = jnp.where(lane == 0, face_low, pltpu.roll(face_high, 1, 1))
    return (
        center * (1.0 - 0.5 * face_high + 0.5 * face_low - 0.5 * face_inner),
        0.5 * face_inner * inner,
        -0.5 * face_low * low,
        0.5 * face_high * high,
    )


def rim_parts(weights, factors):
    rows = weights[0].shape[0]
    which = lax.broadcasted_iota(jnp.int32, weights[0].shape, 0) & 3
    parts = []
    for n, values in enumerate(factors):
        if n == 0:
            values = [jnp.where(which < 2, 1.0, value) for value in values]
        parts.append(sum(weight * value for weight, value in zip(weights, values)))
    return parts[0], jnp.where(which >= 2, parts[1], pltpu.roll(parts[2], rows - 2, 0))


def prepare_kernel(
    flow_east, flow_north, west_in, east_in, first_pack, second_pack, west_inner, east_inner,
    first_rows, second_rows, inner_rows,
    line_out, side_out,
    high_buf, low_buf, face_buf, turned,
):
    levels, rows, cols = flow_east.shape
    count = 4 * levels
    place = own_place()

    @pl.when((place[1] == 0) | (place[1] == place[3] - 1))
    def _():
        south = place[1] == 0
        at = jnp.where(south, 0, rows - 1)
        sign = jnp.where(south, 1.0, -1.0)
        west_turned = tall_transpose(west_in[:, : 2 * LANES])
        west_turned = jnp.where(south, west_turned, moved(west_turned, rows - 1, 0))
        turned[...] = west_turned
        east_turned = tall_transpose(east_in[:, : 2 * LANES])
        high = jnp.where(
            south, moved(east_turned, 0, cols - 1), moved(east_turned, rows - 1, cols - 1)
        )
        for k in range(levels):
            four = slice(4 * k, 4 * k + 4)
            high_buf[four, :] = jnp.broadcast_to(flow_east[k, pl.ds(at, 1), :], (4, cols))
            low_buf[four, :] = jnp.broadcast_to(turned[count + k : count + k + 1, :], (4, cols))
            face_buf[four, :] = jnp.broadcast_to(
                sign * flow_north[k, pl.ds(jnp.where(south, 0, rows - 2), 1), :], (4, cols)
            )
        second = south == ((place[1] & 1) == 0)
        weights = rim_weights(
            jnp.where(second, second_rows[0:count, :], first_rows[0:count, :]),
            inner_rows[...], west_turned[0:count], high[0:count],
            high_buf[...], low_buf[...], face_buf[...], cols - 1,
        )
        for n, weight in enumerate(weights):
            line_out[n] = weight

    @pl.when((place[0] == 0) | (place[0] == place[2] - 1))
    def _():
        western = place[0] == 0
        sign = jnp.where(western, 1.0, -1.0)
        flat = lanes_of((rows, cols))
        norths = jnp.zeros((rows, cols), jnp.float32)
        easts = norths
        for k in range(levels):
            mark = jnp.where(western, k, (k - 1) % LANES)
            norths = jnp.where(flat == mark, moved(flow_north[k], 0, k), norths)
            mark = jnp.where(western, k, (k - 2) % LANES)
            easts = jnp.where(flat == mark, moved(flow_east[k], 0, k), easts)
        norths = jnp.where(western, norths, pltpu.roll(norths, 1, 1))
        easts = jnp.where(western, moved(easts, 0, 64), moved(easts, 0, 66))
        turned[0:LANES, :] = tall_transpose(jnp.where(flat < 64, norths, easts))
        for k in range(levels):
            four = slice(4 * k, 4 * k + 4)
            high_buf[four, :] = jnp.broadcast_to(turned[k : k + 1, :], (4, cols))
            face_buf[four, :] = jnp.broadcast_to(sign * turned[64 + k : 65 + k, :], (4, cols))

        second = western == ((place[0] & 1) == 0)
        center = jnp.where(second, second_pack[:, : 2 * LANES], first_pack[:, : 2 * LANES])
        inside = jnp.where(western, west_inner[...], east_inner[...])
        center = tall_transpose(center)[0:count]
        weights = rim_weights(
            center, tall_transpose(inside)[0:count], 0.0, 0.0, high_buf[...], 0.0, face_buf[...], rows - 1
        )
        for n, weight in enumerate((*weights, 0.5 * center, 0.5 * high_buf[...])):
            side_out[n] = weight


def krylov_kernel(
    b, c_east, c_north, diag, side, first_in, second_in, line_in, side_in,
    v0_out, v1_out, v2_out, out, south_in, north_in,
    low_buf, turned,
):
    rows, cols = b.shape
    count = line_in.shape[1]
    levels = count // 4
    place = own_place()
    even = (place[1] & 1) == 0
    south_in[...] = jnp.where(even, second_in[...], first_in[...])
    north_in[...] = jnp.where(even, first_in[...], second_in[...])
    sides = jnp.concatenate([south_in[232:240, :], side[...], north_in[232:240, :]], axis=0)
    lane = lanes_of(sides.shape)
    full = []
    for a, field in enumerate((b, c_east, c_north, diag)):
        at = slice(200 + 8 * a, 208 + 8 * a)
        main = jnp.concatenate([south_in[at, :], field[...], north_in[at, :]], axis=0)
        beside = jnp.where(
            lane >= LANES - 3,
            moved(sides, 4 * a, LANES - 3),
            jnp.where(lane < 3, moved(sides, 64 + 4 * a, 0), 0.0),
        )
        full.append(jnp.concatenate([main, beside], axis=1))
    vec, ce, cn, dg = full
    tall, wide = vec.shape
    cw = pltpu.roll(ce, 1, 1)
    cs = pltpu.roll(cn, 1, 0)
    vecs = [vec]
    for _ in range(3):
        vec = (
            dg * vec
            + ce * (vec - pltpu.roll(vec, wide - 1, 1))
            + cw * (vec - pltpu.roll(vec, 1, 1))
            + cn * (vec - pltpu.roll(vec, tall - 1, 0))
            + cs * (vec - pltpu.roll(vec, 1, 0))
        )
        vecs.append(vec)
    outs = (v0_out, v1_out, v2_out)
    for target, value in zip(outs, vecs):
        target[...] = value
    tiles = [value[BLOCK : BLOCK + rows, :LANES] for value in vecs]
    spot = lanes_of((1, LANES))
    row = jnp.zeros((1, LANES), jnp.float32)
    for n, (i, j) in enumerate(GRAM):
        part = jnp.sum(tiles[i] * tiles[j], axis=0, keepdims=True)
        row = jnp.where(spot == n, jnp.sum(part, axis=1, keepdims=True), row)
    out[...] = jnp.zeros_like(out)
    for at in range(0, out.shape[0], GROUP):
        out[at + GROUP - 1 : at + GROUP, :] = row

    def emit(parts, first):
        for group in range(count // BLOCK):
            for n, part in enumerate(parts):
                at = GROUP * group + first + n * BLOCK
                out[at : at + BLOCK, :] = part[BLOCK * group : BLOCK * group + BLOCK]

    @pl.when((place[1] == 0) | (place[1] == place[3] - 1))
    def _():
        south = place[1] == 0
        at = jnp.where(south, 0, rows - 1)
        at_in = jnp.where(south, 1, rows - 2)
        factors = []
        for value in outs:
            line = value[pl.ds(BLOCK + at, 1), :]
            factors.append((
                line[:, :cols], value[pl.ds(BLOCK + at_in, 1), :][:, :cols],
                pltpu.roll(line, 1, 1)[:, :cols], pltpu.roll(line, wide - 1, 1)[:, :cols],
            ))
        emit(rim_parts([line_in[n] for n in range(4)], factors), 0)

    @pl.when((place[0] == 0) | (place[0] == place[2] - 1))
    def _():
        western = place[0] == 0
        at = jnp.where(western, 0, cols - 1)
        at_in = jnp.where(western, 1, cols - 2)
        for k in range(levels):
            low_buf[4 * k : 4 * k + 4, :] = jnp.broadcast_to(south_in[240 + k : 241 + k, :], (4, cols))

        def line_up(value, target):
            return jnp.where(western, moved(value, 0, target), moved(value, cols - 1, target))

        factors = []
        for value in outs:
            turned[...] = tall_transpose(value[:, :cols])
            line = pltpu.roll(turned[pl.ds(at, 1), :], LANES - BLOCK, 1)
            factors.append((
                line, pltpu.roll(turned[pl.ds(at_in, 1), :], LANES - BLOCK, 1),
                pltpu.roll(line, 1, 1), pltpu.roll(line, LANES - 1, 1),
            ))
        here, inside, before, behind, center, face = (side_in[n] for n in range(6))
        spots = lanes_of(here.shape)
        low = line_up(low_buf[...], 0)
        here = here + jnp.where(spots == 0, low * center, 0.0)
        before = jnp.where(spots == 0, -0.5 * low * line_up(south_in[0:count, :], 0), before)
        behind = jnp.where(
            spots == rows - 1, face * line_up(north_in[0:count, :], rows - 1), behind
        )
        first, second = rim_parts((here, inside, before, behind), factors)
        half = lanes_of(first.shape) < 64
        emit((jnp.where(half, first, moved(second, 0, 64)),), 2 * BLOCK)


def krylov_weights(sums):
    gram = {pair: sums[0:1, n : n + 1] for n, pair in enumerate(GRAM)}

    def form(left, right):
        total = 0.0
        for i, x in left.items():
            for j, y in right.items():
                total = total + x * y * gram[min(i, j), max(i, j)]
        return total

    one = jnp.ones_like(gram[0, 0])
    remain, search = {0: one}, {0: one}
    weights = {}
    norm = gram[0, 0]
    for iteration in range(3):
        image = {i + 1: x for i, x in search.items()}
        step = norm / form(search, image)
        for i, x in search.items():
            weights[i] = weights.get(i, 0.0) + step * x
        if iteration < 2:
            remain = {
                i: remain.get(i, 0.0) - step * image.get(i, 0.0) for i in range(iteration + 2)
            }
            renewed = form(remain, remain)
            ratio = renewed / norm
            search = {i: x + ratio * search.get(i, 0.0) for i, x in remain.items()}
            norm = renewed
    return weights


def fields_kernel(
    sums_in, v0, v1, v2, u_hbm, v_hbm, flow_east, flow_north, west_in, east_in, south_in, north_in,
    grad_out, x_out, u, v, grad, x_full, south_lam, north_lam, lam_buf, flux_buf, sems,
):
    levels, rows, cols = flow_east.shape
    shape = (rows, cols)
    arrivals = []
    for n, at in enumerate(range(0, levels, 10)):
        at = pl.ds(at, 10)
        arrivals.append([
            pltpu.make_async_copy(source.at[:, at], target.at[:, at], sems.at[5 + 2 * n + m])
            for m, (source, target) in enumerate(((u_hbm, u), (v_hbm, v)))
        ])
        for copy in arrivals[-1]:
            copy.start()
    lane = lanes_of(shape)
    weights = krylov_weights(sums_in)
    x_full[...] = weights[0] * v0[...] + weights[1] * v1[...] + weights[2] * v2[...]
    x = x_full[BLOCK : BLOCK + rows, :cols]
    x_out[...] = x
    count = 4 * levels
    for source, target, at in ((south_in, south_lam, BLOCK - 1), (north_in, north_lam, BLOCK + rows)):
        target[...] = source[0:count, :] + source[2 : count + 2, :] * x_full[at : at + 1, :cols]
    x_west = x_full[BLOCK : BLOCK + rows, 2 * LANES - 1 :]
    x_east = x_full[BLOCK : BLOCK + rows, LANES : LANES + 1]
    part = lane & 3
    halos = []
    for tile in range(2):
        at = slice(tile * LANES, (tile + 1) * LANES)
        west, east = west_in[:, at], east_in[:, at]
        west = west + pltpu.roll(west, LANES - 2, 1) * x_west
        east = east + pltpu.roll(east, LANES - 2, 1) * x_east
        later = jnp.where(part == 2, pltpu.roll(west, 1, 1), pltpu.roll(east, LANES - 1, 1))
        halos.append(jnp.where(part == 0, west, jnp.where(part == 1, east, later)))
    copies = []
    for k in range(levels):
        if k % 10 == 0:
            for copy in arrivals[k // 10]:
                copy.wait()
        fe, fn = 0.5 * flow_east[k], 0.5 * flow_north[k]
        fw = jnp.where(
            lane == 0, 0.5 * moved(west_in[:, LANES : 2 * LANES], 72 + k, 0), pltpu.roll(fe, 1, 1)
        )
        fs = 0.5 * south_in[240 + k : 241 + k, :]
        for s in range(2):
            n = s * levels + k
            slot = n % 10
            line = slice(4 * k + s, 4 * k + s + 1)
            lam = u[s, k] + v[s, k] * x
            lam_buf[slot, 0:rows, :] = lam
            lam_buf[slot, rows : rows + 1, :] = north_lam[line, :]
            halo = moved(halos[k // 32], 4 * (k % 32) + 2 * s, 0)
            east = jnp.where(lane == cols - 1, halo, pltpu.roll(lam, cols - 1, 1))
            west = jnp.where(lane == 0, halo, pltpu.roll(lam, 1, 1))
            flux = fn * (lam_buf[slot, 1 : rows + 1, :] - lam)
            flux_buf[slot, BLOCK : BLOCK + rows, :] = flux
            flux_buf[slot, BLOCK - 1 : BLOCK, :] = fs * (lam[0:1] - south_lam[line, :])
            out = (
                lam
                + fe * (east - lam)
                + fw * (lam - west)
                + flux
                + flux_buf[slot, BLOCK - 1 : BLOCK - 1 + rows, :]
            )
            grad[s, k] = out
        if k % 10 == 9:
            at = pl.ds(k - 9, 10)
            copies.append(
                pltpu.make_async_copy(grad.at[:, at], grad_out.at[:, at], sems.at[k // 10])
            )
            copies[-1].start()
    for copy in copies:
        copy.wait()


def controls_kernel(rims, point_map, point_weight, out, values, hot, total):
    peers, high, wide = out.shape
    place = own_place()
    lane = lanes_of((1, LANES))
    rows = 40
    tiles = rows * (rims.shape[0] // GROUP) // LANES

    def point_tile(n, value, row):
        value = value * point_weight[pl.ds(row, 1), :]
        ids = point_map[pl.ds(row, 1), :]
        column = lax.shift_right_logical(lax.shift_right_logical(ids, 6) * 13108, 16)
        here = slice(n * LANES, (n + 1) * LANES)
        for piece in range(3):
            part = value.astype(jnp.bfloat16).astype(jnp.float32)
            for peer in range(peers):
                at = high * (3 * peer + piece)
                mine = jnp.where(column == peer, part, 0.0)
                values[at : at + high, here] = mine.astype(jnp.bfloat16)
            value = value - part
        target = ids - 32 * SLOTS * column
        target = jnp.transpose(jnp.broadcast_to(target, (LANES, LANES)))
        across = lanes_of((LANES, LANES))
        for at in range(0, wide, LANES):
            hit = jnp.where(across == target - at, 1.0, 0.0)
            hot[here, at : at + LANES] = hit.astype(jnp.bfloat16)

    def product(depth):
        total[...] = jnp.dot(
            values[:, :depth], hot[:depth, :], preferred_element_type=jnp.float32
        )

    last = rims.shape[0] - GROUP
    point_tile(0, rims[0:high, :], place[0])
    point_tile(1, rims[last : last + high, :], peers + place[0])
    beside = (place[0] == 0) | (place[0] == place[2] - 1)

    @pl.when(jnp.logical_not(beside))
    def _():
        product(2 * LANES)

    @pl.when(beside)
    def _():
        first = jnp.where(place[0] == 0, 2 * peers, 2 * peers + tiles)
        for tile in range(tiles):
            parts = []
            for source in (0, 64):
                value = jnp.zeros((BLOCK, LANES), jnp.float32)
                for row in range(tile * LANES // rows, -(-(tile + 1) * LANES // rows)):
                    at = rows * row - tile * LANES
                    piece = rims[GROUP * row + 2 * BLOCK : GROUP * row + 3 * BLOCK, :]
                    value = jnp.where(
                        (lane >= at) & (lane < at + rows), moved(piece, source, at % LANES), value
                    )
                parts.append(value)
            point_tile(2 + tile, jnp.concatenate(parts, axis=0), first + tile)
        product((2 + tiles) * LANES)

    sums = [rims[at - 1 : at, :] for at in range(GROUP, rims.shape[0] + 1, GROUP)]
    while len(sums) > 1:
        sums = [a + b for a, b in zip(sums[0::2], sums[1::2])]
    sums = pltpu.roll(sums[0], 64, 1)
    for peer in range(peers):
        at = 3 * high * peer
        out[peer] = (
            total[at : at + high] + total[at + high : at + 2 * high] + total[at + 2 * high : at + 3 * high]
        )
        at = slice(wide - LANES, wide)
        out[peer, 0:1, at] = jnp.where(lane < 64, out[peer, 0:1, at], sums)


def join_kernel(parts, sums_out, out, spread):
    total = jnp.sum(parts[...], axis=0)
    sums = pltpu.roll(total[0:1, 2 * LANES :], 64, 1)
    sums_out[...] = sums
    weights = krylov_weights(sums)
    first, second = total[0:BLOCK], total[BLOCK:]
    value = (
        first
        + weights[0] * pltpu.roll(first, BLOCK - 2, 0)
        + weights[1] * pltpu.roll(second, BLOCK - 2, 0)
        + weights[2] * second
    )
    spread[...] = jnp.zeros_like(spread)
    for source, target in ((0, 0), (4, 1), (1, 64), (5, 65)):
        spread[target : target + 1, :] = value[source : source + 1]
    for tile in range(3):
        at = slice(tile * LANES, min((tile + 1) * LANES, out.shape[0]))
        out[at, :] = jnp.transpose(spread[:, tile * LANES : (tile + 1) * LANES])[: at.stop - at.start]


def gather_kernel(parts, out):
    levels = out.shape[2]
    lane = lanes_of((1, LANES))
    total = jnp.zeros((SLOTS, LANES), jnp.float32)
    for pair in range(levels // 2):
        value = parts[SLOTS * pair : SLOTS * pair + SLOTS, :]
        total = jnp.where((lane & 63) >> 1 == pair, moved(value, 0, 2 * pair), total)
    out[:, 0, :] = total[:, 0:levels]
    out[:, 1, :] = total[:, 64 : 64 + levels]


def swapped(value, axis, first):
    count = lax.axis_size(axis)
    pairs = []
    for low in range(0 if first else 1, count - 1, 2):
        pairs += [(low, low + 1), (low + 1, low)]
    return lax.ppermute(value, axis, pairs)


def in_vmem(value):
    return pltpu.with_memory_space_constraint(value, pltpu.VMEM)


def in_hbm(value):
    return pltpu.with_memory_space_constraint(value, pltpu.HBM)


def shape_of(*shape):
    return jax.ShapeDtypeStruct(shape, jnp.float32)


def per_device(
    tracer_adjoint,
    surface_adjoint,
    flow_east,
    flow_north,
    vertical_mix,
    land_mask,
    conduct_east,
    conduct_north,
    surface_diagonal,
    pressure_load,
    surface_forcing,
    control_map,
    control_weight,
):
    levels, rows, cols = flow_east.shape
    across, along = lax.axis_size("gx"), lax.axis_size("gy")
    point_map = control_map.reshape(-1, LANES)
    point_weight = control_weight.reshape(-1, LANES)

    tile = shape_of(rows, cols)
    field = shape_of(2, levels, rows, cols)
    pack, inner = shape_of(rows, 3 * LANES), shape_of(rows, 2 * LANES)
    count = 4 * levels
    lines = shape_of(count, cols)
    rows_shape = shape_of(296, cols)
    kept, away = pltpu.VMEM(field.shape, jnp.float32), pltpu.HBM(field.shape, jnp.float32)
    b, u, v, first_pack, second_pack, west_inner, east_inner, edge_flow = pl.pallas_call(
        columns_kernel,
        out_shape=(tile, kept, kept, pack, pack, inner, inner, shape_of(56, cols)),
        in_specs=[HBM] * 11,
        out_specs=(VMEM,) * 8,
        scratch_shapes=[
            pltpu.VMEM((levels, rows, cols), jnp.float32),
            pltpu.SMEM((2, levels), jnp.float32),
            pltpu.SMEM((2, levels), jnp.float32),
            pltpu.VMEM((2, levels, rows, cols), jnp.float32),
            pltpu.VMEM((rows, cols), jnp.float32),
            pltpu.VMEM((levels, rows, cols), jnp.float32),
            pltpu.VMEM((levels, BLOCK, cols), jnp.float32),
            pltpu.VMEM((levels - 1, rows, cols), jnp.float32),
            pltpu.VMEM((levels, rows, cols), jnp.int32),
            pltpu.VMEM((rows, cols), jnp.float32),
            pltpu.VMEM((rows, cols), jnp.float32),
            pltpu.VMEM((rows, cols), jnp.float32),
            pltpu.SemaphoreType.DMA((48,)),
        ],
        compiler_params=BIG,
        name="columns",
    )(
        *(
            in_hbm(value)
            for value in (
                surface_forcing, pressure_load, tracer_adjoint, surface_adjoint, flow_east, flow_north,
                vertical_mix, land_mask, conduct_east, conduct_north, surface_diagonal,
            )
        ),
    )
    first_in = swapped(first_pack, "gx", True)
    second_in = swapped(second_pack, "gx", False)
    u, v, first_rows, second_rows, inner_rows = pl.pallas_call(
        store_kernel,
        out_shape=(away, away, rows_shape, rows_shape, lines),
        in_specs=[VMEM] * 3,
        out_specs=(HBM, HBM, VMEM, VMEM, VMEM),
        scratch_shapes=[pltpu.SemaphoreType.DMA((2,))],
        cost_estimate=pl.CostEstimate(flops=10**6, bytes_accessed=8 * 10**6, transcendentals=0),
        compiler_params=SMALL,
        name="store",
    )(in_vmem(u), in_vmem(v), edge_flow)
    outer = pl.BlockSpec((5 * BLOCK, cols), lambda i: (5, 0))
    first_rows, second_rows, side, west_in, east_in = pl.pallas_call(
        rows_kernel,
        out_shape=(rows_shape, rows_shape, tile, pack, pack),
        grid=(1,),
        in_specs=[VMEM] * 6 + [pl.BlockSpec(memory_space=pl.ANY)] * 2,
        out_specs=(outer, outer) + (VMEM,) * 3,
        input_output_aliases={6: 0, 7: 1},
        compiler_params=SMALL,
        name="rows",
    )(
        b, conduct_east, conduct_north, surface_diagonal, first_in, second_in,
        first_rows, second_rows,
    )
    first_in = swapped(first_rows, "gy", True)
    second_in = swapped(second_rows, "gy", False)
    full = shape_of(rows + 2 * BLOCK, 2 * LANES)
    line_weights, side_weights = pl.pallas_call(
        prepare_kernel,
        out_shape=(shape_of(4, count, cols), shape_of(6, count, cols)),
        in_specs=[VMEM] * 11,
        out_specs=(VMEM,) * 2,
        scratch_shapes=[pltpu.VMEM((count, cols), jnp.float32)] * 3
        + [pltpu.VMEM((2 * LANES, LANES), jnp.float32)],
        cost_estimate=pl.CostEstimate(flops=10**6, bytes_accessed=4 * 10**6, transcendentals=0),
        compiler_params=MIDDLE,
        name="prepare",
    )(
        flow_east, flow_north, west_in, east_in, first_pack, second_pack, west_inner, east_inner,
        first_rows, second_rows, inner_rows,
    )
    v0, v1, v2, rims, south_in, north_in = pl.pallas_call(
        krylov_kernel,
        out_shape=(full, full, full, shape_of(along * GROUP, LANES), rows_shape, rows_shape),
        in_specs=[VMEM] * 9,
        out_specs=(VMEM,) * 6,
        scratch_shapes=[
            pltpu.VMEM((count, cols), jnp.float32),
            pltpu.VMEM((LANES, LANES), jnp.float32),
        ],
        compiler_params=MIDDLE,
        name="krylov",
    )(
        b, conduct_east, conduct_north, surface_diagonal, side, first_in, second_in,
        line_weights, side_weights,
    )
    rims = lax.all_to_all(rims.reshape(along, 1, GROUP * LANES), "gy", 0, 0)
    points = (2 + rows * along // LANES) * LANES
    parts = pl.pallas_call(
        controls_kernel,
        out_shape=shape_of(across, 16, 3 * LANES),
        in_specs=[VMEM] * 3,
        out_specs=VMEM,
        scratch_shapes=[
            pltpu.VMEM((across * 48, points), jnp.bfloat16),
            pltpu.VMEM((points, 3 * LANES), jnp.bfloat16),
            pltpu.VMEM((across * 48, 3 * LANES), jnp.float32),
        ],
        compiler_params=MIDDLE,
        name="controls",
    )(rims.reshape(along * GROUP, LANES), point_map, point_weight)
    parts = lax.all_to_all(parts, "gx", 0, 0)
    sums, joined = pl.pallas_call(
        join_kernel,
        out_shape=(shape_of(1, LANES), shape_of(along * SLOTS, LANES)),
        in_specs=[VMEM],
        out_specs=(VMEM,) * 2,
        scratch_shapes=[pltpu.VMEM((LANES, 3 * LANES), jnp.float32)],
        compiler_params=SMALL,
        name="join",
    )(parts)
    joined = lax.all_to_all(joined.reshape(along, 1, SLOTS * LANES), "gy", 0, 0)
    tracer_grad, x = pl.pallas_call(
        fields_kernel,
        out_shape=(field, tile),
        in_specs=[VMEM] * 4 + [HBM] * 2 + [VMEM] * 6,
        out_specs=(HBM, VMEM),
        scratch_shapes=[
            pltpu.VMEM(field.shape, jnp.float32),
            pltpu.VMEM(field.shape, jnp.float32),
            pltpu.VMEM((2, levels, rows, cols), jnp.float32),
            pltpu.VMEM(full.shape, jnp.float32),
            pltpu.VMEM((count, cols), jnp.float32),
            pltpu.VMEM((count, cols), jnp.float32),
            pltpu.VMEM((10, rows + BLOCK, cols), jnp.float32),
            pltpu.VMEM((10, rows + BLOCK, cols), jnp.float32),
            pltpu.SemaphoreType.DMA((15,)),
        ],
        compiler_params=MIDDLE,
        name="fields",
    )(sums, v0, v1, v2, in_hbm(u), in_hbm(v), flow_east, flow_north, west_in, east_in, south_in, north_in)
    control_grad = pl.pallas_call(
        gather_kernel,
        out_shape=shape_of(SLOTS, 2, levels),
        in_specs=[VMEM],
        out_specs=VMEM,
        compiler_params=SMALL,
        name="gather",
    )(joined.reshape(along * SLOTS, LANES))
    return tracer_grad, x, jnp.transpose(control_grad, (1, 2, 0))


def solution(mesh):
    in_specs = (
        P(None, None, "gy", "gx"),
        P("gy", "gx"),
        P(None, "gy", "gx"),
        P(None, "gy", "gx"),
        P(None, "gy", "gx"),
        P(None, "gy", "gx"),
        P("gy", "gx"),
        P("gy", "gx"),
        P("gy", "gx"),
        P(),
        P(),
        P(),
        P(),
    )
    out_specs = (P(None, None, "gy", "gx"), P("gy", "gx"), P(None, None, ("gx", "gy")))
    return jax.shard_map(
        per_device, mesh=mesh, in_specs=in_specs, out_specs=out_specs, check_vma=False
    )
```
